256 devices in a mesh: dp: 4 (over x_hi, core), rows: 64 (over y, x_lo, z).
Axes of the slice: x: 4 (x_hi: 2, x_lo: 2; x = x_hi * 2 + x_lo), y: 4, z: 8, core: 2. Of those that a mesh axis runs over, the one named last changes fastest.
Arguments:
- image: bfloat16 [4, 192, 48, 512], P('dp', 'rows'), may hold values from -6 to 6
- out_grad: bfloat16 [4, 192, 48, 512], P('dp', 'rows'), may hold values from -1 to 1
- w_qkv: bfloat16 [2, 512, 768], replicated
- w_proj: bfloat16 [2, 256, 512], replicated, may hold values from -0.375 to 0.375
- norm_gain: float32 [2, 512], replicated, may hold values from 0.25 to 1.75
- norm_bias: float32 [2, 512], replicated, may hold values from -3 to 3
- logit_scale: float32 [2, 8], replicated, may hold values from 1.6 to 2.8
- row_band: int32 [192], replicated, may hold values from 0 to 2, as said below
- col_band: int32 [48], replicated, may hold values from 0 to 2, as said below
Outputs:
- grad_image: bfloat16 [4, 192, 48, 512], P('dp', 'rows')
- grad_qkv: float32 [2, 512, 768], P(None, 'rows')
- grad_proj: float32 [2, 256, 512], P(None, None, 'rows')
- grad_gain: float32 [2, 512], P(None, 'rows')
- grad_bias: float32 [2, 512], P(None, 'rows')
The draws below stay inside these ranges and needn't reach their ends.
Inputs may be any that keep to these rules, and one draw needn't show every extreme that they name: `row_band`: labels never fall from one row to the next, and every label 0, 1, 2 occurs. `col_band`: labels never fall from one column to the next, and every label 0, 1, 2 occurs.
All inputs are finite; a program needn't handle non-finite values.
Results may differ from the reference program's by a relative error of at most 0.025.
Values may be sent and summed in bfloat16 or wider, within the bound.
No kernel may reach another device: no remote copies, remote signals or barrier semaphores. Data moves between devices by JAX's collectives and lax.ppermute only.
A program may use at most 64 MiB of HBM per device.

```python
import jax
import jax.numpy as jnp
from jax import lax

C = 512
HEADS = 8
HD = 32
WIN = 24
COLS = 48
IMAGES = 4
NY = 192
HH = 256
SHIFT = 12


def band_labels(key, total):
    first_key, second_key = jax.random.split(key)
    first_cut = jax.random.randint(first_key, (), 1, total // 2)
    second_cut = jax.random.randint(second_key, (), total // 2, total)
    places = jnp.arange(total)
    return (places >= first_cut).astype(jnp.int32) + (places >= second_cut).astype(jnp.int32)


def draw_row_band(key, part):
    key = jax.random.fold_in(key, 11)
    return band_labels(key, NY)


def draw_col_band(key, part):
    key = jax.random.fold_in(key, 17)
    return band_labels(key, COLS)


def draw_w_qkv(key, part):
    key = jax.random.fold_in(key, 23)
    base = jax.random.normal(key, (2, C, 3 * HH), jnp.float32) * C ** (-0.5)
    return base.astype(jnp.bfloat16)


def block_scale(key, shape, shards, low, largest):
    factor_of = 1.0
    for axis_at, blocks in shards:
        heights = jax.random.uniform(jax.random.fold_in(jax.random.fold_in(key, 6), axis_at), (blocks,), jnp.float32, low / len(shards), largest / len(shards))
        factor_of = factor_of * jnp.repeat(jnp.exp(heights), shape[axis_at] // blocks).reshape((-1,) + (1,) * (len(shape) - 1 - axis_at))
    return factor_of


def centred(rng, extent, width, bound, shards=(), kind=jnp.bfloat16):
    gain = block_scale(rng, extent, shards, -0.22, 0.18) if shards else 1.0
    values = jax.random.normal(rng, extent, jnp.float32) * width * gain
    return jnp.minimum(jnp.maximum(values, -bound), bound).astype(kind)


def setup_inputs(seed: int = 0) -> dict:
    splits = jax.random.split(jax.random.key(seed), 10)
    image = centred(splits[0], (IMAGES, NY, COLS, C), 1.0, 6.0, ((0, 4), (1, 64)))
    out_grad = centred(splits[1], (IMAGES, NY, COLS, C), 0.125, 1.0, ((0, 4), (1, 64)))
    w_qkv = draw_w_qkv(jax.random.fold_in(splits[9], 71), 0)
    w_proj = centred(splits[3], (2, HH, C), HH ** -0.5, 0.375)
    norm_gain = jnp.clip(1.0 + 0.15 * jax.random.normal(splits[4], (2, C), jnp.float32), 0.25, 1.75)
    norm_bias = centred(splits[5], (2, C), 0.5, 3.0, (), jnp.float32)
    logit_scale = jnp.clip(jax.random.uniform(splits[6], (2, HEADS), jnp.float32, 1.6, 2.8), 1.6, 2.8)
    row_band = draw_row_band(jax.random.fold_in(splits[9], 71), 0)
    col_band = draw_col_band(jax.random.fold_in(splits[9], 71), 0)
    return dict(image=image, out_grad=out_grad, w_qkv=w_qkv, w_proj=w_proj, norm_gain=norm_gain, norm_bias=norm_bias, logit_scale=logit_scale, row_band=row_band, col_band=col_band)


norm_eps = 1e-05
mask_value = -100.0

def project(tokens, weight, log_scale):
    token_count = tokens.shape[0]
    projected = jnp.dot(tokens, weight, preferred_element_type=jnp.float32)
    queries = projected[:, :HH].reshape(token_count, HEADS, HD)
    key_part = projected[:, HH:2 * HH].reshape(token_count, HEADS, HD)
    temper = jnp.exp(log_scale)[None, :, None]
    q_factor = lax.rsqrt(1.0 + lax.optimization_barrier(jnp.sum(queries * queries, -1, keepdims=True)))
    k_factor = lax.rsqrt(1.0 + lax.optimization_barrier(jnp.sum(key_part * key_part, -1, keepdims=True)))
    q_hat = (queries * q_factor * temper).reshape(token_count, HH).astype(jnp.bfloat16)
    k_hat = (key_part * k_factor).reshape(token_count, HH).astype(jnp.bfloat16)
    return (q_hat, k_hat, projected[:, 2 * HH:].astype(jnp.bfloat16))

def project_back(tokens, weight, log_scale, grad_q, grad_k, grad_v):
    token_count = tokens.shape[0]
    projected = jnp.dot(tokens, weight, preferred_element_type=jnp.float32)
    queries = projected[:, :HH].reshape(token_count, HEADS, HD)
    key_part = projected[:, HH:2 * HH].reshape(token_count, HEADS, HD)
    temper = jnp.exp(log_scale)[None, :, None]
    q_factor = lax.rsqrt(1.0 + lax.optimization_barrier(jnp.sum(queries * queries, -1, keepdims=True)))
    k_factor = lax.rsqrt(1.0 + lax.optimization_barrier(jnp.sum(key_part * key_part, -1, keepdims=True)))
    q_unit = queries * q_factor
    k_unit = key_part * k_factor
    scaled = grad_q.reshape(token_count, HEADS, HD) * temper
    d_query = q_factor * (scaled - q_unit * lax.optimization_barrier(jnp.sum(q_unit * scaled, -1, keepdims=True)))
    k_grad = grad_k.reshape(token_count, HEADS, HD)
    d_key = k_factor * (k_grad - k_unit * lax.optimization_barrier(jnp.sum(k_unit * k_grad, -1, keepdims=True)))
    d_projected = jnp.concatenate([d_query.reshape(token_count, HH), d_key.reshape(token_count, HH), grad_v], 1).astype(jnp.bfloat16)
    grad_weight = lax.dot_general(tokens, d_projected, (((0,), (0,)), ((), ())), preferred_element_type=jnp.float32)
    grad_tokens = lax.dot_general(d_projected, weight, (((1,), (1,)), ((), ())), preferred_element_type=jnp.float32)
    return (grad_tokens, grad_weight)

def normalized(attended, weight):
    outputs = jnp.dot(attended, weight, preferred_element_type=jnp.float32)
    centered = outputs - lax.optimization_barrier(jnp.mean(outputs, -1, keepdims=True))
    inverse = lax.rsqrt(lax.optimization_barrier(jnp.mean(centered * centered, -1, keepdims=True)) + norm_eps)
    return (centered * inverse, inverse)

def finish(tokens, attended, weight, gain_row, offset):
    y_hat, inverse = normalized(attended, weight)
    return (tokens.astype(jnp.float32) + y_hat * gain_row + offset).astype(jnp.bfloat16)

def finish_back(attended, weight, gain_row, grad_out):
    y_hat, inverse = normalized(attended, weight)
    grad_gain = lax.optimization_barrier(jnp.sum(grad_out * y_hat, 0))
    grad_offset = lax.optimization_barrier(jnp.sum(grad_out, 0))
    scaled = grad_out * gain_row
    grad_y = inverse * (scaled - lax.optimization_barrier(jnp.mean(scaled, -1, keepdims=True)) - y_hat * lax.optimization_barrier(jnp.mean(scaled * y_hat, -1, keepdims=True)))
    grad_y = grad_y.astype(jnp.bfloat16)
    grad_weight = lax.dot_general(attended, grad_y, (((0,), (0,)), ((), ())), preferred_element_type=jnp.float32)
    grad_attended = lax.dot_general(grad_y, weight, (((1,), (1,)), ((), ())), preferred_element_type=jnp.float32).astype(jnp.bfloat16)
    return (grad_attended, grad_weight, grad_gain, grad_offset)

def attend(q_hat, k_hat, values, labels):
    q_float = q_hat.astype(jnp.float32).reshape(-1, HEADS, HD)
    k_float = k_hat.astype(jnp.float32).reshape(-1, HEADS, HD)
    v_float = values.astype(jnp.float32).reshape(-1, HEADS, HD)
    scores = jnp.einsum('qhd,khd->hqk', q_float, k_float)
    scores = scores + jnp.where(labels[:, None] == labels[None, :], 0.0, mask_value)[None]
    highest = lax.optimization_barrier(jnp.max(scores, -1, keepdims=True))
    weights = jnp.exp(scores - highest)
    softmaxed = (weights / lax.optimization_barrier(jnp.sum(weights, -1, keepdims=True))).astype(jnp.bfloat16)
    attended = jnp.einsum('hqk,khd->qhd', softmaxed.astype(jnp.float32), v_float)
    return (attended.astype(jnp.bfloat16).reshape(-1, HH), softmaxed)

def attend_back(q_hat, k_hat, values, softmaxed, grad_attended):
    q_float = q_hat.astype(jnp.float32).reshape(-1, HEADS, HD)
    k_float = k_hat.astype(jnp.float32).reshape(-1, HEADS, HD)
    v_float = values.astype(jnp.float32).reshape(-1, HEADS, HD)
    g_float = grad_attended.astype(jnp.float32).reshape(-1, HEADS, HD)
    soft_float = softmaxed.astype(jnp.float32)
    grad_soft = jnp.einsum('qhd,khd->hqk', g_float, v_float)
    row_total = lax.optimization_barrier(jnp.sum(soft_float * grad_soft, -1, keepdims=True))
    rounded = lax.optimization_barrier((soft_float * (grad_soft - row_total)).astype(jnp.bfloat16))
    grad_scores = rounded.astype(jnp.float32)
    grad_q = jnp.einsum('hqk,khd->qhd', grad_scores, k_float).reshape(-1, HH)
    grad_k = jnp.einsum('hqk,qhd->khd', grad_scores, q_float).reshape(-1, HH)
    grad_v = jnp.einsum('hqk,qhd->khd', soft_float, g_float).reshape(-1, HH)
    return (grad_q, grad_k, grad_v)

def window_split(flat):
    depth = flat.shape[-1]
    return flat.reshape(NY // WIN, WIN, COLS // WIN, WIN, depth).transpose(0, 2, 1, 3, 4).reshape(-1, WIN * WIN, depth)

def window_join(windows):
    depth = windows.shape[-1]
    return windows.reshape(NY // WIN, COLS // WIN, WIN, WIN, depth).transpose(0, 2, 1, 3, 4).reshape(NY * COLS, depth)

def block_attention(flat_tokens, params, labels):
    w_mix, w_out, gain_row, offset, log_scale = params
    q_hat, k_hat, values = project(flat_tokens, w_mix, log_scale)
    label_win = window_split(labels.reshape(-1, 1))[:, :, 0]
    windows = (window_split(q_hat), window_split(k_hat), window_split(values), label_win)
    attended = lax.map(lambda window_item: attend(*window_item)[0], windows)
    return (window_join(attended), windows)

def block_forward(token_map, params, labels):
    flat_tokens = token_map.reshape(-1, C)
    attended, windows = block_attention(flat_tokens, params, labels)
    return finish(flat_tokens, attended, params[1], params[2], params[3]).reshape(NY, COLS, C)

def block_backward(token_map, grad_map, params, labels):
    w_mix, w_out, gain_row, offset, log_scale = params
    flat_tokens = token_map.reshape(-1, C)
    attended, windows = block_attention(flat_tokens, params, labels)
    grad_out = grad_map.reshape(-1, C).astype(jnp.float32)
    grad_att, grad_proj, grad_gain, grad_offset = finish_back(attended, w_out, gain_row, grad_out)

    def one_window(window_item):
        q_part, k_part, v_part, label_part, grad_part = window_item
        attended_part, softmaxed = attend(q_part, k_part, v_part, label_part)
        return attend_back(q_part, k_part, v_part, softmaxed, grad_part)
    grad_q, grad_k, grad_v = lax.map(one_window, windows + (window_split(grad_att),))
    grad_from, grad_mix = project_back(flat_tokens, w_mix, log_scale, window_join(grad_q), window_join(grad_k), window_join(grad_v))
    grad_total = (grad_out + grad_from).reshape(NY, COLS, C)
    return (grad_total, (grad_mix, grad_proj, grad_gain, grad_offset))

def reference(image, out_grad, w_qkv, w_proj, norm_gain, norm_bias, logit_scale, row_band, col_band):
    region = 3 * row_band[:, None] + col_band[None, :]
    no_regions = jnp.zeros((NY, COLS), jnp.int32)
    first_params = (w_qkv[0], w_proj[0], norm_gain[0], norm_bias[0], logit_scale[0])
    second_params = (w_qkv[1], w_proj[1], norm_gain[1], norm_bias[1], logit_scale[1])

    def one_image(image_item):
        image_map, grad_map = image_item
        out_first = block_forward(image_map, first_params, no_regions)
        rolled = jnp.roll(out_first, (-SHIFT, -SHIFT), (0, 1))
        grad_rolled = jnp.roll(grad_map, (-SHIFT, -SHIFT), (0, 1))
        grad_second, grads_second = block_backward(rolled, grad_rolled, second_params, region)
        grad_first = jnp.roll(grad_second.astype(jnp.bfloat16), (SHIFT, SHIFT), (0, 1))
        grad_input, grads_first = block_backward(image_map, grad_first, first_params, no_regions)
        stacked = tuple((jnp.stack([early_grad, late_grad]) for early_grad, late_grad in zip(grads_first, grads_second)))
        return (grad_input.astype(jnp.bfloat16), stacked)
    grad_image, weight_grads = lax.map(one_image, (image, out_grad))
    return (grad_image, lax.optimization_barrier(jnp.sum(weight_grads[0], 0)), lax.optimization_barrier(jnp.sum(weight_grads[1], 0)), lax.optimization_barrier(jnp.sum(weight_grads[2], 0)), lax.optimization_barrier(jnp.sum(weight_grads[3], 0)))
```

```python
import functools

import jax
import jax.numpy as jnp
from jax import lax
from jax.experimental import pallas as pl
from jax.experimental.pallas import tpu as pltpu
from jax.sharding import PartitionSpec as P

C = 512
HEADS = 8
HD = 32
WIN = 24
HH = 256
SHIFT = 12
GROUP = 8
TOK = 144
CELLS = WIN * WIN
ROWS_DEV = 3
PACK = 48
DEVS = 64

norm_eps = 1e-05
mask_value = 100.0
f32 = jnp.float32
bf16 = jnp.bfloat16


def dot(a, b):
    return jnp.dot(a, b, preferred_element_type=f32)


def dot_t(a, b):
    return lax.dot_general(a, b, (((1,), (1,)), ((), ())), preferred_element_type=f32)


def dot_0(a, b):
    return lax.dot_general(a, b, (((0,), (0,)), ((), ())), preferred_element_type=f32)


def iota(shape, axis):
    return lax.broadcasted_iota(jnp.int32, shape, axis)


def head_sums(x):
    width = x.shape[1]
    ones = (iota((width, width), 0) // HD == iota((width, width), 1) // HD).astype(f32).astype(bf16)
    high = x.astype(bf16)
    low = (x - high.astype(f32)).astype(bf16)
    return dot(high, ones) + dot(low, ones)


def split_two(x):
    high = x.astype(bf16).astype(f32)
    return high, x - high


def lane_slice(x, at):
    return x[:, at : at + HD]


def send_projected(tokens, weight, scale_ref, block, out_ref):
    projected = dot(tokens, weight)
    query, key, value = projected[:, :HH], projected[:, HH : 2 * HH], projected[:, 2 * HH :]
    lane = iota((1, HH), 1)
    scale = jnp.zeros((1, HH), f32)
    for h in range(HEADS):
        scale = jnp.where(lane // HD == h, scale_ref[block, h], scale)
    q_factor = lax.rsqrt(1.0 + head_sums(query * query))
    k_factor = lax.rsqrt(1.0 + head_sums(key * key))
    q_hat = query * q_factor * jnp.exp(scale)
    k_hat = key * k_factor
    q_high, q_low = split_two(q_factor)
    k_high, k_low = split_two(k_factor)
    slot = iota(q_hat.shape, 1) % HD
    extra = jnp.where(
        slot == 0,
        q_high,
        jnp.where(slot == 1, q_low, jnp.where(slot == 2, k_high, jnp.where(slot == 3, k_low, 0.0))),
    )
    for h in range(HEADS):
        at = h * HD
        out_ref[h] = jnp.concatenate(
            [lane_slice(q_hat, at), lane_slice(k_hat, at), lane_slice(value, at), lane_slice(extra, at)], 1
        ).astype(bf16)


def unpack_heads(packed_ref):
    packed = [packed_ref[h].astype(f32) for h in range(HEADS)]
    rows = [
        jnp.concatenate([lane_slice(packed[h], r * HD) for h in range(HEADS)], 1)
        for r in range(ROWS_DEV)
    ]
    return jnp.concatenate(rows, 0).astype(bf16)


def pack_heads(array, out_ref):
    zeros = jnp.zeros((PACK, HD), f32)
    for h in range(HEADS):
        out_ref[h] = jnp.concatenate(
            [lane_slice(array[r * PACK : (r + 1) * PACK], h * HD) for r in range(ROWS_DEV)] + [zeros], 1
        ).astype(bf16)


def to_windows(array):
    split = array.reshape(GROUP, ROWS_DEV, 2, WIN, array.shape[-1])
    return [split[:, :, w].reshape(CELLS, array.shape[-1]) for w in range(2)]


def from_windows(pair):
    depth = pair[0].shape[-1]
    parts = [part.reshape(GROUP, ROWS_DEV, 1, WIN, depth) for part in pair]
    return jnp.concatenate(parts, 2).reshape(GROUP, TOK, depth)


def roll_tokens(array, by):
    by = by % TOK
    return jnp.concatenate([array[TOK - by :], array[: TOK - by]], 0)


def normalized(attended, weight):
    outputs = dot(attended, weight)
    centered = outputs - jnp.mean(outputs, -1, keepdims=True)
    inverse = lax.rsqrt(jnp.mean(centered * centered, -1, keepdims=True) + norm_eps)
    return centered * inverse, inverse


def finish_back(attended, weight, gain_row, grad_out):
    y_hat, inverse = normalized(attended, weight)
    grad_gain = jnp.sum(grad_out * y_hat, 0, keepdims=True)
    grad_bias = jnp.sum(grad_out, 0, keepdims=True)
    scaled = grad_out * gain_row
    grad_y = inverse * (
        scaled
        - jnp.mean(scaled, -1, keepdims=True)
        - y_hat * jnp.mean(scaled * y_hat, -1, keepdims=True)
    )
    grad_y = grad_y.astype(bf16)
    gains = jnp.concatenate([grad_gain, grad_bias, jnp.zeros((6, C), f32)], 0)
    return grad_y, dot_t(grad_y, weight), gains


def labels_of(axis, window, first_row, row_ref, col_ref):
    shape = (CELLS, 1) if axis == 0 else (1, CELLS)
    at = iota(shape, axis)
    source = at // (ROWS_DEV * WIN)
    rest = at - source * (ROWS_DEV * WIN)
    local_row = rest // WIN
    column = rest - local_row * WIN + window * WIN
    local_row = local_row + (column >= 36).astype(jnp.int32)
    local_row = jnp.where(local_row >= ROWS_DEV, local_row - ROWS_DEV, local_row)
    row = first_row + source * ROWS_DEV + local_row
    row_label = jnp.zeros(shape, jnp.int32)
    col_label = jnp.zeros(shape, jnp.int32)
    for label in (1, 2):
        row_cut = jnp.sum((row_ref[...] < label).astype(jnp.int32), 1, keepdims=True)
        col_cut = jnp.sum((col_ref[...] < label).astype(jnp.int32), 1, keepdims=True)
        row_label = row_label + (row >= row_cut).astype(jnp.int32)
        col_label = col_label + (column >= col_cut).astype(jnp.int32)
    return 3 * row_label + col_label


def masked(scores, window, mask_refs):
    if mask_refs is None:
        return scores
    first_row = mask_refs[0][0]
    one = labels_of(0, window, first_row, *mask_refs[1:])
    two = labels_of(1, window, first_row, *mask_refs[1:])
    return scores - jnp.where(one == two, 0.0, mask_value)


def attend_kernel(masks, x_ref, *refs):
    mask_refs = refs[:3] if masks else None
    out_ref, saved_ref = refs[-2:]
    lane = iota((CELLS, 128), 1)
    per_window = []
    for w, cells in enumerate(to_windows(x_ref[...].astype(f32))):
        query = cells[:, :HD].astype(bf16)
        key = cells[:, HD : 2 * HD].astype(bf16)
        value = jnp.where(lane < HD, pltpu.roll(cells, 64, 1), jnp.where(lane == HD, 1.0, 0.0)).astype(bf16)
        scores = masked(dot_t(query, key), w, mask_refs)
        weights = jnp.exp(scores).astype(bf16)
        summed = dot(weights, value)
        inverse = 1.0 / summed[:, HD : HD + 1]
        attended = jnp.where(lane < HD, summed * inverse, 0.0)
        saved_ref[w] = jnp.where(lane == HD, inverse, attended)
        per_window.append(attended.reshape(GROUP, ROWS_DEV, WIN, 128))
    total = 0.0
    for r in range(ROWS_DEV):
        rows = jnp.concatenate([part[:, r] for part in per_window], 1).reshape(GROUP * PACK, 128)
        total = total + (rows if r == 0 else pltpu.roll(rows, r * HD, 1))
    out_ref[...] = total.astype(bf16).reshape(GROUP, PACK, 128)


def attend_back_kernel(block, masks, head_ref, scale_ref, x_ref, saved_ref, grad_ref, *refs):
    mask_refs = refs[:3] if masks else None
    out_ref = refs[-1]
    lane = iota((CELLS, 128), 1)
    scale_row = jnp.exp(jnp.full((1, 128), scale_ref[block, head_ref[0]], f32))
    packed = grad_ref[...].astype(f32).reshape(GROUP * PACK, 128)
    rolled = [packed if r == 0 else pltpu.roll(packed, 128 - r * HD, 1) for r in range(ROWS_DEV)]
    rolled = [part.reshape(GROUP, 1, 2, WIN, 128) for part in rolled]
    grads = jnp.concatenate(rolled, 1)
    results = []
    for w, cells in enumerate(to_windows(x_ref[...].astype(f32))):
        saved = saved_ref[w]
        grad = grads[:, :, w].reshape(CELLS, 128)
        inverse = saved[:, HD : HD + 1]
        grad = jnp.where(lane < HD, grad * inverse, 0.0).astype(bf16).astype(f32)
        row = jnp.sum(grad * saved, 1, keepdims=True)
        row_high, row_low = split_two(row)
        grad_ext = jnp.where(lane == HD, -row_high, jnp.where(lane == HD + 1, -row_low, grad)).astype(bf16)
        ones = jnp.where((lane == HD) | (lane == HD + 1), 1.0, 0.0)
        value_ext = jnp.where(lane < HD, pltpu.roll(cells, 64, 1), ones).astype(bf16)
        query = cells[:, :HD].astype(bf16)
        key = cells[:, HD : 2 * HD].astype(bf16)
        scores = masked(dot_t(key, query), w, mask_refs)
        weights = jnp.exp(scores).astype(bf16)
        grad_scores = (weights.astype(f32) * dot_t(value_ext, grad_ext)).astype(bf16)
        query_at = jnp.where((lane >= HD) & (lane < 2 * HD), pltpu.roll(cells, HD, 1), 0.0).astype(bf16)
        grad_at = pltpu.roll(grad, 2 * HD, 1).astype(bf16)
        grad_kv = dot(grad_scores, query_at) + dot(weights, grad_at)
        key_at = jnp.where(lane < HD, pltpu.roll(cells, 128 - HD, 1), 0.0).astype(bf16)
        grad_q = dot_0(grad_scores, key_at)
        total = jnp.where(lane < HD, grad_q * scale_row, grad_kv)
        unit = jnp.where(lane < HD, cells / scale_row, jnp.where(lane < 2 * HD, cells, 0.0))
        q_factor = cells[:, 96:97] + cells[:, 97:98]
        k_factor = cells[:, 98:99] + cells[:, 99:100]
        factor = jnp.where(lane < HD, q_factor, jnp.where(lane < 2 * HD, k_factor, 1.0))
        result = factor * (total - unit * head_sums(unit * total))
        results.append(jnp.where(lane >= 96, pltpu.roll(saved, 96, 1), result))
    out_ref[...] = from_windows(results).astype(bf16)


def first_kernel(scale_ref, tokens_ref, w_ref, out_ref):
    send_projected(tokens_ref[...], w_ref[...], scale_ref, 0, out_ref)


def middle_kernel(scale_ref, packed_ref, tokens_ref, w_proj_ref, gain_ref, bias_ref, w_ref, rolled_ref, out_ref):
    attended = unpack_heads(packed_ref)
    y_hat, _ = normalized(attended, w_proj_ref[...])
    out = (tokens_ref[...].astype(f32) + y_hat * gain_ref[0:1] + bias_ref[0:1]).astype(bf16).astype(f32)
    rolled = roll_tokens(out, -SHIFT).astype(bf16)
    rolled_ref[...] = rolled
    send_projected(rolled, w_ref[...], scale_ref, 1, out_ref)


def turn_kernel(packed_ref, grad_ref, w_proj_ref, gain_ref, out_ref, grad_y_ref, gains_ref):
    attended = unpack_heads(packed_ref)
    grad = roll_tokens(grad_ref[...].astype(f32), -SHIFT)
    grad_y, grad_att, gains = finish_back(attended, w_proj_ref[...], gain_ref[1:2], grad)
    pack_heads(grad_att, out_ref)
    grad_y_ref[...] = grad_y
    gains_ref[...] = gains


def gather_qkv(qkv_ref):
    parts = [qkv_ref[h].astype(f32) for h in range(HEADS)]
    return jnp.concatenate(
        [lane_slice(parts[h], kind * HD) for kind in range(3) for h in range(HEADS)], 1
    ).astype(bf16)


def back_kernel(
    qkv_ref, w_ref, grad_ref, packed_ref, w_proj_ref, gain_ref, out_ref, grad0_ref, grad_proj_ref, gains_ref
):
    from_qkv = roll_tokens(dot_t(gather_qkv(qkv_ref), w_ref[...]), SHIFT)
    grad = (grad_ref[...].astype(f32) + from_qkv).astype(bf16)
    grad0_ref[...] = grad
    attended = unpack_heads(packed_ref)
    grad_y, grad_att, gains = finish_back(attended, w_proj_ref[...], gain_ref[0:1], grad.astype(f32))
    pack_heads(grad_att, out_ref)
    grad_proj_ref[...] = dot_0(grad_y, attended)
    gains_ref[...] = gains


def last_kernel(qkv_ref, w_ref, grad_ref, out_ref):
    from_qkv = dot_t(gather_qkv(qkv_ref), w_ref[...])
    out_ref[...] = (grad_ref[...].astype(f32) + from_qkv).astype(bf16)


def weights_kernel(
    qkv0_ref, qkv1_ref, tokens0_ref, tokens1_ref, grad_y1_ref, grad_proj0_ref, gains0_ref, gains1_ref, out_ref
):
    qkv0 = qkv0_ref[...].reshape(GROUP * TOK, 128)
    qkv1 = qkv1_ref[...].reshape(GROUP * TOK, 128)
    grad0 = dot_0(qkv0, tokens0_ref[...])
    grad1 = dot_0(qkv1, tokens1_ref[...])
    proj1 = dot_0(qkv1, grad_y1_ref[...])
    pieces = []
    for ref in (gains0_ref, gains1_ref):
        for row in (0, 1):
            pieces += split_two(ref[row : row + 1])
    grad0 = jnp.concatenate([grad0[:96]] + [jnp.concatenate(pieces, 0), jnp.zeros((24, C), f32)], 0)
    grad1 = jnp.concatenate([grad1[:96], proj1[96:]], 0)
    upper = jnp.concatenate([grad1.T, grad0.T], 1).reshape(DEVS, 8, 256)
    lower = grad_proj0_ref[...].reshape(DEVS, 8, 256)
    out_ref[...] = jnp.concatenate([upper, lower], 1).astype(bf16)


def reduce_kernel(parts_ref, out_ref):
    summed = jnp.sum(parts_ref[...].astype(f32).reshape(8, 8, 16, 256), 0)
    late = [summed[(h + GROUP // 2) % GROUP, :8, :128] for h in range(HEADS)]
    early = [summed[h, :8, 128:] for h in range(HEADS)]
    proj0 = jnp.sum(summed[:, 8:], 0)
    gains = jnp.sum(summed[:, :8, 128:], 0)
    pieces = [lane_slice(part, kind * HD) for kind in range(3) for part in early]
    pieces += [lane_slice(part, kind * HD) for kind in range(3) for part in late]
    pieces += [proj0]
    pieces += [lane_slice(part, 96) for part in late]
    pieces += [gains]
    out_ref[...] = jnp.concatenate(pieces, 1)


def final_kernel(a_ref, b_ref, c_ref, d_ref, qkv_ref, proj_ref, gains_ref):
    total = (a_ref[...] + b_ref[...]) + (c_ref[...] + d_ref[...])
    qkv_ref[0] = total[:, :768]
    qkv_ref[1] = total[:, 768:1536]
    proj_ref[0] = total[:, 1536:1792].T
    proj_ref[1] = total[:, 1792:2048].T
    gains_ref[...] = total[:, 2048:2176].T


def call(kernel, outs, smem, *args):
    specs = [pl.BlockSpec(memory_space=pltpu.SMEM)] * smem
    specs += [pl.BlockSpec(memory_space=pltpu.VMEM)] * (len(args) - smem)
    return pl.pallas_call(
        kernel,
        out_shape=[jax.ShapeDtypeStruct(shape, dtype) for shape, dtype in outs],
        in_specs=specs,
        out_specs=[pl.BlockSpec(memory_space=pltpu.VMEM)] * len(outs),
        compiler_params=pltpu.CompilerParams(vmem_limit_bytes=40 * 2**20),
    )(*args)


def body(image, out_grad, w_qkv, w_proj, norm_gain, norm_bias, logit_scale, row_band, col_band):
    position = lax.axis_index("rows")
    aligned = [[GROUP * g + i for i in range(GROUP)] for g in range(DEVS // GROUP)]
    half = GROUP // 2
    moved = [[(GROUP * g + half + i) % DEVS for i in range(GROUP)] for g in range(DEVS // GROUP)]
    moved_position = (position + DEVS - half) % DEVS
    head0 = (position % GROUP).reshape(1)
    head1 = (moved_position % GROUP).reshape(1)
    first_row = (moved_position // GROUP * WIN).reshape(1)
    masks = (first_row, row_band.reshape(1, -1), col_band.reshape(1, -1))

    def exchange(array, groups):
        return lax.all_to_all(array, "rows", 0, 0, axis_index_groups=groups, tiled=True)

    def gather(array, groups):
        return lax.all_gather(array, "rows", axis_index_groups=groups, tiled=True)

    tokens0 = image.reshape(TOK, C)
    grad_out = out_grad.reshape(TOK, C)
    wide = ((GROUP, TOK, 128), bf16)
    narrow = ((GROUP, PACK, 128), bf16)
    saved = ((2, CELLS, 128), f32)
    cells = ((TOK, C), bf16)
    gains = ((8, C), f32)

    tokens0_all = gather(tokens0, aligned)
    (x0,) = call(first_kernel, [wide], 1, logit_scale, tokens0, w_qkv[0])
    x0 = exchange(x0, aligned)
    a0, saved0 = call(functools.partial(attend_kernel, False), [narrow, saved], 0, x0)
    a0 = exchange(a0, aligned)
    tokens1, x1 = call(
        middle_kernel, [cells, wide], 1, logit_scale, a0, tokens0, w_proj[0], norm_gain, norm_bias, w_qkv[1]
    )
    tokens1_all = gather(tokens1, moved)
    x1 = exchange(x1, moved)
    mask_specs = 1

    def masked_call(kernel, outs, scalars, arrays):
        specs = [pl.BlockSpec(memory_space=pltpu.SMEM)] * len(scalars)
        specs += [pl.BlockSpec(memory_space=pltpu.VMEM)] * len(arrays)
        specs += [pl.BlockSpec(memory_space=pltpu.SMEM)] * mask_specs
        specs += [pl.BlockSpec(memory_space=pltpu.VMEM)] * 2
        return pl.pallas_call(
            kernel,
            out_shape=[jax.ShapeDtypeStruct(shape, dtype) for shape, dtype in outs],
            in_specs=specs,
            out_specs=[pl.BlockSpec(memory_space=pltpu.VMEM)] * len(outs),
            compiler_params=pltpu.CompilerParams(vmem_limit_bytes=40 * 2**20),
        )(*scalars, *arrays, *masks)

    a1, saved1 = masked_call(functools.partial(attend_kernel, True), [narrow, saved], (), (x1,))
    a1 = exchange(a1, moved)
    d1, grad_y1, gains1 = call(turn_kernel, [narrow, cells, gains], 0, a1, grad_out, w_proj[1], norm_gain)
    grad_y1_all = gather(grad_y1, moved)
    d1 = exchange(d1, moved)
    (qkv1,) = masked_call(
        functools.partial(attend_back_kernel, 1, True), [wide], (head1, logit_scale), (x1, saved1, d1)
    )
    d_qkv1 = exchange(qkv1, moved)
    d0, grad0, grad_proj0, gains0 = call(
        back_kernel,
        [narrow, cells, ((C, HH), f32), gains],
        0,
        d_qkv1,
        w_qkv[1],
        grad_out,
        a0,
        w_proj[0],
        norm_gain,
    )
    d0 = exchange(d0, aligned)
    (qkv0,) = call(
        functools.partial(attend_back_kernel, 0, False), [wide], 2, head0, logit_scale, x0, saved0, d0
    )
    (parts,) = call(
        weights_kernel,
        [((DEVS, 16, 256), bf16)],
        0,
        qkv0,
        qkv1,
        tokens0_all,
        tokens1_all,
        grad_y1_all,
        grad_proj0,
        gains0,
        gains1,
    )
    parts = lax.all_to_all(parts, "rows", 0, 0, tiled=True)
    (share,) = call(reduce_kernel, [((8, 2176), f32)], 0, parts)
    others = [lax.ppermute(share, "dp", [(i, i ^ k) for i in range(4)]) for k in (1, 2, 3)]
    d_qkv0 = exchange(qkv0, aligned)
    (grad_image,) = call(last_kernel, [cells], 0, d_qkv0, w_qkv[0], grad0)
    grad_qkv, grad_proj, small = call(
        final_kernel, [((2, 8, 768), f32), ((2, HH, 8), f32), ((128, 8), f32)], 0, share, *others
    )
    small = small[96:104].reshape(2, 2, 2, 8).sum(2)
    return (grad_image.reshape(image.shape), grad_qkv, grad_proj, small[:, 0], small[:, 1])


def solution(mesh):
    placed = (P("dp", "rows", None, None), P("dp", "rows", None, None)) + (P(),) * 7
    return jax.shard_map(
        body,
        mesh=mesh,
        in_specs=placed,
        out_specs=(
            P("dp", "rows", None, None),
            P(None, "rows", None),
            P(None, None, "rows"),
            P(None, "rows"),
            P(None, "rows"),
        ),
        check_vma=False,
    )
```

```python
import functools

import jax
import jax.numpy as jnp
from jax import lax
from jax.experimental import pallas as pl
from jax.experimental.pallas import tpu as pltpu
from jax.sharding import PartitionSpec as P

C = 512
HEADS = 8
HD = 32
WIN = 24
HH = 256
SHIFT = 12
GROUP = 8
TOK = 144
CELLS = WIN * WIN
ROWS_DEV = 3
PACK = 48
DEVS = 64
SENT = 2 * 3 * HH + 2 * HH + 128
HALF = 1152

norm_eps = 1e-05
mask_value = 100.0
f32 = jnp.float32
bf16 = jnp.bfloat16


def dot(a, b):
    return jnp.dot(a, b, preferred_element_type=f32)


def dot_t(a, b):
    return lax.dot_general(a, b, (((1,), (1,)), ((), ())), preferred_element_type=f32)


def dot_0(a, b):
    return lax.dot_general(a, b, (((0,), (0,)), ((), ())), preferred_element_type=f32)


def iota(shape, axis):
    return lax.broadcasted_iota(jnp.int32, shape, axis)


def head_sums(x):
    width = x.shape[1]
    ones = (iota((width, width), 0) // HD == iota((width, width), 1) // HD).astype(f32).astype(bf16)
    high = x.astype(bf16)
    low = (x - high.astype(f32)).astype(bf16)
    return dot(high, ones) + dot(low, ones)


def split_two(x):
    high = x.astype(bf16).astype(f32)
    return high, x - high


def lane_slice(x, at):
    return x[:, at : at + HD]


def send_projected(tokens, weight, scale_ref, block, out_ref):
    projected = dot(tokens, weight)
    query, key, value = projected[:, :HH], projected[:, HH : 2 * HH], projected[:, 2 * HH :]
    lane = iota((1, HH), 1)
    scale = jnp.zeros((1, HH), f32)
    for h in range(HEADS):
        scale = jnp.where(lane // HD == h, scale_ref[block, h], scale)
    q_factor = lax.rsqrt(1.0 + head_sums(query * query))
    k_factor = lax.rsqrt(1.0 + head_sums(key * key))
    q_hat = query * q_factor * jnp.exp(scale)
    k_hat = key * k_factor
    q_high, q_low = split_two(q_factor)
    k_high, k_low = split_two(k_factor)
    slot = iota(q_hat.shape, 1) % HD
    extra = jnp.where(
        slot == 0,
        q_high,
        jnp.where(slot == 1, q_low, jnp.where(slot == 2, k_high, jnp.where(slot == 3, k_low, 0.0))),
    )
    for h in range(HEADS):
        at = h * HD
        out_ref[h] = jnp.concatenate(
            [lane_slice(q_hat, at), lane_slice(k_hat, at), lane_slice(value, at), lane_slice(extra, at)], 1
        ).astype(bf16)


def unpack_heads(packed_ref):
    packed = [packed_ref[h].astype(f32) for h in range(HEADS)]
    rows = [
        jnp.concatenate([lane_slice(packed[h], r * HD) for h in range(HEADS)], 1)
        for r in range(ROWS_DEV)
    ]
    return jnp.concatenate(rows, 0).astype(bf16)


def pack_heads(array, out_ref):
    zeros = jnp.zeros((PACK, HD), f32)
    for h in range(HEADS):
        out_ref[h] = jnp.concatenate(
            [lane_slice(array[r * PACK : (r + 1) * PACK], h * HD) for r in range(ROWS_DEV)] + [zeros], 1
        ).astype(bf16)


def to_windows(array):
    split = array.reshape(GROUP, ROWS_DEV, 2, WIN, array.shape[-1])
    return [split[:, :, w].reshape(CELLS, array.shape[-1]) for w in range(2)]


def from_windows(pair):
    depth = pair[0].shape[-1]
    parts = [part.reshape(GROUP, ROWS_DEV, 1, WIN, depth) for part in pair]
    return jnp.concatenate(parts, 2).reshape(GROUP, TOK, depth)


def roll_tokens(array, by):
    by = by % TOK
    return jnp.concatenate([array[TOK - by :], array[: TOK - by]], 0)


def normalized(attended, weight):
    outputs = dot(attended, weight)
    centered = outputs - jnp.mean(outputs, -1, keepdims=True)
    inverse = lax.rsqrt(jnp.mean(centered * centered, -1, keepdims=True) + norm_eps)
    return centered * inverse, inverse


def finish_back(attended, weight, gain_row, grad_out):
    y_hat, inverse = normalized(attended, weight)
    grad_gain = jnp.sum(grad_out * y_hat, 0, keepdims=True)
    grad_bias = jnp.sum(grad_out, 0, keepdims=True)
    scaled = grad_out * gain_row
    grad_y = inverse * (
        scaled
        - jnp.mean(scaled, -1, keepdims=True)
        - y_hat * jnp.mean(scaled * y_hat, -1, keepdims=True)
    )
    grad_y = grad_y.astype(bf16)
    gains = jnp.concatenate([grad_gain, grad_bias, jnp.zeros((6, C), f32)], 0)
    return grad_y, dot_t(grad_y, weight), gains


def labels_of(axis, window, first_row, row_ref, col_ref):
    shape = (CELLS, 1) if axis == 0 else (1, CELLS)
    at = iota(shape, axis)
    source = at // (ROWS_DEV * WIN)
    rest = at - source * (ROWS_DEV * WIN)
    local_row = rest // WIN
    column = rest - local_row * WIN + window * WIN
    local_row = local_row + (column >= 36).astype(jnp.int32)
    local_row = jnp.where(local_row >= ROWS_DEV, local_row - ROWS_DEV, local_row)
    row = first_row + source * ROWS_DEV + local_row
    row_label = jnp.zeros(shape, jnp.int32)
    col_label = jnp.zeros(shape, jnp.int32)
    for label in (1, 2):
        row_cut = jnp.sum((row_ref[...] < label).astype(jnp.int32), 1, keepdims=True)
        col_cut = jnp.sum((col_ref[...] < label).astype(jnp.int32), 1, keepdims=True)
        row_label = row_label + (row >= row_cut).astype(jnp.int32)
        col_label = col_label + (column >= col_cut).astype(jnp.int32)
    return 3 * row_label + col_label


def masked(scores, window, mask_refs):
    if mask_refs is None:
        return scores
    first_row = mask_refs[0][0]
    one = labels_of(0, window, first_row, *mask_refs[1:])
    two = labels_of(1, window, first_row, *mask_refs[1:])
    return scores - jnp.where(one == two, 0.0, mask_value)


def attend_kernel(masks, x_ref, *refs):
    mask_refs = refs[:3] if masks else None
    out_ref = refs[-1]
    lane = iota((CELLS, 128), 1)
    per_window = []
    for w, cells in enumerate(to_windows(x_ref[...].astype(f32))):
        query = cells[:, :HD].astype(bf16)
        key = cells[:, HD : 2 * HD].astype(bf16)
        value = jnp.where(lane < HD, pltpu.roll(cells, 64, 1), jnp.where(lane == HD, 1.0, 0.0)).astype(bf16)
        scores = masked(dot_t(query, key), w, mask_refs)
        weights = jnp.exp(scores).astype(bf16)
        summed = dot(weights, value)
        attended = jnp.where(lane < HD, summed * (1.0 / summed[:, HD : HD + 1]), 0.0)
        per_window.append(attended.reshape(GROUP, ROWS_DEV, WIN, 128))
    total = 0.0
    for r in range(ROWS_DEV):
        rows = jnp.concatenate([part[:, r] for part in per_window], 1).reshape(GROUP * PACK, 128)
        total = total + (rows if r == 0 else pltpu.roll(rows, r * HD, 1))
    out_ref[...] = total.astype(bf16).reshape(GROUP, PACK, 128)


def attend_back_kernel(block, masks, head_ref, scale_ref, x_ref, grad_ref, *refs):
    mask_refs = refs[:3] if masks else None
    out_ref = refs[-1]
    lane = iota((CELLS, 128), 1)
    low = iota((HD, CELLS), 0)
    scale_row = jnp.exp(jnp.full((1, 128), scale_ref[block, head_ref[0]], f32))
    packed = grad_ref[...].astype(f32).reshape(GROUP * PACK, 128)
    rolled = [packed if r == 0 else pltpu.roll(packed, 128 - r * HD, 1) for r in range(ROWS_DEV)]
    rolled = [part.reshape(GROUP, 1, 2, WIN, 128) for part in rolled]
    grads = jnp.concatenate(rolled, 1)
    results = []
    for w, cells in enumerate(to_windows(x_ref[...].astype(f32))):
        turned = cells.T
        query_t = turned[:HD].astype(bf16)
        key_t = turned[HD : 2 * HD].astype(bf16)
        value_t = turned[2 * HD : 3 * HD]
        grad_t = grads[:, :, w].reshape(CELLS, 128).T[:HD]
        key = cells[:, HD : 2 * HD].astype(bf16)
        scores = masked(dot(key, query_t), w, mask_refs)
        weights = jnp.exp(scores).astype(bf16)
        summed = dot(jnp.concatenate([value_t, jnp.where(low == 0, 1.0, 0.0)], 0).astype(bf16), weights)
        inverse = 1.0 / summed[HD : HD + 1]
        grad_t = (grad_t * inverse).astype(bf16).astype(f32)
        row_high, row_low = split_two(jnp.sum(grad_t * summed[:HD], 0, keepdims=True) * inverse)
        rows = jnp.where(low == 0, -row_high, jnp.where(low == 1, -row_low, 0.0))
        grad_ext = jnp.concatenate([grad_t, rows], 0).astype(bf16)
        ones = jnp.where(lane < HD + 2, 1.0, 0.0)
        value_ext = jnp.where(lane < HD, pltpu.roll(cells, 64, 1), ones)[:, :64].astype(bf16)
        grad_scores = (weights.astype(f32) * dot(value_ext, grad_ext)).astype(bf16)
        query_at = jnp.where((lane >= HD) & (lane < 2 * HD), pltpu.roll(cells, HD, 1), 0.0).astype(bf16)
        zeros = jnp.zeros((HD, CELLS), f32)
        grad_at = jnp.concatenate([zeros, zeros, grad_t, zeros], 0).T.astype(bf16)
        grad_kv = dot(grad_scores, query_at) + dot(weights, grad_at)
        grad_q = dot(key_t, grad_scores)
        grad_q = jnp.concatenate([grad_q, zeros, zeros, zeros], 0).T
        total = jnp.where(lane < HD, grad_q * scale_row, grad_kv)
        unit = jnp.where(lane < HD, cells / scale_row, jnp.where(lane < 2 * HD, cells, 0.0))
        q_factor = cells[:, 96:97] + cells[:, 97:98]
        k_factor = cells[:, 98:99] + cells[:, 99:100]
        factor = jnp.where(lane < HD, q_factor, jnp.where(lane < 2 * HD, k_factor, 1.0))
        results.append(factor * (total - unit * head_sums(unit * total)))
    out_ref[...] = from_windows(results).astype(bf16)


def first_kernel(scale_ref, tokens_ref, w_ref, out_ref):
    send_projected(tokens_ref[...], w_ref[0], scale_ref, 0, out_ref)


def middle_kernel(scale_ref, packed_ref, tokens_ref, w_proj_ref, gain_ref, bias_ref, w_ref, rolled_ref, out_ref):
    attended = unpack_heads(packed_ref)
    y_hat, _ = normalized(attended, w_proj_ref[0])
    out = (tokens_ref[...].astype(f32) + y_hat * gain_ref[0:1] + bias_ref[0:1]).astype(bf16).astype(f32)
    rolled = roll_tokens(out, -SHIFT).astype(bf16)
    rolled_ref[...] = rolled
    send_projected(rolled, w_ref[1], scale_ref, 1, out_ref)


def turn_kernel(packed_ref, grad_ref, w_proj_ref, gain_ref, out_ref, grad_proj_ref, gains_ref):
    attended = unpack_heads(packed_ref)
    grad = roll_tokens(grad_ref[...].astype(f32), -SHIFT)
    grad_y, grad_att, gains = finish_back(attended, w_proj_ref[1], gain_ref[1:2], grad)
    pack_heads(grad_att, out_ref)
    grad_proj_ref[...] = dot_0(grad_y, attended).astype(bf16)
    gains_ref[...] = gains


def gather_qkv(qkv_ref):
    parts = [qkv_ref[h].astype(f32) for h in range(HEADS)]
    return jnp.concatenate(
        [lane_slice(parts[h], kind * HD) for kind in range(3) for h in range(HEADS)], 1
    ).astype(bf16)


def back_kernel(
    qkv_ref,
    w_ref,
    tokens_ref,
    grad_ref,
    packed_ref,
    w_proj_ref,
    gain_ref,
    out_ref,
    grad0_ref,
    grad_qkv_ref,
    grad_proj_ref,
    gains_ref,
):
    d_qkv = gather_qkv(qkv_ref)
    from_qkv = roll_tokens(dot_t(d_qkv, w_ref[1]), SHIFT)
    grad = (grad_ref[...].astype(f32) + from_qkv).astype(bf16)
    grad0_ref[...] = grad
    attended = unpack_heads(packed_ref)
    grad_y, grad_att, gains = finish_back(attended, w_proj_ref[0], gain_ref[0:1], grad.astype(f32))
    pack_heads(grad_att, out_ref)
    grad_qkv_ref[...] = dot_0(tokens_ref[...], d_qkv).astype(bf16)
    grad_proj_ref[...] = dot_0(grad_y, attended).astype(bf16)
    gains_ref[...] = gains


def last_kernel(
    qkv_ref,
    w_ref,
    tokens_ref,
    grad_ref,
    grad_qkv1_ref,
    proj0_ref,
    proj1_ref,
    gains0_ref,
    gains1_ref,
    out_ref,
    parts_ref,
):
    d_qkv = gather_qkv(qkv_ref)
    out_ref[...] = (grad_ref[...].astype(f32) + dot_t(d_qkv, w_ref[0])).astype(bf16)
    pieces = []
    for ref in (gains0_ref, gains1_ref):
        for row in (0, 1):
            pieces += split_two(ref[row : row + 1])
    pieces.append(jnp.zeros((128 - len(pieces), C), f32))
    gains = jnp.concatenate(pieces, 0).T
    at = 0
    for part in (dot_0(tokens_ref[...], d_qkv), grad_qkv1_ref[...], proj0_ref[...], proj1_ref[...], gains):
        width = part.shape[1]
        parts_ref[:, :, at : at + width] = part.astype(bf16).reshape(8, C // 8, width)
        at += width


def first_sum_kernel(parts_ref, out_ref):
    total = jnp.sum(parts_ref[...].astype(f32), 0).reshape(8, 8, SENT)
    right = jnp.concatenate([total[:, :, HALF:], jnp.zeros((8, 8, 2 * HALF - SENT), f32)], 2)
    out_ref[...] = jnp.concatenate([total[:, :, :HALF], right], 1).astype(bf16)


def second_sum_kernel(parts_ref, out_ref):
    out_ref[...] = jnp.sum(parts_ref[...].astype(f32), 0)


def final_kernel(a_ref, b_ref, c_ref, d_ref, qkv_ref, proj_ref, gain_ref, bias_ref):
    total = (a_ref[...] + b_ref[...]) + (c_ref[...] + d_ref[...])
    total = jnp.concatenate([total[:8], total[8:]], 1)
    qkv_ref[0] = total[:, :768]
    qkv_ref[1] = total[:, 768:1536]
    proj_ref[0] = total[:, 1536:1792]
    proj_ref[1] = total[:, 1792:2048]
    gains = total[:, 2048:2176].T
    gain_ref[...] = jnp.concatenate([gains[0:1] + gains[1:2], gains[4:5] + gains[5:6]], 0)
    bias_ref[...] = jnp.concatenate([gains[2:3] + gains[3:4], gains[6:7] + gains[7:8]], 0)


def call(kernel, outs, scalars, arrays, masks=()):
    smem = pl.BlockSpec(memory_space=pltpu.SMEM)
    vmem = pl.BlockSpec(memory_space=pltpu.VMEM)
    specs = [smem] * len(scalars) + [vmem] * len(arrays) + [smem, vmem, vmem][: len(masks)]
    return pl.pallas_call(
        kernel,
        out_shape=[jax.ShapeDtypeStruct(shape, dtype) for shape, dtype in outs],
        in_specs=specs,
        out_specs=[vmem] * len(outs),
        compiler_params=pltpu.CompilerParams(vmem_limit_bytes=24 * 2**20),
    )(*scalars, *arrays, *masks)


def body(image, out_grad, w_qkv, w_proj, norm_gain, norm_bias, logit_scale, row_band, col_band):
    position = lax.axis_index("rows")
    half = GROUP // 2
    rings = range(DEVS // GROUP)
    aligned = [[GROUP * g + i for i in range(GROUP)] for g in rings]
    moved = [[(GROUP * g + half + i) % DEVS for i in range(GROUP)] for g in rings]
    across = [[GROUP * g + i for g in rings] for i in range(GROUP)]
    moved_position = (position + DEVS - half) % DEVS
    head0 = (position % GROUP).reshape(1)
    head1 = (moved_position % GROUP).reshape(1)
    first_row = (moved_position // GROUP * WIN).reshape(1)
    masks = (first_row, row_band.reshape(1, -1), col_band.reshape(1, -1))

    def exchange(array, groups):
        return lax.all_to_all(array, "rows", 0, 0, axis_index_groups=groups, tiled=True)

    tokens0 = image.reshape(TOK, C)
    grad_out = out_grad.reshape(TOK, C)
    wide = ((GROUP, TOK, 128), bf16)
    narrow = ((GROUP, PACK, 128), bf16)
    cells = ((TOK, C), bf16)
    proj = ((C, HH), bf16)
    gains = ((8, C), f32)

    (x0,) = call(first_kernel, [wide], (logit_scale,), (tokens0, w_qkv))
    x0 = exchange(x0, aligned)
    (a0,) = call(functools.partial(attend_kernel, False), [narrow], (), (x0,))
    a0 = exchange(a0, aligned)
    tokens1, x1 = call(
        middle_kernel, [cells, wide], (logit_scale,), (a0, tokens0, w_proj, norm_gain, norm_bias, w_qkv)
    )
    x1 = exchange(x1, moved)
    (a1,) = call(functools.partial(attend_kernel, True), [narrow], (), (x1,), masks)
    a1 = exchange(a1, moved)
    d1, proj1, gains1 = call(turn_kernel, [narrow, proj, gains], (), (a1, grad_out, w_proj, norm_gain))
    d1 = exchange(d1, moved)
    (qkv1,) = call(
        functools.partial(attend_back_kernel, 1, True), [wide], (head1, logit_scale), (x1, d1), masks
    )
    qkv1 = exchange(qkv1, moved)
    d0, grad0, grad_qkv1, proj0, gains0 = call(
        back_kernel,
        [narrow, cells, ((C, 3 * HH), bf16), proj, gains],
        (),
        (qkv1, w_qkv, tokens1, grad_out, a0, w_proj, norm_gain),
    )
    d0 = exchange(d0, aligned)
    (qkv0,) = call(functools.partial(attend_back_kernel, 0, False), [wide], (head0, logit_scale), (x0, d0))
    qkv0 = exchange(qkv0, aligned)
    grad_image, parts = call(
        last_kernel,
        [cells, ((8, C // 8, SENT), bf16)],
        (),
        (qkv0, w_qkv, tokens0, grad0, grad_qkv1, proj0, proj1, gains0, gains1),
    )
    parts = exchange(parts, across)
    (parts,) = call(first_sum_kernel, [((8, 16, HALF), bf16)], (), (parts,))
    parts = exchange(parts, aligned)
    (share,) = call(second_sum_kernel, [((16, HALF), f32)], (), (parts,))
    others = [lax.ppermute(share, "dp", [(i, i ^ k) for i in range(4)]) for k in (1, 2, 3)]
    small = ((2, 8), f32)
    grad_qkv, grad_proj, grad_gain, grad_bias = call(
        final_kernel, [((2, 8, 3 * HH), f32), ((2, 8, HH), f32), small, small], (), (share, *others)
    )
    return (
        grad_image.reshape(image.shape),
        grad_qkv,
        grad_proj.transpose(0, 2, 1),
        grad_gain,
        grad_bias,
    )


def solution(mesh):
    placed = (P("dp", "rows", None, None), P("dp", "rows", None, None)) + (P(),) * 7
    return jax.shard_map(
        body,
        mesh=mesh,
        in_specs=placed,
        out_specs=(
            P("dp", "rows", None, None),
            P(None, "rows", None),
            P(None, None, "rows"),
            P(None, "rows"),
            P(None, "rows"),
        ),
        check_vma=False,
    )
```

```python
import functools

import jax
import jax.numpy as jnp
from jax import lax
from jax.experimental import pallas as pl
from jax.experimental.pallas import tpu as pltpu
from jax.sharding import PartitionSpec as P

C = 512
HEADS = 8
HD = 32
WIN = 24
HH = 256
SHIFT = 12
GROUP = 8
TOK = 144
CELLS = WIN * WIN
ROWS_DEV = 3
PACK = 48
DEVS = 64
VMEM_LIMIT = 24 * 2**20
EARLY = 3 * HH + 2 * HH
TILES = (3 * HH + EARLY // 2 + 128) // 128

norm_eps = 1e-05
mask_value = 100.0
f32 = jnp.float32
bf16 = jnp.bfloat16


def dot(a, b):
    return jnp.dot(a, b, preferred_element_type=f32)


def dot_t(a, b):
    return lax.dot_general(a, b, (((1,), (1,)), ((), ())), preferred_element_type=f32)


def dot_0(a, b):
    return lax.dot_general(a, b, (((0,), (0,)), ((), ())), preferred_element_type=f32)


def iota(shape, axis):
    return lax.broadcasted_iota(jnp.int32, shape, axis)


def head_sums(x):
    width = x.shape[1]
    ones = (iota((width, width), 0) // HD == iota((width, width), 1) // HD).astype(f32).astype(bf16)
    high = x.astype(bf16)
    low = (x - high.astype(f32)).astype(bf16)
    return dot(high, ones) + dot(low, ones)


def split_two(x):
    high = x.astype(bf16).astype(f32)
    return high, x - high


def lane_slice(x, at):
    return x[:, at : at + HD]


def send_projected(tokens, weight, scale_ref, block, out_ref):
    projected = dot(tokens, weight)
    query, key, value = projected[:, :HH], projected[:, HH : 2 * HH], projected[:, 2 * HH :]
    lane = iota((1, HH), 1)
    scale = jnp.zeros((1, HH), f32)
    for h in range(HEADS):
        scale = jnp.where(lane // HD == h, scale_ref[block, h], scale)
    q_factor = lax.rsqrt(1.0 + head_sums(query * query))
    k_factor = lax.rsqrt(1.0 + head_sums(key * key))
    q_hat = query * q_factor * jnp.exp(scale)
    k_hat = key * k_factor
    q_high, q_low = split_two(q_factor)
    k_high, k_low = split_two(k_factor)
    slot = iota(q_hat.shape, 1) % HD
    extra = jnp.where(
        slot == 0,
        q_high,
        jnp.where(slot == 1, q_low, jnp.where(slot == 2, k_high, jnp.where(slot == 3, k_low, 0.0))),
    )
    for h in range(HEADS):
        at = h * HD
        out_ref[h] = jnp.concatenate(
            [lane_slice(q_hat, at), lane_slice(k_hat, at), lane_slice(value, at), lane_slice(extra, at)], 1
        ).astype(bf16)


def unpack_heads(packed_ref):
    packed = [packed_ref[h].astype(f32) for h in range(HEADS)]
    rows = [
        jnp.concatenate([lane_slice(packed[h], r * HD) for h in range(HEADS)], 1)
        for r in range(ROWS_DEV)
    ]
    return jnp.concatenate(rows, 0).astype(bf16)


def pack_heads(array, out_ref):
    zeros = jnp.zeros((PACK, HD), f32)
    for h in range(HEADS):
        out_ref[h] = jnp.concatenate(
            [lane_slice(array[r * PACK : (r + 1) * PACK], h * HD) for r in range(ROWS_DEV)] + [zeros], 1
        ).astype(bf16)


def to_windows(array):
    split = array.reshape(GROUP, ROWS_DEV, 2, WIN, array.shape[-1])
    return [split[:, :, w].reshape(CELLS, array.shape[-1]) for w in range(2)]


def from_windows(pair):
    depth = pair[0].shape[-1]
    parts = [part.reshape(GROUP, ROWS_DEV, 1, WIN, depth) for part in pair]
    return jnp.concatenate(parts, 2).reshape(GROUP, TOK, depth)


def roll_tokens(array, by):
    by = by % TOK
    return jnp.concatenate([array[TOK - by :], array[: TOK - by]], 0)


def normalized(attended, weight):
    outputs = dot(attended, weight)
    centered = outputs - jnp.mean(outputs, -1, keepdims=True)
    inverse = lax.rsqrt(jnp.mean(centered * centered, -1, keepdims=True) + norm_eps)
    return centered * inverse, inverse


def finish_back(attended, weight, gain_row, grad_out):
    y_hat, inverse = normalized(attended, weight)
    grad_gain = jnp.sum(grad_out * y_hat, 0, keepdims=True)
    grad_bias = jnp.sum(grad_out, 0, keepdims=True)
    scaled = grad_out * gain_row
    grad_y = inverse * (
        scaled
        - jnp.mean(scaled, -1, keepdims=True)
        - y_hat * jnp.mean(scaled * y_hat, -1, keepdims=True)
    )
    grad_y = grad_y.astype(bf16)
    gains = jnp.concatenate([grad_gain, grad_bias, jnp.zeros((6, C), f32)], 0)
    return grad_y, dot_t(grad_y, weight), gains


def labels_of(axis, window, first_row, row_ref, col_ref):
    shape = (CELLS, 1) if axis == 0 else (1, CELLS)
    at = iota(shape, axis)
    source = at // (ROWS_DEV * WIN)
    rest = at - source * (ROWS_DEV * WIN)
    local_row = rest // WIN
    column = rest - local_row * WIN + window * WIN
    local_row = local_row + (column >= 36).astype(jnp.int32)
    local_row = jnp.where(local_row >= ROWS_DEV, local_row - ROWS_DEV, local_row)
    row = first_row + source * ROWS_DEV + local_row
    row_label = jnp.zeros(shape, jnp.int32)
    col_label = jnp.zeros(shape, jnp.int32)
    for label in (1, 2):
        row_cut = jnp.sum((row_ref[...] < label).astype(jnp.int32), 1, keepdims=True)
        col_cut = jnp.sum((col_ref[...] < label).astype(jnp.int32), 1, keepdims=True)
        row_label = row_label + (row >= row_cut).astype(jnp.int32)
        col_label = col_label + (column >= col_cut).astype(jnp.int32)
    return 3 * row_label + col_label


def masked(scores, window, mask_refs):
    if mask_refs is None:
        return scores
    first_row = mask_refs[0][0]
    one = labels_of(0, window, first_row, *mask_refs[1:])
    two = labels_of(1, window, first_row, *mask_refs[1:])
    return scores - jnp.where(one == two, 0.0, mask_value)


def attend_kernel(masks, x_ref, *refs):
    mask_refs = refs[:3] if masks else None
    out_ref = refs[-1]
    lane = iota((CELLS, 128), 1)
    per_window = []
    for w, cells in enumerate(to_windows(x_ref[...].astype(f32))):
        query = cells[:, :HD].astype(bf16)
        key = cells[:, HD : 2 * HD].astype(bf16)
        value = jnp.where(lane < HD, pltpu.roll(cells, 64, 1), jnp.where(lane == HD, 1.0, 0.0)).astype(bf16)
        scores = masked(dot_t(query, key), w, mask_refs)
        weights = jnp.exp(scores).astype(bf16)
        summed = dot(weights, value)
        attended = jnp.where(lane < HD, summed * (1.0 / summed[:, HD : HD + 1]), 0.0)
        per_window.append(attended.reshape(GROUP, ROWS_DEV, WIN, 128))
    total = 0.0
    for r in range(ROWS_DEV):
        rows = jnp.concatenate([part[:, r] for part in per_window], 1).reshape(GROUP * PACK, 128)
        total = total + (rows if r == 0 else pltpu.roll(rows, r * HD, 1))
    out_ref[...] = total.astype(bf16).reshape(GROUP, PACK, 128)


def attend_back_kernel(block, masks, head_ref, scale_ref, x_ref, grad_ref, *refs):
    mask_refs = refs[:3] if masks else None
    out_ref = refs[-1]
    lane = iota((CELLS, 128), 1)
    low = iota((HD, CELLS), 0)
    scale_row = jnp.exp(jnp.full((1, 128), scale_ref[block, head_ref[0]], f32))
    packed = grad_ref[...].astype(f32).reshape(GROUP * PACK, 128)
    rolled = [packed if r == 0 else pltpu.roll(packed, 128 - r * HD, 1) for r in range(ROWS_DEV)]
    rolled = [part.reshape(GROUP, 1, 2, WIN, 128) for part in rolled]
    grads = jnp.concatenate(rolled, 1)
    results = []
    for w, cells in enumerate(to_windows(x_ref[...].astype(f32))):
        turned = cells.T
        query_t = turned[:HD].astype(bf16)
        key_t = turned[HD : 2 * HD].astype(bf16)
        value_t = turned[2 * HD : 3 * HD]
        grad_t = grads[:, :, w].reshape(CELLS, 128).T[:HD]
        key = cells[:, HD : 2 * HD].astype(bf16)
        scores = masked(dot(key, query_t), w, mask_refs)
        weights = jnp.exp(scores).astype(bf16)
        summed = dot(jnp.concatenate([value_t, jnp.where(low == 0, 1.0, 0.0)], 0).astype(bf16), weights)
        inverse = 1.0 / summed[HD : HD + 1]
        grad_t = (grad_t * inverse).astype(bf16).astype(f32)
        row_high, row_low = split_two(jnp.sum(grad_t * summed[:HD], 0, keepdims=True) * inverse)
        rows = jnp.where(low == 0, -row_high, jnp.where(low == 1, -row_low, 0.0))
        grad_ext = jnp.concatenate([grad_t, rows], 0).astype(bf16)
        ones = jnp.where(lane < HD + 2, 1.0, 0.0)
        value_ext = jnp.where(lane < HD, pltpu.roll(cells, 64, 1), ones)[:, :64].astype(bf16)
        grad_scores = (weights.astype(f32) * dot(value_ext, grad_ext)).astype(bf16)
        query_at = jnp.where((lane >= HD) & (lane < 2 * HD), pltpu.roll(cells, HD, 1), 0.0).astype(bf16)
        zeros = jnp.zeros((HD, CELLS), f32)
        grad_at = jnp.concatenate([zeros, zeros, grad_t, zeros], 0).T.astype(bf16)
        grad_kv = dot(grad_scores, query_at) + dot(weights, grad_at)
        grad_q = dot(key_t, grad_scores)
        grad_q = jnp.concatenate([grad_q, zeros, zeros, zeros], 0).T
        total = jnp.where(lane < HD, grad_q * scale_row, grad_kv)
        unit = jnp.where(lane < HD, cells / scale_row, jnp.where(lane < 2 * HD, cells, 0.0))
        q_factor = cells[:, 96:97] + cells[:, 97:98]
        k_factor = cells[:, 98:99] + cells[:, 99:100]
        factor = jnp.where(lane < HD, q_factor, jnp.where(lane < 2 * HD, k_factor, 1.0))
        results.append(factor * (total - unit * head_sums(unit * total)))
    out_ref[...] = from_windows(results).astype(bf16)


def first_kernel(scale_ref, tokens_ref, w_ref, out_ref):
    send_projected(tokens_ref[...], w_ref[...], scale_ref, 0, out_ref)


def middle_kernel(scale_ref, packed_ref, gain_ref, bias_ref, tokens_ref, w_proj_ref, w_ref, out_ref, rolled_ref):
    attended = unpack_heads(packed_ref)
    y_hat, _ = normalized(attended, w_proj_ref[...])
    out = (tokens_ref[...].astype(f32) + y_hat * gain_ref[0:1] + bias_ref[0:1]).astype(bf16).astype(f32)
    rolled = roll_tokens(out, -SHIFT).astype(bf16)
    rolled_ref[...] = rolled
    send_projected(rolled, w_ref[...], scale_ref, 1, out_ref)


def turn_kernel(packed_ref, gain_ref, grad_ref, w_proj_ref, out_ref, grad_proj_ref, gains_ref):
    attended = unpack_heads(packed_ref)
    grad = roll_tokens(grad_ref[...].astype(f32), -SHIFT)
    grad_y, grad_att, gains = finish_back(attended, w_proj_ref[...], gain_ref[1:2], grad)
    pack_heads(grad_att, out_ref)
    grad_proj_ref[...] = dot_0(grad_y, attended).astype(bf16)
    gains_ref[...] = gains


def gather_qkv(qkv_ref):
    parts = [qkv_ref[h].astype(f32) for h in range(HEADS)]
    return jnp.concatenate(
        [lane_slice(parts[h], kind * HD) for kind in range(3) for h in range(HEADS)], 1
    ).astype(bf16)


def give(array, side, kept_ref, given_ref):
    half = array.shape[1] // 2
    left, right = array[:, :half], array[:, half:]
    kept_ref[...] = jnp.where(side == 0, left, right).astype(bf16)
    given_ref[...] = jnp.where(side == 0, right, left).astype(bf16)


def back_kernel(
    core_ref,
    qkv_ref,
    packed_ref,
    gain_ref,
    w_ref,
    w_proj_ref,
    grad_ref,
    proj1_ref,
    tokens_ref,
    out_ref,
    gains_ref,
    grad0_ref,
    kept_ref,
    given_ref,
):
    d_qkv = gather_qkv(qkv_ref)
    from_qkv = roll_tokens(dot_t(d_qkv, w_ref[...]), SHIFT)
    grad = (grad_ref[...].astype(f32) + from_qkv).astype(bf16)
    grad0_ref[...] = grad
    attended = unpack_heads(packed_ref)
    grad_y, grad_att, gains = finish_back(attended, w_proj_ref[...], gain_ref[0:1], grad.astype(f32))
    pack_heads(grad_att, out_ref)
    parts = [dot_0(tokens_ref[...], d_qkv), proj1_ref[...].astype(f32), dot_0(grad_y, attended)]
    early = jnp.concatenate(parts, 1)
    give(early, core_ref[0], kept_ref, given_ref)
    gains_ref[...] = gains


def last_kernel(
    qkv_ref, w_ref, tokens_ref, got_ref, gains0_ref, gains1_ref, grad_ref, kept_ref, parts_ref, out_ref
):
    d_qkv = gather_qkv(qkv_ref)
    out_ref[...] = (grad_ref[...].astype(f32) + dot_t(d_qkv, w_ref[...])).astype(bf16)
    pieces = []
    for ref in (gains0_ref, gains1_ref):
        for row in (0, 1):
            pieces += split_two(ref[row : row + 1])
    pieces.append(jnp.zeros((128 - len(pieces), C), f32))
    gains = jnp.concatenate(pieces, 0).T
    early = kept_ref[...].astype(f32) + got_ref[...].astype(f32)
    tile = 0
    for part in (dot_0(tokens_ref[...], d_qkv), early, gains):
        for at in range(0, part.shape[1], 128):
            block = part[:, at : at + 128].astype(bf16).reshape(8, C // 8, 128)
            parts_ref[:, tile * (C // 8) : (tile + 1) * (C // 8), :] = block
            tile += 1


def first_sum_kernel(parts_ref, out_ref):
    total = jnp.sum(parts_ref[...].astype(f32), 0).reshape(TILES, 8, 8, 128)
    for ring in range(8):
        out_ref[ring] = total[:, ring].reshape(TILES * 8, 128).astype(bf16)


def second_sum_kernel(parts_ref, out_ref):
    out_ref[...] = jnp.sum(parts_ref[...].astype(f32), 0)


def final_kernel(core_ref, own_ref, core1_ref, chip_ref, chip1_ref, qkv_ref, proj_ref, gain_ref, bias_ref):
    same = own_ref[...] + chip_ref[...]
    other = core1_ref[...] + chip1_ref[...]
    both = (same + other).reshape(TILES, 8, 128)
    first = core_ref[0] == 0
    left = jnp.where(first, same, other).reshape(TILES, 8, 128)
    right = jnp.where(first, other, same).reshape(TILES, 8, 128)
    tiles = [left[i] for i in range(6, 11)] + [right[i] for i in range(6, 11)]
    qkv_ref[0] = jnp.concatenate([both[i] for i in range(6)], 1)
    qkv_ref[1] = jnp.concatenate(tiles[:6], 1)
    proj_ref[1] = jnp.concatenate(tiles[6:8], 1)
    proj_ref[0] = jnp.concatenate(tiles[8:], 1)
    gains = both[11].T
    gain_ref[...] = jnp.concatenate([gains[0:1] + gains[1:2], gains[4:5] + gains[5:6]], 0)
    bias_ref[...] = jnp.concatenate([gains[2:3] + gains[3:4], gains[6:7] + gains[7:8]], 0)


class Fetched:
    def __init__(self, source, ref, sem):
        self.ref, self.copy = ref, pltpu.make_async_copy(source, ref, sem)
        self.copy.start()
        self.waited = False

    def __getitem__(self, at):
        if not self.waited:
            self.copy.wait()
            self.waited = True
        return self.ref[at]


class Stored:
    def __init__(self, ref, target, sem):
        self.ref, self.copy = ref, pltpu.make_async_copy(ref, target, sem)

    def __setitem__(self, at, value):
        self.ref[at] = value
        self.copy.start()


def call(kernel, outs, scalars, arrays, masks=(), fetched=(), stored=()):
    arrays = [item if isinstance(item, tuple) else (item, None) for item in arrays]
    fetched = [item if isinstance(item, tuple) else (item, None) for item in fetched]
    counts = [len(scalars), len(arrays), len(fetched), len(masks), len(outs), len(stored), len(fetched), len(stored)]

    def wrapped(*refs):
        parts, at = [], 0
        for count in counts:
            parts.append(refs[at : at + count])
            at += count
        scalar_refs, array_refs, sources, mask_refs, out_refs, targets, filled, sent = parts
        sems = refs[-1]
        near = [ref if block is None else ref.at[block] for ref, (_, block) in zip(array_refs, arrays)]
        far = []
        for i, (_, block) in enumerate(fetched):
            source = sources[i] if block is None else sources[i].at[block]
            far.append(Fetched(source, filled[i], sems.at[i]))
        results = [Stored(sent[i], targets[i], sems.at[len(fetched) + i]) for i in range(len(stored))]
        kernel(*scalar_refs, *near, *far, *mask_refs, *out_refs, *results)
        for result in results:
            result.copy.wait()

    smem = pl.BlockSpec(memory_space=pltpu.SMEM)
    vmem = pl.BlockSpec(memory_space=pltpu.VMEM)
    hbm = pl.BlockSpec(memory_space=pltpu.HBM)
    scratch = [
        pltpu.VMEM(array.shape if block is None else array.shape[1:], array.dtype) for array, block in fetched
    ]
    scratch += [pltpu.VMEM(*out) for out in stored]
    if scratch:
        scratch.append(pltpu.SemaphoreType.DMA((len(scratch),)))
    return pl.pallas_call(
        wrapped,
        out_shape=[jax.ShapeDtypeStruct(*out) for out in outs] + [pltpu.HBM(*out) for out in stored],
        in_specs=[smem] * len(scalars)
        + [vmem] * len(arrays)
        + [hbm] * len(fetched)
        + [smem, vmem, vmem][: len(masks)],
        out_specs=[vmem] * len(outs) + [hbm] * len(stored),
        scratch_shapes=scratch,
        compiler_params=pltpu.CompilerParams(vmem_limit_bytes=VMEM_LIMIT),
    )(
        *scalars,
        *(array for array, _ in arrays),
        *(pltpu.with_memory_space_constraint(array, pltpu.HBM) for array, _ in fetched),
        *masks,
    )


def body(image, out_grad, w_qkv, w_proj, norm_gain, norm_bias, logit_scale, row_band, col_band):
    position = lax.axis_index("rows")
    half = GROUP // 2
    rings = range(DEVS // GROUP)
    aligned = [[GROUP * g + i for i in range(GROUP)] for g in rings]
    across = [[GROUP * g + i for g in rings] for i in range(GROUP)]
    moved = [[(GROUP * g + half + i) % DEVS for i in range(GROUP)] for g in rings]
    moved_position = (position + DEVS - half) % DEVS
    head0 = (position % GROUP).reshape(1)
    head1 = (moved_position % GROUP).reshape(1)
    first_row = (moved_position // GROUP * WIN).reshape(1)
    core = (lax.axis_index("dp") % 2).reshape(1)
    image, head0, head1, first_row, core = lax.optimization_barrier((image, head0, head1, first_row, core))
    masks = (first_row, row_band.reshape(1, -1), col_band.reshape(1, -1))

    def exchange(array, groups):
        return lax.all_to_all(array, "rows", 0, 0, axis_index_groups=groups, tiled=True)

    tokens0 = image.reshape(TOK, C)
    grad_out = out_grad.reshape(TOK, C)
    wide = ((GROUP, TOK, 128), bf16)
    narrow = ((GROUP, PACK, 128), bf16)
    cells = ((TOK, C), bf16)
    proj = ((C, HH), bf16)
    gains = ((8, C), f32)
    half_early = ((C, EARLY // 2), bf16)

    def swap(array, apart):
        return lax.ppermute(array, "dp", [(i, i ^ apart) for i in range(4)])

    (x0,) = call(first_kernel, [wide], (logit_scale,), (), fetched=(tokens0, (w_qkv, 0)))
    x0 = exchange(x0, aligned)
    (a0,) = call(functools.partial(attend_kernel, False), [narrow], (), (x0,))
    a0 = exchange(a0, aligned)
    x1, tokens1 = call(
        middle_kernel,
        [wide],
        (logit_scale,),
        (a0, norm_gain, norm_bias, tokens0, (w_proj, 0), (w_qkv, 1)),
        stored=[cells],
    )
    x1 = exchange(x1, moved)
    (a1,) = call(functools.partial(attend_kernel, True), [narrow], (), (x1,), masks)
    a1 = exchange(a1, moved)
    d1, proj1, gains1 = call(
        turn_kernel, [narrow, proj, gains], (), (a1, norm_gain, grad_out, (w_proj, 1))
    )
    d1 = exchange(d1, moved)
    (qkv1,) = call(
        functools.partial(attend_back_kernel, 1, True), [wide], (head1, logit_scale), (x1, d1), masks
    )
    qkv1 = exchange(qkv1, moved)
    d0, gains0, grad0, kept, given = call(
        back_kernel,
        [narrow, gains],
        (core,),
        (qkv1, a0, norm_gain, (w_qkv, 1), (w_proj, 0), grad_out, proj1),
        fetched=(tokens1,),
        stored=[cells, half_early, half_early],
    )
    d0, got = lax.optimization_barrier((d0, swap(given, 1)))
    d0 = exchange(d0, aligned)
    (qkv0,) = call(functools.partial(attend_back_kernel, 0, False), [wide], (head0, logit_scale), (x0, d0))
    qkv0 = exchange(qkv0, aligned)
    parts, grad_image = call(
        last_kernel,
        [((8, TILES * C // 8, 128), bf16), cells],
        (),
        (qkv0, (w_qkv, 0), tokens0, got, gains0, gains1),
        fetched=(grad0, kept),
    )
    parts = exchange(parts, across)
    (parts,) = call(first_sum_kernel, [((8, TILES * 8, 128), bf16)], (), (parts,))
    parts = exchange(parts, aligned)
    (share,) = call(second_sum_kernel, [((TILES * 8, 128), f32)], (), (parts,))
    small = ((2, 8), f32)
    grad_qkv, grad_proj, grad_gain, grad_bias = call(
        final_kernel,
        [((2, 8, 3 * HH), f32), ((2, 8, HH), f32), small, small],
        (core,),
        (share, swap(share, 1), swap(share, 2), swap(share, 3)),
    )
    return (
        grad_image.reshape(image.shape),
        grad_qkv,
        grad_proj.transpose(0, 2, 1),
        grad_gain,
        grad_bias,
    )


def solution(mesh):
    placed = (P("dp", "rows", None, None), P("dp", "rows", None, None)) + (P(),) * 7
    return jax.shard_map(
        body,
        mesh=mesh,
        in_specs=placed,
        out_specs=(
            P("dp", "rows", None, None),
            P(None, "rows", None),
            P(None, None, "rows"),
            P(None, "rows"),
            P(None, "rows"),
        ),
        check_vma=False,
    )
```

```python
import functools

import jax
import jax.numpy as jnp
from jax import lax
from jax.experimental import pallas as pl
from jax.experimental.pallas import tpu as pltpu
from jax.sharding import PartitionSpec as P

C = 512
HEADS = 8
HD = 32
WIN = 24
HH = 256
SHIFT = 12
GROUP = 8
TOK = 144
CELLS = WIN * WIN
ROWS_DEV = 3
PACK = 48
DEVS = 64
VMEM_LIMIT = 24 * 2**20
EARLY = 3 * HH + 2 * HH
SHORT = 112
TILES = (3 * HH + EARLY // 2 + 128) // 128

norm_eps = 1e-05
mask_value = 100.0
f32 = jnp.float32
bf16 = jnp.bfloat16


def dot(a, b):
    return jnp.dot(a, b, preferred_element_type=f32)


def dot_t(a, b):
    return lax.dot_general(a, b, (((1,), (1,)), ((), ())), preferred_element_type=f32)


def dot_0(a, b):
    return lax.dot_general(a, b, (((0,), (0,)), ((), ())), preferred_element_type=f32)


def iota(shape, axis):
    return lax.broadcasted_iota(jnp.int32, shape, axis)


def head_sums(x):
    width = x.shape[1]
    ones = (iota((width, width), 0) // HD == iota((width, width), 1) // HD).astype(f32).astype(bf16)
    high = x.astype(bf16)
    low = (x - high.astype(f32)).astype(bf16)
    return dot(high, ones) + dot(low, ones)


def split_two(x):
    high = x.astype(bf16).astype(f32)
    return high, x - high


def lane_slice(x, at):
    return x[:, at : at + HD]


def send_projected(tokens, weight, scale_ref, block, out_ref):
    projected = dot(tokens, weight)
    query, key, value = projected[:, :HH], projected[:, HH : 2 * HH], projected[:, 2 * HH :]
    lane = iota((1, HH), 1)
    scale = jnp.zeros((1, HH), f32)
    scales = scale_ref[...][block : block + 1]
    for h in range(HEADS):
        scale = jnp.where(lane // HD == h, scales[:, h : h + 1], scale)
    q_factor = lax.rsqrt(1.0 + head_sums(query * query))
    k_factor = lax.rsqrt(1.0 + head_sums(key * key))
    q_hat = query * q_factor * jnp.exp(scale)
    k_hat = key * k_factor
    q_high, q_low = split_two(q_factor)
    k_high, k_low = split_two(k_factor)
    slot = iota(q_hat.shape, 1) % HD
    extra = jnp.where(
        slot == 0,
        q_high,
        jnp.where(slot == 1, q_low, jnp.where(slot == 2, k_high, jnp.where(slot == 3, k_low, 0.0))),
    )
    for h in range(HEADS):
        at = h * HD
        out_ref[h] = jnp.concatenate(
            [lane_slice(q_hat, at), lane_slice(k_hat, at), lane_slice(value, at), lane_slice(extra, at)], 1
        ).astype(bf16)


def unpack_heads(packed_ref):
    packed = [packed_ref[h].astype(f32) for h in range(HEADS)]
    rows = [
        jnp.concatenate([lane_slice(packed[h], r * HD) for h in range(HEADS)], 1)
        for r in range(ROWS_DEV)
    ]
    return jnp.concatenate(rows, 0).astype(bf16)


def pack_heads(array, out_ref):
    zeros = jnp.zeros((PACK, HD), f32)
    for h in range(HEADS):
        out_ref[h] = jnp.concatenate(
            [lane_slice(array[r * PACK : (r + 1) * PACK], h * HD) for r in range(ROWS_DEV)] + [zeros], 1
        ).astype(bf16)


def to_windows(array):
    split = array.reshape(GROUP, ROWS_DEV, 2, WIN, array.shape[-1])
    return [split[:, :, w].reshape(CELLS, array.shape[-1]) for w in range(2)]


def from_windows(pair):
    depth = pair[0].shape[-1]
    parts = [part.reshape(GROUP, ROWS_DEV, 1, WIN, depth) for part in pair]
    return jnp.concatenate(parts, 2).reshape(GROUP, TOK, depth)


def pack_cells(cells):
    tail = cells[:, SHORT:].reshape(GROUP * 32, 128)
    moved = [pltpu.roll(tail, 96 - 32 * kind, 1).reshape(GROUP, 32, 128) for kind in range(3)]
    moved = jnp.concatenate(moved + [jnp.zeros((GROUP, SHORT - 96, 128), f32)], 1)
    lane = iota(moved.shape, 2)
    return jnp.where(lane < 96, cells[:, :SHORT], moved)


def roll_tokens(array, by):
    by = by % TOK
    return jnp.concatenate([array[TOK - by :], array[: TOK - by]], 0)


def normalized(attended, weight):
    outputs = dot(attended, weight)
    centered = outputs - jnp.mean(outputs, -1, keepdims=True)
    inverse = lax.rsqrt(jnp.mean(centered * centered, -1, keepdims=True) + norm_eps)
    return centered * inverse, inverse


def finish_back(attended, weight, gain_row, grad_out):
    y_hat, inverse = normalized(attended, weight)
    grad_gain = jnp.sum(grad_out * y_hat, 0, keepdims=True)
    grad_bias = jnp.sum(grad_out, 0, keepdims=True)
    scaled = grad_out * gain_row
    grad_y = inverse * (
        scaled
        - jnp.mean(scaled, -1, keepdims=True)
        - y_hat * jnp.mean(scaled * y_hat, -1, keepdims=True)
    )
    grad_y = grad_y.astype(bf16)
    gains = jnp.concatenate([grad_gain, grad_bias, jnp.zeros((6, C), f32)], 0)
    return grad_y, dot_t(grad_y, weight), gains


def labels_of(axis, window, first_row, row_ref, col_ref):
    shape = (CELLS, 1) if axis == 0 else (1, CELLS)
    at = iota(shape, axis)
    source = at // (ROWS_DEV * WIN)
    rest = at - source * (ROWS_DEV * WIN)
    local_row = rest // WIN
    column = rest - local_row * WIN + window * WIN
    local_row = local_row + (column >= 36).astype(jnp.int32)
    local_row = jnp.where(local_row >= ROWS_DEV, local_row - ROWS_DEV, local_row)
    row = first_row + source * ROWS_DEV + local_row
    row_label = jnp.zeros(shape, jnp.int32)
    col_label = jnp.zeros(shape, jnp.int32)
    for label in (1, 2):
        row_cut = jnp.sum((row_ref[...] < label).astype(jnp.int32), 1, keepdims=True)
        col_cut = jnp.sum((col_ref[...] < label).astype(jnp.int32), 1, keepdims=True)
        row_label = row_label + (row >= row_cut).astype(jnp.int32)
        col_label = col_label + (column >= col_cut).astype(jnp.int32)
    return 3 * row_label + col_label


def masked(scores, window, mask_refs):
    if mask_refs is None:
        return scores
    first_row = mask_refs[0][0]
    one = labels_of(0, window, first_row, *mask_refs[1:])
    two = labels_of(1, window, first_row, *mask_refs[1:])
    return scores - jnp.where(one == two, 0.0, mask_value)


def attend_kernel(masks, x_ref, *refs):
    mask_refs = refs[:3] if masks else None
    out_ref = refs[-1]
    lane = iota((CELLS, 128), 1)
    per_window = []
    for w, cells in enumerate(to_windows(x_ref[...].astype(f32))):
        query = cells[:, :HD].astype(bf16)
        key = cells[:, HD : 2 * HD].astype(bf16)
        value = jnp.where(lane < HD, pltpu.roll(cells, 64, 1), jnp.where(lane == HD, 1.0, 0.0)).astype(bf16)
        scores = masked(dot_t(query, key), w, mask_refs)
        weights = jnp.exp(scores).astype(bf16)
        summed = dot(weights, value)
        attended = jnp.where(lane < HD, summed * (1.0 / summed[:, HD : HD + 1]), 0.0)
        per_window.append(attended.reshape(GROUP, ROWS_DEV, WIN, 128))
    total = 0.0
    for r in range(ROWS_DEV):
        rows = jnp.concatenate([part[:, r] for part in per_window], 1).reshape(GROUP * PACK, 128)
        total = total + (rows if r == 0 else pltpu.roll(rows, r * HD, 1))
    out_ref[...] = total.astype(bf16).reshape(GROUP, PACK, 128)


def attend_back_kernel(block, masks, head_ref, scale_ref, x_ref, grad_ref, *refs):
    mask_refs = refs[:3] if masks else None
    out_ref = refs[-1]
    lane = iota((CELLS, 128), 1)
    low = iota((HD, CELLS), 0)
    scale_row = jnp.exp(jnp.full((1, 128), scale_ref[block, head_ref[0]], f32))
    packed = grad_ref[...].astype(f32).reshape(GROUP * PACK, 128)
    rolled = [packed if r == 0 else pltpu.roll(packed, 128 - r * HD, 1) for r in range(ROWS_DEV)]
    rolled = [part.reshape(GROUP, 1, 2, WIN, 128) for part in rolled]
    grads = jnp.concatenate(rolled, 1)
    results = []
    for w, cells in enumerate(to_windows(x_ref[...].astype(f32))):
        turned = cells.T
        query_t = turned[:HD].astype(bf16)
        key_t = turned[HD : 2 * HD].astype(bf16)
        value_t = turned[2 * HD : 3 * HD]
        grad_t = grads[:, :, w].reshape(CELLS, 128).T[:HD]
        key = cells[:, HD : 2 * HD].astype(bf16)
        scores = masked(dot(key, query_t), w, mask_refs)
        weights = jnp.exp(scores).astype(bf16)
        summed = dot(jnp.concatenate([value_t, jnp.where(low == 0, 1.0, 0.0)], 0).astype(bf16), weights)
        inverse = 1.0 / summed[HD : HD + 1]
        grad_t = (grad_t * inverse).astype(bf16).astype(f32)
        row_high, row_low = split_two(jnp.sum(grad_t * summed[:HD], 0, keepdims=True) * inverse)
        rows = jnp.where(low == 0, -row_high, jnp.where(low == 1, -row_low, 0.0))
        grad_ext = jnp.concatenate([grad_t, rows], 0).astype(bf16)
        ones = jnp.where(lane < HD + 2, 1.0, 0.0)
        value_ext = jnp.where(lane < HD, pltpu.roll(cells, 64, 1), ones)[:, :64].astype(bf16)
        grad_scores = (weights.astype(f32) * dot(value_ext, grad_ext)).astype(bf16)
        query_at = jnp.where((lane >= HD) & (lane < 2 * HD), pltpu.roll(cells, HD, 1), 0.0).astype(bf16)
        zeros = jnp.zeros((HD, CELLS), f32)
        grad_at = jnp.concatenate([zeros, zeros, grad_t, zeros], 0).T.astype(bf16)
        grad_kv = dot(grad_scores, query_at) + dot(weights, grad_at)
        grad_q = dot(key_t, grad_scores)
        grad_q = jnp.concatenate([grad_q, zeros, zeros, zeros], 0).T
        total = jnp.where(lane < HD, grad_q * scale_row, grad_kv)
        unit = jnp.where(lane < HD, cells / scale_row, jnp.where(lane < 2 * HD, cells, 0.0))
        q_factor = cells[:, 96:97] + cells[:, 97:98]
        k_factor = cells[:, 98:99] + cells[:, 99:100]
        factor = jnp.where(lane < HD, q_factor, jnp.where(lane < 2 * HD, k_factor, 1.0))
        results.append(factor * (total - unit * head_sums(unit * total)))
    out_ref[...] = pack_cells(from_windows(results)).astype(bf16)


def first_kernel(tokens_ref, w_ref, scale_ref, out_ref):
    send_projected(tokens_ref[...], w_ref[...], scale_ref, 0, out_ref)


def middle_kernel(packed_ref, scale_ref, gain_ref, bias_ref, tokens_ref, w_proj_ref, w_ref, out_ref, rolled_ref):
    attended = unpack_heads(packed_ref)
    y_hat, _ = normalized(attended, w_proj_ref[...])
    out = (tokens_ref[...].astype(f32) + y_hat * gain_ref[0:1] + bias_ref[0:1]).astype(bf16).astype(f32)
    rolled = roll_tokens(out, -SHIFT).astype(bf16)
    rolled_ref[...] = rolled
    send_projected(rolled, w_ref[...], scale_ref, 1, out_ref)


def turn_kernel(packed_ref, gain_ref, grad_ref, w_proj_ref, out_ref, grad_proj_ref, gains_ref):
    attended = unpack_heads(packed_ref)
    grad = roll_tokens(grad_ref[...].astype(f32), -SHIFT)
    grad_y, grad_att, gains = finish_back(attended, w_proj_ref[...], gain_ref[1:2], grad)
    pack_heads(grad_att, out_ref)
    grad_proj_ref[...] = dot_0(grad_y, attended).astype(bf16)
    gains_ref[...] = gains


def gather_qkv(qkv_ref):
    parts = [qkv_ref[h].astype(f32) for h in range(HEADS)]
    top = [lane_slice(parts[h][:SHORT], kind * HD) for kind in range(3) for h in range(HEADS)]
    tail = [lane_slice(parts[h][kind * 32 : kind * 32 + 32], 96) for kind in range(3) for h in range(HEADS)]
    return jnp.concatenate([jnp.concatenate(top, 1), jnp.concatenate(tail, 1)], 0).astype(bf16)


def give(array, side, kept_ref, given_ref):
    half = array.shape[1] // 2
    left, right = array[:, :half], array[:, half:]
    kept_ref[...] = jnp.where(side == 0, left, right).astype(bf16)
    given_ref[...] = jnp.where(side == 0, right, left).astype(bf16)


def back_kernel(
    core_ref,
    qkv_ref,
    packed_ref,
    gain_ref,
    w_ref,
    w_proj_ref,
    grad_ref,
    proj1_ref,
    tokens_ref,
    out_ref,
    gains_ref,
    grad0_ref,
    kept_ref,
    given_ref,
):
    d_qkv = gather_qkv(qkv_ref)
    from_qkv = roll_tokens(dot_t(d_qkv, w_ref[...]), SHIFT)
    grad = (grad_ref[...].astype(f32) + from_qkv).astype(bf16)
    grad0_ref[...] = grad
    attended = unpack_heads(packed_ref)
    grad_y, grad_att, gains = finish_back(attended, w_proj_ref[...], gain_ref[0:1], grad.astype(f32))
    pack_heads(grad_att, out_ref)
    parts = [dot_0(tokens_ref[...], d_qkv), proj1_ref[...].astype(f32), dot_0(grad_y, attended)]
    early = jnp.concatenate(parts, 1)
    give(early, core_ref[0], kept_ref, given_ref)
    gains_ref[...] = gains


def image_kernel(qkv_ref, w_ref, grad_ref, out_ref):
    out_ref[...] = (grad_ref[...].astype(f32) + dot_t(gather_qkv(qkv_ref), w_ref[...])).astype(bf16)


def last_kernel(qkv_ref, tokens_ref, got_ref, gains0_ref, gains1_ref, kept_ref, parts_ref):
    d_qkv = gather_qkv(qkv_ref)
    pieces = []
    for ref in (gains0_ref, gains1_ref):
        for row in (0, 1):
            pieces += split_two(ref[row : row + 1])
    pieces.append(jnp.zeros((128 - len(pieces), C), f32))
    gains = jnp.concatenate(pieces, 0).T
    early = kept_ref[...].astype(f32) + got_ref[...].astype(f32)
    tile = 0
    for part in (dot_0(tokens_ref[...], d_qkv), early, gains):
        for at in range(0, part.shape[1], 128):
            block = part[:, at : at + 128].astype(bf16).reshape(8, C // 8, 128)
            parts_ref[:, tile * (C // 8) : (tile + 1) * (C // 8), :] = block
            tile += 1


def first_sum_kernel(parts_ref, out_ref):
    total = jnp.sum(parts_ref[...].astype(f32), 0).reshape(TILES, 8, 8, 128)
    for ring in range(8):
        out_ref[ring] = total[:, ring].reshape(TILES * 8, 128).astype(bf16)


def second_sum_kernel(parts_ref, out_ref):
    out_ref[...] = jnp.sum(parts_ref[...].astype(f32), 0)


def add_kernel(one_ref, two_ref, out_ref):
    out_ref[...] = one_ref[...] + two_ref[...]


def final_kernel(core_ref, own_ref, other_ref, qkv_ref, proj_ref, gain_ref, bias_ref):
    own = own_ref[...].reshape(TILES, 8, 128)
    other = other_ref[...].reshape(TILES, 8, 128)
    both = own + other
    first = core_ref[0] == 0
    left, right = jnp.where(first, own, other), jnp.where(first, other, own)
    tiles = [left[i] for i in range(6, 11)] + [right[i] for i in range(6, 11)]
    qkv_ref[0] = jnp.concatenate([both[i] for i in range(6)], 1)
    qkv_ref[1] = jnp.concatenate(tiles[:6], 1)
    proj_ref[1] = jnp.concatenate(tiles[6:8], 1)
    proj_ref[0] = jnp.concatenate(tiles[8:], 1)
    gains = both[11].T
    gain_ref[...] = jnp.concatenate([gains[0:1] + gains[1:2], gains[4:5] + gains[5:6]], 0)
    bias_ref[...] = jnp.concatenate([gains[2:3] + gains[3:4], gains[6:7] + gains[7:8]], 0)


def pieces_of(shape):
    return 4 if shape[0] % 64 == 0 and shape[0] * shape[1] >= 2**18 else 1


def copies_of(source, target, sems, first):
    count = pieces_of(target.shape)
    rows = target.shape[0] // count
    if count == 1:
        return [pltpu.make_async_copy(source, target, sems.at[first])]
    return [
        pltpu.make_async_copy(
            source.at[pl.ds(i * rows, rows)], target.at[pl.ds(i * rows, rows)], sems.at[first + i]
        )
        for i in range(count)
    ]


class Fetched:
    def __init__(self, source, ref, sems, first):
        self.ref, self.copies = ref, copies_of(source, ref, sems, first)
        for copy in self.copies:
            copy.start()
        self.waited = False

    def __getitem__(self, at):
        if not self.waited:
            for copy in self.copies:
                copy.wait()
            self.waited = True
        return self.ref[at]


class Stored:
    def __init__(self, ref, target, sems, first):
        self.ref, self.copies = ref, copies_of(ref, target, sems, first)

    def __setitem__(self, at, value):
        self.ref[at] = value
        for copy in self.copies:
            copy.start()


def call(kernel, outs, scalars, arrays, masks=(), fetched=(), stored=()):
    arrays = [item if isinstance(item, tuple) else (item, None) for item in arrays]
    fetched = [item if isinstance(item, tuple) else (item, None) for item in fetched]
    counts = [len(scalars), len(arrays), len(fetched), len(masks), len(outs), len(stored), len(fetched), len(stored)]

    def wrapped(*refs):
        parts, at = [], 0
        for count in counts:
            parts.append(refs[at : at + count])
            at += count
        scalar_refs, array_refs, sources, mask_refs, out_refs, targets, filled, sent = parts
        sems = refs[-1]
        near = [ref if block is None else ref.at[block] for ref, (_, block) in zip(array_refs, arrays)]
        far, results, first = [], [], 0
        for i, (_, block) in enumerate(fetched):
            source = sources[i] if block is None else sources[i].at[block]
            far.append(Fetched(source, filled[i], sems, first))
            first += pieces_of(filled[i].shape)
        for i in range(len(stored)):
            results.append(Stored(sent[i], targets[i], sems, first))
            first += pieces_of(sent[i].shape)
        kernel(*scalar_refs, *near, *far, *mask_refs, *out_refs, *results)
        for result in results:
            for copy in result.copies:
                copy.wait()

    smem = pl.BlockSpec(memory_space=pltpu.SMEM)
    vmem = pl.BlockSpec(memory_space=pltpu.VMEM)
    hbm = pl.BlockSpec(memory_space=pltpu.HBM)
    scratch = [
        pltpu.VMEM(array.shape if block is None else array.shape[1:], array.dtype) for array, block in fetched
    ]
    scratch += [pltpu.VMEM(*out) for out in stored]
    if scratch:
        scratch.append(pltpu.SemaphoreType.DMA((sum(pieces_of(buffer.shape) for buffer in scratch),)))
    return pl.pallas_call(
        wrapped,
        out_shape=[jax.ShapeDtypeStruct(*out) for out in outs] + [pltpu.HBM(*out) for out in stored],
        in_specs=[smem] * len(scalars)
        + [vmem] * len(arrays)
        + [hbm] * len(fetched)
        + [smem, vmem, vmem][: len(masks)],
        out_specs=[vmem] * len(outs) + [hbm] * len(stored),
        scratch_shapes=scratch,
        compiler_params=pltpu.CompilerParams(vmem_limit_bytes=VMEM_LIMIT),
    )(
        *scalars,
        *(array for array, _ in arrays),
        *(pltpu.with_memory_space_constraint(array, pltpu.HBM) for array, _ in fetched),
        *masks,
    )


def body(image, out_grad, w_qkv, w_proj, norm_gain, norm_bias, logit_scale, row_band, col_band):
    position = lax.axis_index("rows")
    half = GROUP // 2
    rings = range(DEVS // GROUP)
    aligned = [[GROUP * g + i for i in range(GROUP)] for g in rings]
    across = [[GROUP * g + i for g in rings] for i in range(GROUP)]
    moved = [[(GROUP * g + half + i) % DEVS for i in range(GROUP)] for g in rings]
    moved_position = (position + DEVS - half) % DEVS
    head0 = (position % GROUP).reshape(1)
    head1 = (moved_position % GROUP).reshape(1)
    first_row = (moved_position // GROUP * WIN).reshape(1)
    core = (lax.axis_index("dp") % 2).reshape(1)
    image, head0, head1, first_row, core = lax.optimization_barrier((image, head0, head1, first_row, core))
    masks = (first_row, row_band.reshape(1, -1), col_band.reshape(1, -1))

    def exchange(array, groups):
        return lax.all_to_all(array, "rows", 0, 0, axis_index_groups=groups, tiled=True)

    tokens0 = image.reshape(TOK, C)
    grad_out = out_grad.reshape(TOK, C)
    wide = ((GROUP, TOK, 128), bf16)
    short = ((GROUP, SHORT, 128), bf16)
    narrow = ((GROUP, PACK, 128), bf16)
    cells = ((TOK, C), bf16)
    proj = ((C, HH), bf16)
    gains = ((8, C), f32)
    half_early = ((C, EARLY // 2), bf16)

    def swap(array, apart):
        return lax.ppermute(array, "dp", [(i, i ^ apart) for i in range(4)])

    (x0,) = call(first_kernel, [wide], (), (), fetched=(tokens0, (w_qkv, 0), logit_scale))
    x0 = exchange(x0, aligned)
    (a0,) = call(functools.partial(attend_kernel, False), [narrow], (), (x0,))
    a0 = exchange(a0, aligned)
    x1, tokens1 = call(
        middle_kernel,
        [wide],
        (),
        (a0, logit_scale, norm_gain, norm_bias, tokens0, (w_proj, 0), (w_qkv, 1)),
        stored=[cells],
    )
    x1 = exchange(x1, moved)
    (a1,) = call(functools.partial(attend_kernel, True), [narrow], (), (x1,), masks)
    a1 = exchange(a1, moved)
    d1, proj1, gains1 = call(
        turn_kernel, [narrow, proj, gains], (), (a1, norm_gain, grad_out, (w_proj, 1))
    )
    d1 = exchange(d1, moved)
    (qkv1,) = call(
        functools.partial(attend_back_kernel, 1, True), [short], (head1, logit_scale), (x1, d1), masks
    )
    qkv1 = exchange(qkv1, moved)
    d0, gains0, grad0, kept, given = call(
        back_kernel,
        [narrow, gains],
        (core,),
        (qkv1, a0, norm_gain, (w_qkv, 1), (w_proj, 0), grad_out, proj1),
        fetched=(tokens1,),
        stored=[cells, half_early, half_early],
    )
    d0, got = lax.optimization_barrier((d0, swap(given, 1)))
    d0 = exchange(d0, aligned)
    (qkv0,) = call(functools.partial(attend_back_kernel, 0, False), [short], (head0, logit_scale), (x0, d0))
    qkv0 = exchange(qkv0, aligned)
    (parts,) = call(
        last_kernel,
        [((8, TILES * C // 8, 128), bf16)],
        (),
        (qkv0, tokens0, got, gains0, gains1),
        fetched=(kept,),
    )
    parts = exchange(parts, across)
    (parts,) = call(first_sum_kernel, [((8, TILES * 8, 128), bf16)], (), (parts,))
    parts = exchange(parts, aligned)
    (share,) = call(second_sum_kernel, [((TILES * 8, 128), f32)], (), (parts,))
    (share,) = call(add_kernel, [((TILES * 8, 128), f32)], (), (share, swap(share, 2)))
    other = swap(share, 1)
    qkv0, _ = lax.optimization_barrier((qkv0, share))
    (grad_image,) = call(image_kernel, [cells], (), (qkv0, (w_qkv, 0), grad0))
    small = ((2, 8), f32)
    grad_qkv, grad_proj, grad_gain, grad_bias = call(
        final_kernel,
        [((2, 8, 3 * HH), f32), ((2, 8, HH), f32), small, small],
        (core,),
        (share, other),
    )
    return (
        grad_image.reshape(image.shape),
        grad_qkv,
        grad_proj.transpose(0, 2, 1),
        grad_gain,
        grad_bias,
    )


def solution(mesh):
    placed = (P("dp", "rows", None, None), P("dp", "rows", None, None)) + (P(),) * 7
    return jax.shard_map(
        body,
        mesh=mesh,
        in_specs=placed,
        out_specs=(
            P("dp", "rows", None, None),
            P(None, "rows", None),
            P(None, None, "rows"),
            P(None, "rows"),
            P(None, "rows"),
        ),
        check_vma=False,
    )
```

```python
import functools

import jax
import jax.numpy as jnp
from jax import lax
from jax.experimental import pallas as pl
from jax.experimental.pallas import tpu as pltpu
from jax.sharding import PartitionSpec as P

C = 512
HEADS = 8
HD = 32
WIN = 24
HH = 256
SHIFT = 12
GROUP = 8
TOK = 144
CELLS = WIN * WIN
ROWS_DEV = 3
PACK = 48
DEVS = 64
VMEM_LIMIT = 24 * 2**20
EARLY = 3 * HH + 2 * HH
SHORT = 112
LATE = 3 * HH
TILES = (LATE // 2 + EARLY // 2) // 128
SENT = TILES * C // 8 + 16
SHARE = TILES * 8 + 16

norm_eps = 1e-05
mask_value = 100.0
f32 = jnp.float32
bf16 = jnp.bfloat16


def dot(a, b):
    return jnp.dot(a, b, preferred_element_type=f32)


def dot_t(a, b):
    return lax.dot_general(a, b, (((1,), (1,)), ((), ())), preferred_element_type=f32)


def dot_0(a, b):
    return lax.dot_general(a, b, (((0,), (0,)), ((), ())), preferred_element_type=f32)


def iota(shape, axis):
    return lax.broadcasted_iota(jnp.int32, shape, axis)


def head_sums(x):
    width = x.shape[1]
    ones = (iota((width, width), 0) // HD == iota((width, width), 1) // HD).astype(f32).astype(bf16)
    high = x.astype(bf16)
    low = (x - high.astype(f32)).astype(bf16)
    return dot(high, ones) + dot(low, ones)


def split_two(x):
    high = x.astype(bf16).astype(f32)
    return high, x - high


def lane_slice(x, at):
    return x[:, at : at + HD]


def send_projected(tokens, weight, scale_ref, block, out_ref, factors_ref):
    projected = dot(tokens, weight)
    query, key, value = projected[:, :HH], projected[:, HH : 2 * HH], projected[:, 2 * HH :]
    lane = iota((1, HH), 1)
    scale = jnp.zeros((1, HH), f32)
    scales = scale_ref[...][block : block + 1]
    for h in range(HEADS):
        scale = jnp.where(lane // HD == h, scales[:, h : h + 1], scale)
    q_factor = lax.rsqrt(1.0 + head_sums(query * query))
    k_factor = lax.rsqrt(1.0 + head_sums(key * key))
    slot = iota((PACK, HH), 1) % HD
    factors = jnp.zeros((PACK, HH), f32)
    for r in range(ROWS_DEV):
        rows = slice(r * PACK, (r + 1) * PACK)
        values = [*split_two(q_factor[rows]), *split_two(k_factor[rows])]
        for i, part in enumerate(values):
            factors = jnp.where(slot == 4 * r + i, part, factors)
    factors_ref[...] = factors.astype(bf16)
    q_hat = query * q_factor * jnp.exp(scale)
    k_hat = key * k_factor
    zeros = jnp.zeros((SHORT - 3 * (TOK - SHORT), HD), f32)
    for h in range(HEADS):
        parts = [lane_slice(part, h * HD) for part in (q_hat, k_hat, value)]
        tail = jnp.concatenate([part[SHORT:] for part in parts] + [zeros], 0)
        out_ref[h] = jnp.concatenate([part[:SHORT] for part in parts] + [tail], 1).astype(bf16)


def unpack_cells(x_ref):
    x = x_ref[...].astype(f32)
    lane = iota((GROUP * 32, 128), 1)
    rolled = [
        pltpu.roll(x[:, kind * 32 : kind * 32 + 32].reshape(GROUP * 32, 128), 32 + 32 * kind, 1)
        for kind in range(3)
    ]
    tail = jnp.where(lane < HD, rolled[0], jnp.where(lane < 2 * HD, rolled[1], rolled[2]))
    return jnp.concatenate([x, tail.reshape(GROUP, 32, 128)], 1)


def unpack_heads(packed_ref):
    packed = [packed_ref[h].astype(f32) for h in range(HEADS)]
    rows = [
        jnp.concatenate([lane_slice(packed[h], r * HD) for h in range(HEADS)], 1)
        for r in range(ROWS_DEV)
    ]
    return jnp.concatenate(rows, 0).astype(bf16)


def pack_heads(array, factors, out_ref):
    factors = factors.astype(f32)
    for h in range(HEADS):
        parts = [lane_slice(array[r * PACK : (r + 1) * PACK], h * HD) for r in range(ROWS_DEV)]
        out_ref[h] = jnp.concatenate(parts + [lane_slice(factors, h * HD)], 1).astype(bf16)


def to_windows(array):
    split = array.reshape(GROUP, ROWS_DEV, 2, WIN, array.shape[-1])
    return [split[:, :, w].reshape(CELLS, array.shape[-1]) for w in range(2)]


def from_windows(pair):
    depth = pair[0].shape[-1]
    parts = [part.reshape(GROUP, ROWS_DEV, 1, WIN, depth) for part in pair]
    return jnp.concatenate(parts, 2).reshape(GROUP, TOK, depth)


def pack_cells(cells):
    tail = cells[:, SHORT:].reshape(GROUP * 32, 128)
    moved = [pltpu.roll(tail, 96 - 32 * kind, 1).reshape(GROUP, 32, 128) for kind in range(3)]
    moved = jnp.concatenate(moved + [jnp.zeros((GROUP, SHORT - 96, 128), f32)], 1)
    lane = iota(moved.shape, 2)
    return jnp.where(lane < 96, cells[:, :SHORT], moved)


def roll_tokens(array, by):
    by = by % TOK
    return jnp.concatenate([array[TOK - by :], array[: TOK - by]], 0)


def normalized(attended, weight):
    outputs = dot(attended, weight)
    centered = outputs - jnp.mean(outputs, -1, keepdims=True)
    inverse = lax.rsqrt(jnp.mean(centered * centered, -1, keepdims=True) + norm_eps)
    return centered * inverse, inverse


def finish_back(attended, weight, gain_row, grad_out):
    y_hat, inverse = normalized(attended, weight)
    grad_gain = jnp.sum(grad_out * y_hat, 0, keepdims=True)
    grad_bias = jnp.sum(grad_out, 0, keepdims=True)
    scaled = grad_out * gain_row
    grad_y = inverse * (
        scaled
        - jnp.mean(scaled, -1, keepdims=True)
        - y_hat * jnp.mean(scaled * y_hat, -1, keepdims=True)
    )
    grad_y = grad_y.astype(bf16)
    gains = jnp.concatenate([grad_gain, grad_bias, jnp.zeros((6, C), f32)], 0)
    return grad_y, dot_t(grad_y, weight), gains


def labels_of(axis, window, first_row, row_ref, col_ref):
    shape = (CELLS, 1) if axis == 0 else (1, CELLS)
    at = iota(shape, axis)
    source = at // (ROWS_DEV * WIN)
    rest = at - source * (ROWS_DEV * WIN)
    local_row = rest // WIN
    column = rest - local_row * WIN + window * WIN
    local_row = local_row + (column >= 36).astype(jnp.int32)
    local_row = jnp.where(local_row >= ROWS_DEV, local_row - ROWS_DEV, local_row)
    row = first_row + source * ROWS_DEV + local_row
    row_label = jnp.zeros(shape, jnp.int32)
    col_label = jnp.zeros(shape, jnp.int32)
    for label in (1, 2):
        row_cut = jnp.sum((row_ref[...] < label).astype(jnp.int32), 1, keepdims=True)
        col_cut = jnp.sum((col_ref[...] < label).astype(jnp.int32), 1, keepdims=True)
        row_label = row_label + (row >= row_cut).astype(jnp.int32)
        col_label = col_label + (column >= col_cut).astype(jnp.int32)
    return 3 * row_label + col_label


def masked(scores, window, mask_refs):
    if mask_refs is None:
        return scores
    first_row = mask_refs[0][0]
    one = labels_of(0, window, first_row, *mask_refs[1:])
    two = labels_of(1, window, first_row, *mask_refs[1:])
    return scores - jnp.where(one == two, 0.0, mask_value)


def attend_kernel(masks, x_ref, *refs):
    mask_refs = refs[:3] if masks else None
    out_ref = refs[-1]
    lane = iota((CELLS, 128), 1)
    per_window = []
    for w, cells in enumerate(to_windows(unpack_cells(x_ref))):
        query = cells[:, :HD].astype(bf16)
        key = cells[:, HD : 2 * HD].astype(bf16)
        value = jnp.where(lane < HD, pltpu.roll(cells, 64, 1), jnp.where(lane == HD, 1.0, 0.0)).astype(bf16)
        scores = masked(dot_t(query, key), w, mask_refs)
        weights = jnp.exp(scores).astype(bf16)
        summed = dot(weights, value)
        attended = jnp.where(lane < HD, summed * (1.0 / summed[:, HD : HD + 1]), 0.0)
        per_window.append(attended.reshape(GROUP, ROWS_DEV, WIN, 128))
    total = 0.0
    for r in range(ROWS_DEV):
        rows = jnp.concatenate([part[:, r] for part in per_window], 1).reshape(GROUP * PACK, 128)
        total = total + (rows if r == 0 else pltpu.roll(rows, r * HD, 1))
    out_ref[...] = total.astype(bf16).reshape(GROUP, PACK, 128)


def attend_back_kernel(block, masks, head_ref, scale_ref, x_ref, grad_ref, *refs):
    mask_refs = refs[:3] if masks else None
    out_ref = refs[-1]
    lane = iota((CELLS, 128), 1)
    low = iota((HD, CELLS), 0)
    scale_row = jnp.exp(jnp.full((1, 128), scale_ref[block, head_ref[0]], f32))
    unscale_row = 1.0 / scale_row
    packed = grad_ref[...].astype(f32).reshape(GROUP * PACK, 128)
    low_lane = iota(packed.shape, 1) < HD
    rolled = [packed] + [
        jnp.where(low_lane, pltpu.roll(packed, 128 - r * HD, 1), pltpu.roll(packed, 128 - r * 4, 1))
        for r in range(1, ROWS_DEV)
    ]
    rolled = [part.reshape(GROUP, 1, 2, WIN, 128) for part in rolled]
    grads = jnp.concatenate(rolled, 1)
    results = []
    for w, cells in enumerate(to_windows(unpack_cells(x_ref))):
        turned = cells.T
        query_t = turned[:HD].astype(bf16)
        key_t = turned[HD : 2 * HD].astype(bf16)
        value_t = turned[2 * HD : 3 * HD]
        grad = grads[:, :, w].reshape(CELLS, 128)
        grad_t = grad.T[:HD]
        key = cells[:, HD : 2 * HD].astype(bf16)
        scores = masked(dot(key, query_t), w, mask_refs)
        weights = jnp.exp(scores).astype(bf16)
        summed = dot(jnp.concatenate([value_t, jnp.where(low == 0, 1.0, 0.0)], 0).astype(bf16), weights)
        inverse = 1.0 / summed[HD : HD + 1]
        grad_t = (grad_t * inverse).astype(bf16).astype(f32)
        row_high, row_low = split_two(jnp.sum(grad_t * summed[:HD], 0, keepdims=True) * inverse)
        rows = jnp.where(low == 0, -row_high, jnp.where(low == 1, -row_low, 0.0))
        grad_ext = jnp.concatenate([grad_t, rows], 0).astype(bf16)
        ones = jnp.where(lane < HD + 2, 1.0, 0.0)
        value_ext = jnp.where(lane < HD, pltpu.roll(cells, 64, 1), ones)[:, :64].astype(bf16)
        grad_scores = (weights.astype(f32) * dot(value_ext, grad_ext)).astype(bf16)
        query_at = jnp.where((lane >= HD) & (lane < 2 * HD), pltpu.roll(cells, HD, 1), 0.0).astype(bf16)
        zeros = jnp.zeros((HD, CELLS), f32)
        grad_at = jnp.concatenate([zeros, zeros, grad_t, zeros], 0).T.astype(bf16)
        grad_kv = dot(grad_scores, query_at) + dot(weights, grad_at)
        grad_q = dot(key_t, grad_scores)
        grad_q = jnp.concatenate([grad_q, zeros, zeros, zeros], 0).T
        total = jnp.where(lane < HD, grad_q * scale_row, grad_kv)
        unit = jnp.where(lane < HD, cells * unscale_row, jnp.where(lane < 2 * HD, cells, 0.0))
        q_factor = grad[:, 96:97] + grad[:, 97:98]
        k_factor = grad[:, 98:99] + grad[:, 99:100]
        factor = jnp.where(lane < HD, q_factor, jnp.where(lane < 2 * HD, k_factor, 1.0))
        results.append(factor * (total - unit * head_sums(unit * total)))
    out_ref[...] = pack_cells(from_windows(results)).astype(bf16)


def first_kernel(tokens_ref, w_ref, scale_ref, out_ref, factors_ref):
    send_projected(tokens_ref[...], w_ref[...], scale_ref, 0, out_ref, factors_ref)


def middle_kernel(packed_ref, scale_ref, gain_ref, bias_ref, tokens_ref, w_proj_ref, w_ref, out_ref, rolled_ref, factors_ref):
    attended = unpack_heads(packed_ref)
    y_hat, _ = normalized(attended, w_proj_ref[...])
    out = (tokens_ref[...].astype(f32) + y_hat * gain_ref[0:1] + bias_ref[0:1]).astype(bf16).astype(f32)
    rolled = roll_tokens(out, -SHIFT).astype(bf16)
    rolled_ref[...] = rolled
    send_projected(rolled, w_ref[...], scale_ref, 1, out_ref, factors_ref)


def turn_kernel(core_ref, packed_ref, gain_ref, grad_ref, w_proj_ref, factors_ref, out_ref, kept_ref, given_ref, gains_ref):
    attended = unpack_heads(packed_ref)
    grad = roll_tokens(grad_ref[...].astype(f32), -SHIFT)
    grad_y, grad_att, gains = finish_back(attended, w_proj_ref[...], gain_ref[1:2], grad)
    pack_heads(grad_att, factors_ref[...], out_ref)
    kept, given = halves(attended, core_ref[0])
    kept_ref[...] = dot_0(grad_y, kept).astype(bf16)
    given_ref[...] = dot_0(grad_y, given).astype(bf16)
    gains_ref[...] = gains


def gather_qkv(qkv_ref):
    parts = [qkv_ref[h].astype(f32) for h in range(HEADS)]
    top = [lane_slice(parts[h][:SHORT], kind * HD) for kind in range(3) for h in range(HEADS)]
    tail = [lane_slice(parts[h][kind * 32 : kind * 32 + 32], 96) for kind in range(3) for h in range(HEADS)]
    return jnp.concatenate([jnp.concatenate(top, 1), jnp.concatenate(tail, 1)], 0).astype(bf16)


def halves(array, core):
    half = array.shape[1] // 2
    left, right = array[:, :half].astype(f32), array[:, half:].astype(f32)
    return jnp.where(core == 0, left, right).astype(bf16), jnp.where(core == 0, right, left).astype(bf16)


def back_kernel(
    core_ref,
    qkv_ref,
    packed_ref,
    gain_ref,
    w_ref,
    w_proj_ref,
    grad_ref,
    proj1_kept_ref,
    proj1_given_ref,
    tokens_ref,
    factors_ref,
    out_ref,
    gains_ref,
    grad0_ref,
    kept_ref,
    given_ref,
):
    d_qkv = gather_qkv(qkv_ref)
    from_qkv = roll_tokens(dot_t(d_qkv, w_ref[...]), SHIFT)
    grad = (grad_ref[...].astype(f32) + from_qkv).astype(bf16)
    grad0_ref[...] = grad
    attended = unpack_heads(packed_ref)
    grad_y, grad_att, gains = finish_back(attended, w_proj_ref[...], gain_ref[0:1], grad.astype(f32))
    sides = zip(halves(d_qkv, core_ref[0]), (proj1_kept_ref, proj1_given_ref), halves(attended, core_ref[0]))
    kept, given = [
        jnp.concatenate(
            [dot_0(tokens_ref[...], part).astype(bf16), proj1_ref[...], dot_0(grad_y, att).astype(bf16)], 1
        )
        for part, proj1_ref, att in sides
    ]
    kept_ref[...] = kept
    given_ref[...] = given
    pack_heads(grad_att, factors_ref[...], out_ref)
    gains_ref[...] = gains


def image_kernel(qkv_ref, w_ref, grad_ref, out_ref):
    out_ref[...] = (grad_ref[...].astype(f32) + dot_t(gather_qkv(qkv_ref), w_ref[...])).astype(bf16)


def last_kernel(core_ref, qkv_ref, tokens_ref, kept_ref, given_ref):
    kept, given = halves(gather_qkv(qkv_ref), core_ref[0])
    given_ref[...] = dot_0(tokens_ref[...], given).astype(bf16)
    kept_ref[...] = dot_0(tokens_ref[...], kept).astype(bf16)


def parts_kernel(late_ref, got_late_ref, got_ref, gains0_ref, gains1_ref, kept_ref, parts_ref):
    pieces = []
    for ref in (gains0_ref, gains1_ref):
        for row in (0, 1):
            pieces += split_two(ref[row : row + 1])
    gains = jnp.concatenate(pieces + [jnp.zeros((16 - len(pieces), C), f32)], 0)
    depth = C // 8
    for ring in range(8):
        block = gains[:, ring // 2 * 128 : ring // 2 * 128 + 128]
        block = pltpu.roll(block, depth, 1) if ring % 2 else block
        parts_ref[ring, TILES * depth :] = block.astype(bf16)
    late = late_ref[...].astype(f32) + got_late_ref[...].astype(f32)
    early = kept_ref[...].astype(f32) + got_ref[...].astype(f32)
    tile = 0
    for part in (late, early):
        for at in range(0, part.shape[1], 128):
            block = part[:, at : at + 128].astype(bf16).reshape(8, depth, 128)
            parts_ref[:, tile * depth : (tile + 1) * depth, :] = block
            tile += 1


def first_sum_kernel(parts_ref, out_ref):
    total = jnp.sum(parts_ref[...].astype(f32), 0)
    gains = total[TILES * C // 8 :]
    total = total[: TILES * C // 8].reshape(TILES, 8, 8, 128)
    for place in range(8):
        rolled = pltpu.roll(gains, 128 - 8 * place, 1) if place else gains
        out_ref[place] = jnp.concatenate([total[:, place].reshape(TILES * 8, 128), rolled], 0).astype(bf16)


def second_sum_kernel(parts_ref, out_ref):
    out_ref[...] = jnp.sum(parts_ref[...].astype(f32), 0)


def add_kernel(one_ref, two_ref, out_ref):
    out_ref[...] = one_ref[...] + two_ref[...]


def final_kernel(core_ref, own_ref, other_ref, qkv_ref, proj_ref, gain_ref, bias_ref):
    own = own_ref[: TILES * 8].reshape(TILES, 8, 128)
    other = other_ref[: TILES * 8].reshape(TILES, 8, 128)
    first = core_ref[0] == 0
    left, right = jnp.where(first, own, other), jnp.where(first, other, own)
    for block, tiles in ((0, (0, 1, 2)), (1, (3, 4, 5))):
        qkv_ref[block] = jnp.concatenate([side[i] for side in (left, right) for i in tiles], 1)
    proj_ref[1] = jnp.concatenate([left[6], right[6]], 1)
    proj_ref[0] = jnp.concatenate([left[7], right[7]], 1)
    gains = (own_ref[TILES * 8 :] + other_ref[TILES * 8 :])[:, :8]
    gain_ref[...] = jnp.concatenate([gains[0:1] + gains[1:2], gains[4:5] + gains[5:6]], 0)
    bias_ref[...] = jnp.concatenate([gains[2:3] + gains[3:4], gains[6:7] + gains[7:8]], 0)


def pieces_of(shape):
    return 4 if shape[0] % 64 == 0 and shape[0] * shape[1] >= 2**18 else 1


def copies_of(source, target, sems, first):
    count = pieces_of(target.shape)
    rows = target.shape[0] // count
    if count == 1:
        return [pltpu.make_async_copy(source, target, sems.at[first])]
    return [
        pltpu.make_async_copy(
            source.at[pl.ds(i * rows, rows)], target.at[pl.ds(i * rows, rows)], sems.at[first + i]
        )
        for i in range(count)
    ]


class Fetched:
    def __init__(self, source, ref, sems, first):
        self.ref, self.copies = ref, copies_of(source, ref, sems, first)
        for copy in self.copies:
            copy.start()
        self.waited = False

    def __getitem__(self, at):
        if not self.waited:
            for copy in self.copies:
                copy.wait()
            self.waited = True
        return self.ref[at]


class Stored:
    def __init__(self, ref, target, sems, first):
        self.ref, self.copies = ref, copies_of(ref, target, sems, first)

    def __setitem__(self, at, value):
        self.ref[at] = value
        for copy in self.copies:
            copy.start()


def call(kernel, outs, scalars, arrays, masks=(), fetched=(), stored=()):
    arrays = [item if isinstance(item, tuple) else (item, None) for item in arrays]
    fetched = [item if isinstance(item, tuple) else (item, None) for item in fetched]
    counts = [len(scalars), len(arrays), len(fetched), len(masks), len(outs), len(stored), len(fetched), len(stored)]

    def wrapped(*refs):
        parts, at = [], 0
        for count in counts:
            parts.append(refs[at : at + count])
            at += count
        scalar_refs, array_refs, sources, mask_refs, out_refs, targets, filled, sent = parts
        sems = refs[-1]
        near = [ref if block is None else ref.at[block] for ref, (_, block) in zip(array_refs, arrays)]
        far, results, first = [], [], 0
        for i, (_, block) in enumerate(fetched):
            source = sources[i] if block is None else sources[i].at[block]
            far.append(Fetched(source, filled[i], sems, first))
            first += pieces_of(filled[i].shape)
        for i in range(len(stored)):
            results.append(Stored(sent[i], targets[i], sems, first))
            first += pieces_of(sent[i].shape)
        kernel(*scalar_refs, *near, *far, *mask_refs, *out_refs, *results)
        for result in results:
            for copy in result.copies:
                copy.wait()

    smem = pl.BlockSpec(memory_space=pltpu.SMEM)
    vmem = pl.BlockSpec(memory_space=pltpu.VMEM)
    hbm = pl.BlockSpec(memory_space=pltpu.HBM)
    scratch = [
        pltpu.VMEM(array.shape if block is None else array.shape[1:], array.dtype) for array, block in fetched
    ]
    scratch += [pltpu.VMEM(*out) for out in stored]
    if scratch:
        scratch.append(pltpu.SemaphoreType.DMA((sum(pieces_of(buffer.shape) for buffer in scratch),)))
    return pl.pallas_call(
        wrapped,
        out_shape=[jax.ShapeDtypeStruct(*out) for out in outs] + [pltpu.HBM(*out) for out in stored],
        in_specs=[smem] * len(scalars)
        + [vmem] * len(arrays)
        + [hbm] * len(fetched)
        + [smem, vmem, vmem][: len(masks)],
        out_specs=[vmem] * len(outs) + [hbm] * len(stored),
        scratch_shapes=scratch,
        compiler_params=pltpu.CompilerParams(vmem_limit_bytes=VMEM_LIMIT),
    )(
        *scalars,
        *(array for array, _ in arrays),
        *(pltpu.with_memory_space_constraint(array, pltpu.HBM) for array, _ in fetched),
        *masks,
    )


def body(image, out_grad, w_qkv, w_proj, norm_gain, norm_bias, logit_scale, row_band, col_band):
    position = lax.axis_index("rows")
    half = GROUP // 2
    rings = range(DEVS // GROUP)
    aligned = [[GROUP * g + i for i in range(GROUP)] for g in rings]
    across = [[GROUP * g + i for g in rings] for i in range(GROUP)]
    moved = [[(GROUP * g + half + i) % DEVS for i in range(GROUP)] for g in rings]
    moved_position = (position + DEVS - half) % DEVS
    head0 = (position % GROUP).reshape(1)
    head1 = (moved_position % GROUP).reshape(1)
    first_row = (moved_position // GROUP * WIN).reshape(1)
    core = (lax.axis_index("dp") % 2).reshape(1)
    image, head0, head1, first_row, core = lax.optimization_barrier((image, head0, head1, first_row, core))
    masks = (first_row, row_band.reshape(1, -1), col_band.reshape(1, -1))

    def exchange(array, groups):
        return lax.all_to_all(array, "rows", 0, 0, axis_index_groups=groups, tiled=True)

    tokens0 = image.reshape(TOK, C)
    grad_out = out_grad.reshape(TOK, C)
    short = ((GROUP, SHORT, 128), bf16)
    factors = ((PACK, HH), bf16)
    narrow = ((GROUP, PACK, 128), bf16)
    cells = ((TOK, C), bf16)
    proj = ((C, HH // 2), bf16)
    gains = ((8, C), f32)
    half_early = ((C, EARLY // 2), bf16)
    half_late = ((C, LATE // 2), bf16)

    def swap(array, apart):
        return lax.ppermute(array, "dp", [(i, i ^ apart) for i in range(4)])

    x0, factors0 = call(
        first_kernel, [short], (), (), fetched=(tokens0, (w_qkv, 0), logit_scale), stored=[factors]
    )
    x0 = exchange(x0, aligned)
    (a0,) = call(functools.partial(attend_kernel, False), [narrow], (), (x0,))
    a0 = exchange(a0, aligned)
    x1, tokens1, factors1 = call(
        middle_kernel,
        [short],
        (),
        (a0, logit_scale, norm_gain, norm_bias, tokens0, (w_proj, 0), (w_qkv, 1)),
        stored=[cells, factors],
    )
    x1 = exchange(x1, moved)
    (a1,) = call(functools.partial(attend_kernel, True), [narrow], (), (x1,), masks)
    a1 = exchange(a1, moved)
    d1, proj1_kept, proj1_given, gains1 = call(
        turn_kernel,
        [narrow, proj, proj, gains],
        (core,),
        (a1, norm_gain, grad_out, (w_proj, 1), factors1),
    )
    d1 = exchange(d1, moved)
    (qkv1,) = call(
        functools.partial(attend_back_kernel, 1, True), [short], (head1, logit_scale), (x1, d1), masks
    )
    qkv1 = exchange(qkv1, moved)
    d0, gains0, grad0, kept, given = call(
        back_kernel,
        [narrow, gains],
        (core,),
        (qkv1, a0, norm_gain, (w_qkv, 1), (w_proj, 0), grad_out, proj1_kept, proj1_given, tokens1, factors0),
        stored=[cells, half_early, half_early],
    )
    d0 = exchange(d0, aligned)
    (qkv0,) = call(functools.partial(attend_back_kernel, 0, False), [short], (head0, logit_scale), (x0, d0))
    qkv0 = exchange(qkv0, aligned)
    qkv0, given = lax.optimization_barrier((qkv0, given))
    got = swap(given, 1)
    late, given_late = call(last_kernel, [half_late, half_late], (core,), (qkv0, tokens0))
    got_late = swap(given_late, 1)
    (parts,) = call(
        parts_kernel,
        [((8, SENT, 128), bf16)],
        (),
        (late, got_late, got, gains0, gains1, kept),
    )
    parts = exchange(parts, across)
    (parts,) = call(first_sum_kernel, [((8, SHARE, 128), bf16)], (), (parts,))
    parts = exchange(parts, aligned)
    (share,) = call(second_sum_kernel, [((SHARE, 128), f32)], (), (parts,))
    (share,) = call(add_kernel, [((SHARE, 128), f32)], (), (share, swap(share, 2)))
    other = swap(share, 1)
    qkv0, _ = lax.optimization_barrier((qkv0, share))
    (grad_image,) = call(image_kernel, [cells], (), (qkv0, (w_qkv, 0), grad0))
    small = ((2, 8), f32)
    grad_qkv, grad_proj, grad_gain, grad_bias = call(
        final_kernel,
        [((2, 8, 3 * HH), f32), ((2, 8, HH), f32), small, small],
        (core,),
        (share, other),
    )
    return (
        grad_image.reshape(image.shape),
        grad_qkv,
        grad_proj.transpose(0, 2, 1),
        grad_gain,
        grad_bias,
    )


def solution(mesh):
    placed = (P("dp", "rows", None, None), P("dp", "rows", None, None)) + (P(),) * 7
    return jax.shard_map(
        body,
        mesh=mesh,
        in_specs=placed,
        out_specs=(
            P("dp", "rows", None, None),
            P(None, "rows", None),
            P(None, None, "rows"),
            P(None, "rows"),
            P(None, "rows"),
        ),
        check_vma=False,
    )
```

```python
import functools

import jax
import jax.numpy as jnp
from jax import lax
from jax.experimental import pallas as pl
from jax.experimental.pallas import tpu as pltpu
from jax.sharding import PartitionSpec as P

C = 512
HEADS = 8
HD = 32
WIN = 24
HH = 256
SHIFT = 12
GROUP = 8
TOK = 144
CELLS = WIN * WIN
ROWS_DEV = 3
PACK = 48
DEVS = 64
VMEM_LIMIT = 24 * 2**20
EARLY = 3 * HH + 2 * HH
SHORT = 112
LATE = 3 * HH
TILES = (LATE // 2 + EARLY // 2) // 128
SENT = TILES * C // 8 + 16
SHARE = TILES * 8 + 16

norm_eps = 1e-05
f32 = jnp.float32
bf16 = jnp.bfloat16


def dot(a, b):
    return jnp.dot(a, b, preferred_element_type=f32)


def dot_t(a, b):
    return lax.dot_general(a, b, (((1,), (1,)), ((), ())), preferred_element_type=f32)


def dot_0(a, b):
    return lax.dot_general(a, b, (((0,), (0,)), ((), ())), preferred_element_type=f32)


def iota(shape, axis):
    return lax.broadcasted_iota(jnp.int32, shape, axis)


def head_sums(x):
    width = x.shape[1]
    ones = (iota((width, width), 0) // HD == iota((width, width), 1) // HD).astype(f32).astype(bf16)
    high = x.astype(bf16)
    low = (x - high.astype(f32)).astype(bf16)
    return dot(high, ones) + dot(low, ones)


def split_two(x):
    high = x.astype(bf16).astype(f32)
    return high, x - high


def lane_slice(x, at):
    return x[:, at : at + HD]


def send_projected(tokens, weight, scale_ref, block, out_ref):
    projected = dot(tokens, weight)
    query, key, value = projected[:, :HH], projected[:, HH : 2 * HH], projected[:, 2 * HH :]
    lane = iota((1, HH), 1)
    scale = jnp.zeros((1, HH), f32)
    scales = scale_ref[...][block : block + 1]
    for h in range(HEADS):
        scale = jnp.where(lane // HD == h, scales[:, h : h + 1], scale)
    q_factor = lax.rsqrt(1.0 + head_sums(query * query))
    k_factor = lax.rsqrt(1.0 + head_sums(key * key))
    q_hat = query * q_factor * jnp.exp(scale)
    k_hat = key * k_factor
    slot = iota((16, HH), 1) % HD
    factors = jnp.zeros((16, HH), f32)
    for i in range(TOK // 16):
        rows = slice(16 * i, 16 * i + 16)
        factors = jnp.where(slot == 2 * i, q_factor[rows], jnp.where(slot == 2 * i + 1, k_factor[rows], factors))
    for h in range(HEADS):
        parts = [lane_slice(part, h * HD) for part in (q_hat, k_hat, value)]
        tail = jnp.concatenate([part[SHORT:] for part in parts] + [lane_slice(factors, h * HD)], 0)
        out_ref[h] = jnp.concatenate([part[:SHORT] for part in parts] + [tail], 1).astype(bf16)


def unpack_cells(x_ref):
    x = x_ref[...].astype(f32)
    lane = iota((GROUP * 32, 128), 1)
    rolled = [
        pltpu.roll(x[:, kind * 32 : kind * 32 + 32].reshape(GROUP * 32, 128), 32 + 32 * kind, 1)
        for kind in range(3)
    ]
    tail = jnp.where(lane < HD, rolled[0], jnp.where(lane < 2 * HD, rolled[1], rolled[2]))
    return jnp.concatenate([x, tail.reshape(GROUP, 32, 128)], 1)


def unpack_factors(x_ref):
    rows = x_ref[...].astype(f32)[:, SHORT - 16 :].reshape(GROUP * 16, 128)
    rolled = [pltpu.roll(rows, 128 - 2 * i, 1) if i else rows for i in range(TOK // 16)]
    return jnp.concatenate([part.reshape(GROUP, 16, 128) for part in rolled], 1)


def unpack_heads(packed_ref):
    packed = [packed_ref[h].astype(f32) for h in range(HEADS)]
    rows = [
        jnp.concatenate([lane_slice(packed[h], r * HD) for h in range(HEADS)], 1)
        for r in range(ROWS_DEV)
    ]
    return jnp.concatenate(rows, 0).astype(bf16)


def pack_heads(array, out_ref):
    zeros = jnp.zeros((PACK, HD), f32)
    for h in range(HEADS):
        parts = [lane_slice(array[r * PACK : (r + 1) * PACK], h * HD) for r in range(ROWS_DEV)]
        out_ref[h] = jnp.concatenate(parts + [zeros], 1).astype(bf16)


def to_windows(array):
    split = array.reshape(GROUP, ROWS_DEV, 2, WIN, array.shape[-1])
    return [split[:, :, w].reshape(CELLS, array.shape[-1]) for w in range(2)]


def from_windows(pair):
    depth = pair[0].shape[-1]
    parts = [part.reshape(GROUP, ROWS_DEV, 1, WIN, depth) for part in pair]
    return jnp.concatenate(parts, 2).reshape(GROUP, TOK, depth)


def pack_cells(cells):
    tail = cells[:, SHORT:].reshape(GROUP * 32, 128)
    moved = [pltpu.roll(tail, 96 - 32 * kind, 1).reshape(GROUP, 32, 128) for kind in range(3)]
    moved = jnp.concatenate(moved + [jnp.zeros((GROUP, SHORT - 96, 128), f32)], 1)
    lane = iota(moved.shape, 2)
    return jnp.where(lane < 96, cells[:, :SHORT], moved)


def roll_tokens(array, by):
    by = by % TOK
    return jnp.concatenate([array[TOK - by :], array[: TOK - by]], 0)


def normalized(attended, weight):
    outputs = dot(attended, weight)
    centered = outputs - jnp.mean(outputs, -1, keepdims=True)
    inverse = lax.rsqrt(jnp.mean(centered * centered, -1, keepdims=True) + norm_eps)
    return centered * inverse, inverse


def finish_back(attended, weight, gain_row, grad_out):
    y_hat, inverse = normalized(attended, weight)
    grad_gain = jnp.sum(grad_out * y_hat, 0, keepdims=True)
    grad_bias = jnp.sum(grad_out, 0, keepdims=True)
    scaled = grad_out * gain_row
    grad_y = inverse * (
        scaled
        - jnp.mean(scaled, -1, keepdims=True)
        - y_hat * jnp.mean(scaled * y_hat, -1, keepdims=True)
    )
    grad_y = grad_y.astype(bf16)
    gains = jnp.concatenate([grad_gain, grad_bias, jnp.zeros((6, C), f32)], 0)
    return grad_y, dot_t(grad_y, weight), gains


def tags_of(window, first_row_ref, row_ref, col_ref):
    lane = iota((WIN, 128), 1)
    place = iota((WIN, 1), 0)
    column = place + window * WIN
    col_label = jnp.zeros((WIN, 1), jnp.int32)
    for label in (1, 2):
        cut = jnp.sum((col_ref[...] < label).astype(jnp.int32), 1, keepdims=True)
        col_label = col_label + (column >= cut).astype(jnp.int32)
    blocks = []
    for source in range(GROUP):
        rows = [row_ref[first_row_ref[0] + source * ROWS_DEV + r] for r in range(ROWS_DEV)]
        for r in range(ROWS_DEV):
            row_label = rows[r]
            if window == 1:
                row_label = jnp.where(column >= 36, rows[(r + 1) % ROWS_DEV], rows[r])
            blocks.append(jnp.where(lane == col_label + 3 * row_label + 96, 10.0, 0.0))
    return jnp.concatenate(blocks, 0)


def tagged(cells, window, mask_refs):
    if mask_refs is None:
        return cells
    return jnp.where(iota(cells.shape, 1) < 96, cells, tags_of(window, *mask_refs))


def with_tags(cells, at, key):
    lane = iota(cells.shape, 1)
    own = cells if at == 0 else pltpu.roll(cells, 128 - at, 1)
    tags = pltpu.roll(cells, 64, 1)
    if key:
        tags = jnp.where(lane < HD + 9, tags - 10.0, tags)
    return jnp.where(lane < HD, own, tags)[:, :64].astype(bf16)


def together(steps):
    steps = list(steps)
    while steps:
        steps = [step for step in steps if next(step, 0) is None]


def attend_kernel(masks, x_ref, *refs):
    mask_refs = refs[:3] if masks else None
    out_ref = refs[-1]
    lane = iota((CELLS, 128), 1)
    per_window = [None, None]

    def attend(w, cells):
        cells = tagged(cells, w, mask_refs)
        query = with_tags(cells, 0, False) if masks else cells[:, :HD].astype(bf16)
        key = with_tags(cells, HD, True) if masks else cells[:, HD : 2 * HD].astype(bf16)
        value = jnp.where(lane < HD, pltpu.roll(cells, 64, 1), jnp.where(lane == HD, 1.0, 0.0)).astype(bf16)
        yield
        scores = dot_t(query, key)
        yield
        weights = jnp.exp(scores).astype(bf16)
        yield
        summed = dot(weights, value)
        yield
        attended = jnp.where(lane < HD, summed * (1.0 / summed[:, HD : HD + 1]), 0.0)
        per_window[w] = attended.reshape(GROUP, ROWS_DEV, WIN, 128)

    together(attend(w, cells) for w, cells in enumerate(to_windows(unpack_cells(x_ref))))
    total = 0.0
    for r in range(ROWS_DEV):
        rows = jnp.concatenate([part[:, r] for part in per_window], 1).reshape(GROUP * PACK, 128)
        total = total + (rows if r == 0 else pltpu.roll(rows, r * HD, 1))
    out_ref[...] = total.astype(bf16).reshape(GROUP, PACK, 128)


def attend_back_kernel(block, masks, head_ref, scale_ref, x_ref, grad_ref, *refs):
    mask_refs = refs[:3] if masks else None
    out_ref = refs[-1]
    lane = iota((CELLS, 128), 1)
    low = iota((HD, CELLS), 0)
    zeros = jnp.zeros((HD, CELLS), f32)
    scale_row = jnp.exp(jnp.full((1, 128), scale_ref[block, head_ref[0]], f32))
    unscale_row = 1.0 / scale_row
    packed = grad_ref[...].astype(f32).reshape(GROUP * PACK, 128)
    rolled = [packed if r == 0 else pltpu.roll(packed, 128 - r * HD, 1) for r in range(ROWS_DEV)]
    rolled = [part.reshape(GROUP, 1, 2, WIN, 128) for part in rolled]
    grads = jnp.concatenate(rolled, 1)
    factors = to_windows(unpack_factors(x_ref))
    results = [None, None]

    def attend_back(w, cells):
        cells = tagged(cells, w, mask_refs)
        turned = cells.T
        query_t = (jnp.concatenate([turned[:HD], turned[96:]], 0) if masks else turned[:HD]).astype(bf16)
        key_t = turned[HD : 2 * HD].astype(bf16)
        value_t = turned[2 * HD : 3 * HD]
        grad_t = grads[:, :, w].reshape(CELLS, 128).T[:HD]
        key = with_tags(cells, HD, True) if masks else cells[:, HD : 2 * HD].astype(bf16)
        yield
        scores = dot(key, query_t)
        yield
        weights = jnp.exp(scores).astype(bf16)
        yield
        summed = dot(jnp.concatenate([value_t, jnp.where(low == 0, 1.0, 0.0)], 0).astype(bf16), weights)
        yield
        inverse = 1.0 / summed[HD : HD + 1]
        grad_t = (grad_t * inverse).astype(bf16).astype(f32)
        row_high, row_low = split_two(jnp.sum(grad_t * summed[:HD], 0, keepdims=True) * inverse)
        rows = jnp.where(low == 0, -row_high, jnp.where(low == 1, -row_low, 0.0))
        grad_ext = jnp.concatenate([grad_t, rows], 0).astype(bf16)
        yield
        ones = jnp.where(lane < HD + 2, 1.0, 0.0)
        value_ext = jnp.where(lane < HD, pltpu.roll(cells, 64, 1), ones)[:, :64].astype(bf16)
        yield
        grad_scores = (weights.astype(f32) * dot(value_ext, grad_ext)).astype(bf16)
        yield
        query_at = jnp.where((lane >= HD) & (lane < 2 * HD), pltpu.roll(cells, HD, 1), 0.0).astype(bf16)
        grad_at = jnp.concatenate([zeros, zeros, grad_t, zeros], 0).T.astype(bf16)
        yield
        grad_kv = dot(grad_scores, query_at) + dot(weights, grad_at)
        yield
        grad_q = dot(key_t, grad_scores)
        yield
        grad_q = jnp.concatenate([grad_q, zeros, zeros, zeros], 0).T
        yield
        total = jnp.where(lane < HD, grad_q * scale_row, grad_kv)
        unit = jnp.where(lane < HD, cells * unscale_row, jnp.where(lane < 2 * HD, cells, 0.0))
        q_factor, k_factor = factors[w][:, 96:97], factors[w][:, 97:98]
        factor = jnp.where(lane < HD, q_factor, jnp.where(lane < 2 * HD, k_factor, 1.0))
        results[w] = factor * (total - unit * head_sums(unit * total))

    together(attend_back(w, cells) for w, cells in enumerate(to_windows(unpack_cells(x_ref))))
    out_ref[...] = pack_cells(from_windows(results)).astype(bf16)


def first_kernel(tokens_ref, w_ref, scale_ref, out_ref):
    send_projected(tokens_ref[...], w_ref[...], scale_ref, 0, out_ref)


def middle_kernel(packed_ref, scale_ref, gain_ref, bias_ref, tokens_ref, w_proj_ref, w_ref, out_ref, rolled_ref):
    attended = unpack_heads(packed_ref)
    y_hat, _ = normalized(attended, w_proj_ref[...])
    out = (tokens_ref[...].astype(f32) + y_hat * gain_ref[0:1] + bias_ref[0:1]).astype(bf16).astype(f32)
    rolled = roll_tokens(out, -SHIFT).astype(bf16)
    rolled_ref[...] = rolled
    send_projected(rolled, w_ref[...], scale_ref, 1, out_ref)


def turn_kernel(core_ref, packed_ref, gain_ref, grad_ref, w_proj_ref, out_ref, kept_ref, given_ref, gains_ref):
    attended = unpack_heads(packed_ref)
    grad = roll_tokens(grad_ref[...].astype(f32), -SHIFT)
    grad_y, grad_att, gains = finish_back(attended, w_proj_ref[...], gain_ref[1:2], grad)
    pack_heads(grad_att, out_ref)
    kept, given = halves(attended, core_ref[0])
    kept_ref[...] = dot_0(grad_y, kept).astype(bf16)
    given_ref[...] = dot_0(grad_y, given).astype(bf16)
    gains_ref[...] = gains


def gather_qkv(qkv_ref):
    parts = [qkv_ref[h].astype(f32) for h in range(HEADS)]
    top = [lane_slice(parts[h][:SHORT], kind * HD) for kind in range(3) for h in range(HEADS)]
    tail = [lane_slice(parts[h][kind * 32 : kind * 32 + 32], 96) for kind in range(3) for h in range(HEADS)]
    return jnp.concatenate([jnp.concatenate(top, 1), jnp.concatenate(tail, 1)], 0).astype(bf16)


def halves(array, core):
    half = array.shape[1] // 2
    left, right = array[:, :half].astype(f32), array[:, half:].astype(f32)
    return jnp.where(core == 0, left, right).astype(bf16), jnp.where(core == 0, right, left).astype(bf16)


def back_kernel(
    core_ref,
    qkv_ref,
    packed_ref,
    gain_ref,
    w_ref,
    w_proj_ref,
    grad_ref,
    proj1_kept_ref,
    proj1_given_ref,
    tokens_ref,
    out_ref,
    gains_ref,
    grad0_ref,
    kept_ref,
    given_ref,
):
    d_qkv = gather_qkv(qkv_ref)
    from_qkv = roll_tokens(dot_t(d_qkv, w_ref[...]), SHIFT)
    grad = (grad_ref[...].astype(f32) + from_qkv).astype(bf16)
    grad0_ref[...] = grad
    attended = unpack_heads(packed_ref)
    grad_y, grad_att, gains = finish_back(attended, w_proj_ref[...], gain_ref[0:1], grad.astype(f32))
    sides = zip(halves(d_qkv, core_ref[0]), (proj1_kept_ref, proj1_given_ref), halves(attended, core_ref[0]))
    kept, given = [
        jnp.concatenate(
            [dot_0(tokens_ref[...], part).astype(bf16), proj1_ref[...], dot_0(grad_y, att).astype(bf16)], 1
        )
        for part, proj1_ref, att in sides
    ]
    kept_ref[...] = kept
    given_ref[...] = given
    pack_heads(grad_att, out_ref)
    gains_ref[...] = gains


def image_kernel(qkv_ref, w_ref, grad_ref, out_ref):
    out_ref[...] = (grad_ref[...].astype(f32) + dot_t(gather_qkv(qkv_ref), w_ref[...])).astype(bf16)


def last_kernel(core_ref, qkv_ref, tokens_ref, kept_ref, given_ref):
    kept, given = halves(gather_qkv(qkv_ref), core_ref[0])
    given_ref[...] = dot_0(tokens_ref[...], given).astype(bf16)
    kept_ref[...] = dot_0(tokens_ref[...], kept).astype(bf16)


def parts_kernel(late_ref, got_late_ref, got_ref, gains0_ref, gains1_ref, kept_ref, parts_ref):
    pieces = []
    for ref in (gains0_ref, gains1_ref):
        for row in (0, 1):
            pieces += split_two(ref[row : row + 1])
    gains = jnp.concatenate(pieces + [jnp.zeros((16 - len(pieces), C), f32)], 0)
    depth = C // 8
    for ring in range(8):
        block = gains[:, ring // 2 * 128 : ring // 2 * 128 + 128]
        block = pltpu.roll(block, depth, 1) if ring % 2 else block
        parts_ref[ring, TILES * depth :] = block.astype(bf16)
    late = late_ref[...].astype(f32) + got_late_ref[...].astype(f32)
    early = kept_ref[...].astype(f32) + got_ref[...].astype(f32)
    tile = 0
    for part in (late, early):
        for at in range(0, part.shape[1], 128):
            block = part[:, at : at + 128].astype(bf16).reshape(8, depth, 128)
            parts_ref[:, tile * depth : (tile + 1) * depth, :] = block
            tile += 1


def first_sum_kernel(parts_ref, out_ref):
    total = jnp.sum(parts_ref[...].astype(f32), 0)
    gains = total[TILES * C // 8 :]
    total = total[: TILES * C // 8].reshape(TILES, 8, 8, 128)
    for place in range(8):
        rolled = pltpu.roll(gains, 128 - 8 * place, 1) if place else gains
        out_ref[place] = jnp.concatenate([total[:, place].reshape(TILES * 8, 128), rolled], 0).astype(bf16)


def second_sum_kernel(parts_ref, out_ref):
    out_ref[...] = jnp.sum(parts_ref[...].astype(f32), 0)


def add_kernel(one_ref, two_ref, out_ref):
    out_ref[...] = one_ref[...] + two_ref[...]


def final_kernel(core_ref, own_ref, other_ref, qkv_ref, proj_ref, gain_ref, bias_ref):
    own = own_ref[: TILES * 8].reshape(TILES, 8, 128)
    other = other_ref[: TILES * 8].reshape(TILES, 8, 128)
    first = core_ref[0] == 0
    left, right = jnp.where(first, own, other), jnp.where(first, other, own)
    for block, tiles in ((0, (0, 1, 2)), (1, (3, 4, 5))):
        qkv_ref[block] = jnp.concatenate([side[i] for side in (left, right) for i in tiles], 1)
    proj_ref[1] = jnp.concatenate([left[6], right[6]], 1)
    proj_ref[0] = jnp.concatenate([left[7], right[7]], 1)
    gains = (own_ref[TILES * 8 :] + other_ref[TILES * 8 :])[:, :8]
    gain_ref[...] = jnp.concatenate([gains[0:1] + gains[1:2], gains[4:5] + gains[5:6]], 0)
    bias_ref[...] = jnp.concatenate([gains[2:3] + gains[3:4], gains[6:7] + gains[7:8]], 0)


def pieces_of(shape):
    return 4 if shape[0] % 64 == 0 and shape[0] * shape[1] >= 2**18 else 1


def copies_of(source, target, sems, first):
    count = pieces_of(target.shape)
    rows = target.shape[0] // count
    if count == 1:
        return [pltpu.make_async_copy(source, target, sems.at[first])]
    return [
        pltpu.make_async_copy(
            source.at[pl.ds(i * rows, rows)], target.at[pl.ds(i * rows, rows)], sems.at[first + i]
        )
        for i in range(count)
    ]


class Fetched:
    def __init__(self, source, ref, sems, first):
        self.ref, self.copies = ref, copies_of(source, ref, sems, first)
        for copy in self.copies:
            copy.start()
        self.waited = False

    def __getitem__(self, at):
        if not self.waited:
            for copy in self.copies:
                copy.wait()
            self.waited = True
        return self.ref[at]


class Stored:
    def __init__(self, ref, target, sems, first):
        self.ref, self.copies = ref, copies_of(ref, target, sems, first)

    def __setitem__(self, at, value):
        self.ref[at] = value
        for copy in self.copies:
            copy.start()


def call(kernel, outs, scalars, arrays, masks=(), fetched=(), stored=()):
    arrays = [item if isinstance(item, tuple) else (item, None) for item in arrays]
    fetched = [item if isinstance(item, tuple) else (item, None) for item in fetched]
    counts = [len(scalars), len(arrays), len(fetched), len(masks), len(outs), len(stored), len(fetched), len(stored)]

    def wrapped(*refs):
        parts, at = [], 0
        for count in counts:
            parts.append(refs[at : at + count])
            at += count
        scalar_refs, array_refs, sources, mask_refs, out_refs, targets, filled, sent = parts
        sems = refs[-1]
        near = [ref if block is None else ref.at[block] for ref, (_, block) in zip(array_refs, arrays)]
        far, results, first = [], [], 0
        for i, (_, block) in enumerate(fetched):
            source = sources[i] if block is None else sources[i].at[block]
            far.append(Fetched(source, filled[i], sems, first))
            first += pieces_of(filled[i].shape)
        for i in range(len(stored)):
            results.append(Stored(sent[i], targets[i], sems, first))
            first += pieces_of(sent[i].shape)
        kernel(*scalar_refs, *near, *far, *mask_refs, *out_refs, *results)
        for result in results:
            for copy in result.copies:
                copy.wait()

    smem = pl.BlockSpec(memory_space=pltpu.SMEM)
    vmem = pl.BlockSpec(memory_space=pltpu.VMEM)
    hbm = pl.BlockSpec(memory_space=pltpu.HBM)
    scratch = [
        pltpu.VMEM(array.shape if block is None else array.shape[1:], array.dtype) for array, block in fetched
    ]
    scratch += [pltpu.VMEM(*out) for out in stored]
    if scratch:
        scratch.append(pltpu.SemaphoreType.DMA((sum(pieces_of(buffer.shape) for buffer in scratch),)))
    return pl.pallas_call(
        wrapped,
        out_shape=[jax.ShapeDtypeStruct(*out) for out in outs] + [pltpu.HBM(*out) for out in stored],
        in_specs=[smem] * len(scalars)
        + [vmem] * len(arrays)
        + [hbm] * len(fetched)
        + [smem, smem, vmem][: len(masks)],
        out_specs=[vmem] * len(outs) + [hbm] * len(stored),
        scratch_shapes=scratch,
        compiler_params=pltpu.CompilerParams(vmem_limit_bytes=VMEM_LIMIT),
    )(
        *scalars,
        *(array for array, _ in arrays),
        *(pltpu.with_memory_space_constraint(array, pltpu.HBM) for array, _ in fetched),
        *masks,
    )


def body(image, out_grad, w_qkv, w_proj, norm_gain, norm_bias, logit_scale, row_band, col_band):
    position = lax.axis_index("rows")
    half = GROUP // 2
    rings = range(DEVS // GROUP)
    aligned = [[GROUP * g + i for i in range(GROUP)] for g in rings]
    across = [[GROUP * g + i for g in rings] for i in range(GROUP)]
    moved = [[(GROUP * g + half + i) % DEVS for i in range(GROUP)] for g in rings]
    moved_position = (position + DEVS - half) % DEVS
    head0 = (position % GROUP).reshape(1)
    head1 = (moved_position % GROUP).reshape(1)
    first_row = (moved_position // GROUP * WIN).reshape(1)
    core = (lax.axis_index("dp") % 2).reshape(1)
    image, head0, head1, first_row, core = lax.optimization_barrier((image, head0, head1, first_row, core))
    masks = (first_row, row_band, col_band.reshape(1, -1))

    def exchange(array, groups):
        return lax.all_to_all(array, "rows", 0, 0, axis_index_groups=groups, tiled=True)

    tokens0 = image.reshape(TOK, C)
    grad_out = out_grad.reshape(TOK, C)
    short = ((GROUP, SHORT, 128), bf16)
    narrow = ((GROUP, PACK, 128), bf16)
    cells = ((TOK, C), bf16)
    proj = ((C, HH // 2), bf16)
    gains = ((8, C), f32)
    half_early = ((C, EARLY // 2), bf16)
    half_late = ((C, LATE // 2), bf16)

    def swap(array, apart):
        return lax.ppermute(array, "dp", [(i, i ^ apart) for i in range(4)])

    (x0,) = call(first_kernel, [short], (), (), fetched=(tokens0, (w_qkv, 0), logit_scale))
    x0 = exchange(x0, aligned)
    (a0,) = call(functools.partial(attend_kernel, False), [narrow], (), (x0,))
    a0 = exchange(a0, aligned)
    x1, tokens1 = call(
        middle_kernel,
        [short],
        (),
        (a0, logit_scale, norm_gain, norm_bias, tokens0, (w_proj, 0), (w_qkv, 1)),
        stored=[cells],
    )
    x1 = exchange(x1, moved)
    (a1,) = call(functools.partial(attend_kernel, True), [narrow], (), (x1,), masks)
    a1 = exchange(a1, moved)
    d1, proj1_kept, proj1_given, gains1 = call(
        turn_kernel,
        [narrow, proj, proj, gains],
        (core,),
        (a1, norm_gain, grad_out, (w_proj, 1)),
    )
    d1 = exchange(d1, moved)
    (qkv1,) = call(
        functools.partial(attend_back_kernel, 1, True), [short], (head1, logit_scale), (x1, d1), masks
    )
    qkv1 = exchange(qkv1, moved)
    d0, gains0, grad0, kept, given = call(
        back_kernel,
        [narrow, gains],
        (core,),
        (qkv1, a0, norm_gain, (w_qkv, 1), (w_proj, 0), grad_out, proj1_kept, proj1_given, tokens1),
        stored=[cells, half_early, half_early],
    )
    d0 = exchange(d0, aligned)
    (qkv0,) = call(functools.partial(attend_back_kernel, 0, False), [short], (head0, logit_scale), (x0, d0))
    qkv0 = exchange(qkv0, aligned)
    qkv0, given = lax.optimization_barrier((qkv0, given))
    got = swap(given, 1)
    late, given_late = call(last_kernel, [half_late, half_late], (core,), (qkv0, tokens0))
    got_late = swap(given_late, 1)
    (parts,) = call(
        parts_kernel,
        [((8, SENT, 128), bf16)],
        (),
        (late, got_late, got, gains0, gains1, kept),
    )
    parts = exchange(parts, across)
    (parts,) = call(first_sum_kernel, [((8, SHARE, 128), bf16)], (), (parts,))
    parts = exchange(parts, aligned)
    (share,) = call(second_sum_kernel, [((SHARE, 128), f32)], (), (parts,))
    (share,) = call(add_kernel, [((SHARE, 128), f32)], (), (share, swap(share, 2)))
    other = swap(share, 1)
    qkv0, _ = lax.optimization_barrier((qkv0, share))
    (grad_image,) = call(image_kernel, [cells], (), (qkv0, (w_qkv, 0), grad0))
    small = ((2, 8), f32)
    grad_qkv, grad_proj, grad_gain, grad_bias = call(
        final_kernel,
        [((2, 8, 3 * HH), f32), ((2, 8, HH), f32), small, small],
        (core,),
        (share, other),
    )
    return (
        grad_image.reshape(image.shape),
        grad_qkv,
        grad_proj.transpose(0, 2, 1),
        grad_gain,
        grad_bias,
    )


def solution(mesh):
    placed = (P("dp", "rows", None, None), P("dp", "rows", None, None)) + (P(),) * 7
    return jax.shard_map(
        body,
        mesh=mesh,
        in_specs=placed,
        out_specs=(
            P("dp", "rows", None, None),
            P(None, "rows", None),
            P(None, None, "rows"),
            P(None, "rows"),
            P(None, "rows"),
        ),
        check_vma=False,
    )
```

```python
import functools

import jax
import jax.numpy as jnp
from jax import lax
from jax.experimental import pallas as pl
from jax.experimental.pallas import tpu as pltpu
from jax.sharding import PartitionSpec as P

C = 512
HEADS = 8
HD = 32
WIN = 24
HH = 256
SHIFT = 12
GROUP = 8
TOK = 144
CELLS = WIN * WIN
ROWS_DEV = 3
PACK = 48
DEVS = 64
ORDER = (0, 2, 4, 6, 1, 3, 5, 7)
MOVED = (0, 2, 4, 6, 7, 5, 3, 1)
ACROSS = (7, 6, 5, 4, 3, 2, 1, 0)
VMEM_LIMIT = 24 * 2**20
EARLY = 3 * HH + 2 * HH
SHORT = 112
LATE = 3 * HH
TILES = (LATE // 2 + EARLY // 2) // 128
SENT = TILES * C // 8 + 16
SHARE = TILES * 8 + 16

norm_eps = 1e-05
f32 = jnp.float32
bf16 = jnp.bfloat16


def dot(a, b):
    return jnp.dot(a, b, preferred_element_type=f32)


def dot_t(a, b):
    return lax.dot_general(a, b, (((1,), (1,)), ((), ())), preferred_element_type=f32)


def dot_0(a, b):
    return lax.dot_general(a, b, (((0,), (0,)), ((), ())), preferred_element_type=f32)


def iota(shape, axis):
    return lax.broadcasted_iota(jnp.int32, shape, axis)


def head_sums(x):
    width = x.shape[1]
    ones = (iota((width, width), 0) // HD == iota((width, width), 1) // HD).astype(f32).astype(bf16)
    high = x.astype(bf16)
    low = (x - high.astype(f32)).astype(bf16)
    return dot(high, ones) + dot(low, ones)


def split_two(x):
    high = x.astype(bf16).astype(f32)
    return high, x - high


def lane_slice(x, at):
    return x[:, at : at + HD]


def send_projected(tokens, weight, scale_ref, block, out_ref):
    projected = dot(tokens, weight)
    query, key, value = projected[:, :HH], projected[:, HH : 2 * HH], projected[:, 2 * HH :]
    lane = iota((1, HH), 1)
    scale = jnp.zeros((1, HH), f32)
    scales = scale_ref[...][block : block + 1]
    for h in range(HEADS):
        scale = jnp.where(lane // HD == h, scales[:, h : h + 1], scale)
    q_factor = lax.rsqrt(1.0 + head_sums(query * query))
    k_factor = lax.rsqrt(1.0 + head_sums(key * key))
    q_hat = query * q_factor * jnp.exp(scale)
    k_hat = key * k_factor
    slot = iota((16, HH), 1) % HD
    factors = jnp.zeros((16, HH), f32)
    for i in range(TOK // 16):
        rows = slice(16 * i, 16 * i + 16)
        factors = jnp.where(slot == 2 * i, q_factor[rows], jnp.where(slot == 2 * i + 1, k_factor[rows], factors))
    for h in range(HEADS):
        parts = [lane_slice(part, h * HD) for part in (q_hat, k_hat, value)]
        tail = jnp.concatenate([part[SHORT:] for part in parts] + [lane_slice(factors, h * HD)], 0)
        out_ref[h] = jnp.concatenate([part[:SHORT] for part in parts] + [tail], 1).astype(bf16)


def unpack_cells(x_ref):
    x = x_ref[...].astype(f32)
    lane = iota((GROUP * 32, 128), 1)
    rolled = [
        pltpu.roll(x[:, kind * 32 : kind * 32 + 32].reshape(GROUP * 32, 128), 32 + 32 * kind, 1)
        for kind in range(3)
    ]
    tail = jnp.where(lane < HD, rolled[0], jnp.where(lane < 2 * HD, rolled[1], rolled[2]))
    return jnp.concatenate([x, tail.reshape(GROUP, 32, 128)], 1)


def unpack_factors(x_ref):
    rows = x_ref[...].astype(f32)[:, SHORT - 16 :].reshape(GROUP * 16, 128)
    rolled = [pltpu.roll(rows, 128 - 2 * i, 1) if i else rows for i in range(TOK // 16)]
    return jnp.concatenate([part.reshape(GROUP, 16, 128) for part in rolled], 1)


def unpack_heads(packed_ref):
    packed = [packed_ref[h].astype(f32) for h in range(HEADS)]
    rows = [
        jnp.concatenate([lane_slice(packed[h], r * HD) for h in range(HEADS)], 1)
        for r in range(ROWS_DEV)
    ]
    return jnp.concatenate(rows, 0).astype(bf16)


def pack_heads(array, out_ref):
    zeros = jnp.zeros((PACK, HD), f32)
    for h in range(HEADS):
        parts = [lane_slice(array[r * PACK : (r + 1) * PACK], h * HD) for r in range(ROWS_DEV)]
        out_ref[h] = jnp.concatenate(parts + [zeros], 1).astype(bf16)


def to_windows(array):
    split = array.reshape(GROUP, ROWS_DEV, 2, WIN, array.shape[-1])
    return [split[:, :, w].reshape(CELLS, array.shape[-1]) for w in range(2)]


def from_windows(pair):
    depth = pair[0].shape[-1]
    parts = [part.reshape(GROUP, ROWS_DEV, 1, WIN, depth) for part in pair]
    return jnp.concatenate(parts, 2).reshape(GROUP, TOK, depth)


def pack_cells(cells):
    tail = cells[:, SHORT:].reshape(GROUP * 32, 128)
    moved = [pltpu.roll(tail, 96 - 32 * kind, 1).reshape(GROUP, 32, 128) for kind in range(3)]
    moved = jnp.concatenate(moved + [jnp.zeros((GROUP, SHORT - 96, 128), f32)], 1)
    lane = iota(moved.shape, 2)
    return jnp.where(lane < 96, cells[:, :SHORT], moved)


def roll_tokens(array, by):
    by = by % TOK
    return jnp.concatenate([array[TOK - by :], array[: TOK - by]], 0)


def normalized(attended, weight):
    outputs = dot(attended, weight)
    centered = outputs - jnp.mean(outputs, -1, keepdims=True)
    inverse = lax.rsqrt(jnp.mean(centered * centered, -1, keepdims=True) + norm_eps)
    return centered * inverse, inverse


def finish_back(attended, weight, gain_row, grad_out):
    y_hat, inverse = normalized(attended, weight)
    grad_gain = jnp.sum(grad_out * y_hat, 0, keepdims=True)
    grad_bias = jnp.sum(grad_out, 0, keepdims=True)
    scaled = grad_out * gain_row
    grad_y = inverse * (
        scaled
        - jnp.mean(scaled, -1, keepdims=True)
        - y_hat * jnp.mean(scaled * y_hat, -1, keepdims=True)
    )
    grad_y = grad_y.astype(bf16)
    gains = jnp.concatenate([grad_gain, grad_bias, jnp.zeros((6, C), f32)], 0)
    return grad_y, dot_t(grad_y, weight), gains


def tags_of(window, first_row_ref, row_ref, col_ref):
    lane = iota((WIN, 128), 1)
    place = iota((WIN, 1), 0)
    column = place + window * WIN
    col_label = jnp.zeros((WIN, 1), jnp.int32)
    for label in (1, 2):
        cut = jnp.sum((col_ref[...] < label).astype(jnp.int32), 1, keepdims=True)
        col_label = col_label + (column >= cut).astype(jnp.int32)
    blocks = []
    for source in MOVED:
        rows = [row_ref[first_row_ref[0] + source * ROWS_DEV + r] for r in range(ROWS_DEV)]
        for r in range(ROWS_DEV):
            row_label = rows[r]
            if window == 1:
                row_label = jnp.where(column >= 36, rows[(r + 1) % ROWS_DEV], rows[r])
            blocks.append(jnp.where(lane == col_label + 3 * row_label + 96, 10.0, 0.0))
    return jnp.concatenate(blocks, 0)


def tagged(cells, window, mask_refs):
    if mask_refs is None:
        return cells
    return jnp.where(iota(cells.shape, 1) < 96, cells, tags_of(window, *mask_refs))


def with_tags(cells, at, key):
    lane = iota(cells.shape, 1)
    own = cells if at == 0 else pltpu.roll(cells, 128 - at, 1)
    tags = pltpu.roll(cells, 64, 1)
    if key:
        tags = jnp.where(lane < HD + 9, tags - 10.0, tags)
    return jnp.where(lane < HD, own, tags)[:, :64].astype(bf16)


def together(steps):
    steps = list(steps)
    while steps:
        steps = [step for step in steps if next(step, 0) is None]


def attend_kernel(masks, x_ref, *refs):
    mask_refs = refs[:3] if masks else None
    out_ref = refs[-1]
    lane = iota((CELLS, 128), 1)
    per_window = [None, None]

    def attend(w, cells):
        cells = tagged(cells, w, mask_refs)
        query = with_tags(cells, 0, False) if masks else cells[:, :HD].astype(bf16)
        key = with_tags(cells, HD, True) if masks else cells[:, HD : 2 * HD].astype(bf16)
        value = jnp.where(lane < HD, pltpu.roll(cells, 64, 1), jnp.where(lane == HD, 1.0, 0.0)).astype(bf16)
        yield
        scores = dot_t(query, key)
        yield
        weights = jnp.exp(scores).astype(bf16)
        yield
        summed = dot(weights, value)
        yield
        attended = jnp.where(lane < HD, summed * (1.0 / summed[:, HD : HD + 1]), 0.0)
        per_window[w] = attended.reshape(GROUP, ROWS_DEV, WIN, 128)

    together(attend(w, cells) for w, cells in enumerate(to_windows(unpack_cells(x_ref))))
    total = 0.0
    for r in range(ROWS_DEV):
        rows = jnp.concatenate([part[:, r] for part in per_window], 1).reshape(GROUP * PACK, 128)
        total = total + (rows if r == 0 else pltpu.roll(rows, r * HD, 1))
    out_ref[...] = total.astype(bf16).reshape(GROUP, PACK, 128)


def attend_back_kernel(block, masks, head_ref, scale_ref, x_ref, grad_ref, *refs):
    mask_refs = refs[:3] if masks else None
    out_ref = refs[-1]
    lane = iota((CELLS, 128), 1)
    low = iota((HD, CELLS), 0)
    zeros = jnp.zeros((HD, CELLS), f32)
    scale_row = jnp.exp(jnp.full((1, 128), scale_ref[block, head_ref[0]], f32))
    unscale_row = 1.0 / scale_row
    packed = grad_ref[...].astype(f32).reshape(GROUP * PACK, 128)
    rolled = [packed if r == 0 else pltpu.roll(packed, 128 - r * HD, 1) for r in range(ROWS_DEV)]
    rolled = [part.reshape(GROUP, 1, 2, WIN, 128) for part in rolled]
    grads = jnp.concatenate(rolled, 1)
    factors = to_windows(unpack_factors(x_ref))
    results = [None, None]

    def attend_back(w, cells):
        cells = tagged(cells, w, mask_refs)
        turned = cells.T
        query_t = (jnp.concatenate([turned[:HD], turned[96:]], 0) if masks else turned[:HD]).astype(bf16)
        key_t = turned[HD : 2 * HD].astype(bf16)
        value_t = turned[2 * HD : 3 * HD]
        grad_t = grads[:, :, w].reshape(CELLS, 128).T[:HD]
        key = with_tags(cells, HD, True) if masks else cells[:, HD : 2 * HD].astype(bf16)
        yield
        scores = dot(key, query_t)
        yield
        weights = jnp.exp(scores).astype(bf16)
        yield
        summed = dot(jnp.concatenate([value_t, jnp.where(low == 0, 1.0, 0.0)], 0).astype(bf16), weights)
        yield
        inverse = 1.0 / summed[HD : HD + 1]
        grad_t = (grad_t * inverse).astype(bf16).astype(f32)
        row_high, row_low = split_two(jnp.sum(grad_t * summed[:HD], 0, keepdims=True) * inverse)
        rows = jnp.where(low == 0, -row_high, jnp.where(low == 1, -row_low, 0.0))
        grad_ext = jnp.concatenate([grad_t, rows], 0).astype(bf16)
        yield
        ones = jnp.where(lane < HD + 2, 1.0, 0.0)
        value_ext = jnp.where(lane < HD, pltpu.roll(cells, 64, 1), ones)[:, :64].astype(bf16)
        yield
        grad_scores = (weights.astype(f32) * dot(value_ext, grad_ext)).astype(bf16)
        yield
        query_at = jnp.where((lane >= HD) & (lane < 2 * HD), pltpu.roll(cells, HD, 1), 0.0).astype(bf16)
        grad_at = jnp.concatenate([zeros, zeros, grad_t, zeros], 0).T.astype(bf16)
        yield
        grad_kv = dot(grad_scores, query_at) + dot(weights, grad_at)
        yield
        grad_q = dot(key_t, grad_scores)
        yield
        grad_q = jnp.concatenate([grad_q, zeros, zeros, zeros], 0).T
        yield
        total = jnp.where(lane < HD, grad_q * scale_row, grad_kv)
        unit = jnp.where(lane < HD, cells * unscale_row, jnp.where(lane < 2 * HD, cells, 0.0))
        q_factor, k_factor = factors[w][:, 96:97], factors[w][:, 97:98]
        factor = jnp.where(lane < HD, q_factor, jnp.where(lane < 2 * HD, k_factor, 1.0))
        results[w] = factor * (total - unit * head_sums(unit * total))

    together(attend_back(w, cells) for w, cells in enumerate(to_windows(unpack_cells(x_ref))))
    out_ref[...] = pack_cells(from_windows(results)).astype(bf16)


def first_kernel(tokens_ref, w_ref, scale_ref, out_ref):
    send_projected(tokens_ref[...], w_ref[...], scale_ref, 0, out_ref)


def middle_kernel(packed_ref, scale_ref, gain_ref, bias_ref, tokens_ref, w_proj_ref, w_ref, out_ref, rolled_ref):
    attended = unpack_heads(packed_ref)
    y_hat, _ = normalized(attended, w_proj_ref[...])
    out = (tokens_ref[...].astype(f32) + y_hat * gain_ref[0:1] + bias_ref[0:1]).astype(bf16).astype(f32)
    rolled = roll_tokens(out, -SHIFT).astype(bf16)
    rolled_ref[...] = rolled
    send_projected(rolled, w_ref[...], scale_ref, 1, out_ref)


def turn_kernel(core_ref, packed_ref, gain_ref, grad_ref, w_proj_ref, out_ref, kept_ref, given_ref, gains_ref):
    attended = unpack_heads(packed_ref)
    grad = roll_tokens(grad_ref[...].astype(f32), -SHIFT)
    grad_y, grad_att, gains = finish_back(attended, w_proj_ref[...], gain_ref[1:2], grad)
    pack_heads(grad_att, out_ref)
    kept, given = halves(attended, core_ref[0])
    kept_ref[...] = dot_0(grad_y, kept).astype(bf16)
    given_ref[...] = dot_0(grad_y, given).astype(bf16)
    gains_ref[...] = gains


def gather_qkv(qkv_ref):
    parts = [qkv_ref[h].astype(f32) for h in range(HEADS)]
    top = [lane_slice(parts[h][:SHORT], kind * HD) for kind in range(3) for h in range(HEADS)]
    tail = [lane_slice(parts[h][kind * 32 : kind * 32 + 32], 96) for kind in range(3) for h in range(HEADS)]
    return jnp.concatenate([jnp.concatenate(top, 1), jnp.concatenate(tail, 1)], 0).astype(bf16)


def halves(array, core):
    half = array.shape[1] // 2
    left, right = array[:, :half].astype(f32), array[:, half:].astype(f32)
    return jnp.where(core == 0, left, right).astype(bf16), jnp.where(core == 0, right, left).astype(bf16)


def back_kernel(
    core_ref,
    qkv_ref,
    packed_ref,
    gain_ref,
    w_ref,
    w_proj_ref,
    grad_ref,
    proj1_kept_ref,
    proj1_given_ref,
    tokens_ref,
    out_ref,
    gains_ref,
    grad0_ref,
    kept_ref,
    given_ref,
):
    d_qkv = gather_qkv(qkv_ref)
    from_qkv = roll_tokens(dot_t(d_qkv, w_ref[...]), SHIFT)
    grad = (grad_ref[...].astype(f32) + from_qkv).astype(bf16)
    grad0_ref[...] = grad
    attended = unpack_heads(packed_ref)
    grad_y, grad_att, gains = finish_back(attended, w_proj_ref[...], gain_ref[0:1], grad.astype(f32))
    sides = zip(halves(d_qkv, core_ref[0]), (proj1_kept_ref, proj1_given_ref), halves(attended, core_ref[0]))
    kept, given = [
        jnp.concatenate(
            [dot_0(tokens_ref[...], part).astype(bf16), proj1_ref[...], dot_0(grad_y, att).astype(bf16)], 1
        )
        for part, proj1_ref, att in sides
    ]
    kept_ref[...] = kept
    given_ref[...] = given
    pack_heads(grad_att, out_ref)
    gains_ref[...] = gains


def image_kernel(qkv_ref, w_ref, grad_ref, out_ref):
    out_ref[...] = (grad_ref[...].astype(f32) + dot_t(gather_qkv(qkv_ref), w_ref[...])).astype(bf16)


def last_kernel(core_ref, qkv_ref, tokens_ref, kept_ref, given_ref):
    kept, given = halves(gather_qkv(qkv_ref), core_ref[0])
    given_ref[...] = dot_0(tokens_ref[...], given).astype(bf16)
    kept_ref[...] = dot_0(tokens_ref[...], kept).astype(bf16)


def parts_kernel(late_ref, got_late_ref, got_ref, gains0_ref, gains1_ref, kept_ref, parts_ref):
    pieces = []
    for ref in (gains0_ref, gains1_ref):
        for row in (0, 1):
            pieces += split_two(ref[row : row + 1])
    gains = jnp.concatenate(pieces + [jnp.zeros((16 - len(pieces), C), f32)], 0)
    depth = C // 8
    for ring in range(8):
        block = gains[:, ring // 2 * 128 : ring // 2 * 128 + 128]
        block = pltpu.roll(block, depth, 1) if ring % 2 else block
        parts_ref[ACROSS.index(ring), TILES * depth :] = block.astype(bf16)
    late = late_ref[...].astype(f32) + got_late_ref[...].astype(f32)
    early = kept_ref[...].astype(f32) + got_ref[...].astype(f32)
    tile = 0
    for part in (late, early):
        for at in range(0, part.shape[1], 128):
            block = part[:, at : at + 128].astype(bf16).reshape(8, depth, 128)
            parts_ref[:, tile * depth : (tile + 1) * depth, :] = jnp.stack([block[ring] for ring in ACROSS])
            tile += 1


def first_sum_kernel(parts_ref, out_ref):
    total = jnp.sum(parts_ref[...].astype(f32), 0)
    gains = total[TILES * C // 8 :]
    total = total[: TILES * C // 8].reshape(TILES, 8, 8, 128)
    for place in range(8):
        rolled = pltpu.roll(gains, 128 - 8 * place, 1) if place else gains
        block = jnp.concatenate([total[:, place].reshape(TILES * 8, 128), rolled], 0)
        out_ref[ORDER.index(place)] = block.astype(bf16)


def second_sum_kernel(parts_ref, out_ref):
    out_ref[...] = jnp.sum(parts_ref[...].astype(f32), 0)


def add_kernel(one_ref, two_ref, out_ref):
    out_ref[...] = one_ref[...] + two_ref[...]


def final_kernel(core_ref, own_ref, other_ref, qkv_ref, proj_ref, gain_ref, bias_ref):
    own = own_ref[: TILES * 8].reshape(TILES, 8, 128)
    other = other_ref[: TILES * 8].reshape(TILES, 8, 128)
    first = core_ref[0] == 0
    left, right = jnp.where(first, own, other), jnp.where(first, other, own)
    for block, tiles in ((0, (0, 1, 2)), (1, (3, 4, 5))):
        qkv_ref[block] = jnp.concatenate([side[i] for side in (left, right) for i in tiles], 1)
    proj_ref[1] = jnp.concatenate([left[6], right[6]], 1)
    proj_ref[0] = jnp.concatenate([left[7], right[7]], 1)
    gains = (own_ref[TILES * 8 :] + other_ref[TILES * 8 :])[:, :8]
    gain_ref[...] = jnp.concatenate([gains[0:1] + gains[1:2], gains[4:5] + gains[5:6]], 0)
    bias_ref[...] = jnp.concatenate([gains[2:3] + gains[3:4], gains[6:7] + gains[7:8]], 0)


def pieces_of(shape):
    return 4 if shape[0] % 64 == 0 and shape[0] * shape[1] >= 2**18 else 1


def copies_of(source, target, sems, first):
    count = pieces_of(target.shape)
    rows = target.shape[0] // count
    if count == 1:
        return [pltpu.make_async_copy(source, target, sems.at[first])]
    return [
        pltpu.make_async_copy(
            source.at[pl.ds(i * rows, rows)], target.at[pl.ds(i * rows, rows)], sems.at[first + i]
        )
        for i in range(count)
    ]


class Fetched:
    def __init__(self, source, ref, sems, first):
        self.ref, self.copies = ref, copies_of(source, ref, sems, first)
        for copy in self.copies:
            copy.start()
        self.waited = False

    def __getitem__(self, at):
        if not self.waited:
            for copy in self.copies:
                copy.wait()
            self.waited = True
        return self.ref[at]


class Stored:
    def __init__(self, ref, target, sems, first):
        self.ref, self.copies = ref, copies_of(ref, target, sems, first)

    def __setitem__(self, at, value):
        self.ref[at] = value
        for copy in self.copies:
            copy.start()


def call(kernel, outs, scalars, arrays, masks=(), fetched=(), stored=()):
    arrays = [item if isinstance(item, tuple) else (item, None) for item in arrays]
    fetched = [item if isinstance(item, tuple) else (item, None) for item in fetched]
    counts = [len(scalars), len(arrays), len(fetched), len(masks), len(outs), len(stored), len(fetched), len(stored)]

    def wrapped(*refs):
        parts, at = [], 0
        for count in counts:
            parts.append(refs[at : at + count])
            at += count
        scalar_refs, array_refs, sources, mask_refs, out_refs, targets, filled, sent = parts
        sems = refs[-1]
        near = [ref if block is None else ref.at[block] for ref, (_, block) in zip(array_refs, arrays)]
        far, results, first = [], [], 0
        for i, (_, block) in enumerate(fetched):
            source = sources[i] if block is None else sources[i].at[block]
            far.append(Fetched(source, filled[i], sems, first))
            first += pieces_of(filled[i].shape)
        for i in range(len(stored)):
            results.append(Stored(sent[i], targets[i], sems, first))
            first += pieces_of(sent[i].shape)
        kernel(*scalar_refs, *near, *far, *mask_refs, *out_refs, *results)
        for result in results:
            for copy in result.copies:
                copy.wait()

    smem = pl.BlockSpec(memory_space=pltpu.SMEM)
    vmem = pl.BlockSpec(memory_space=pltpu.VMEM)
    hbm = pl.BlockSpec(memory_space=pltpu.HBM)
    scratch = [
        pltpu.VMEM(array.shape if block is None else array.shape[1:], array.dtype) for array, block in fetched
    ]
    scratch += [pltpu.VMEM(*out) for out in stored]
    if scratch:
        scratch.append(pltpu.SemaphoreType.DMA((sum(pieces_of(buffer.shape) for buffer in scratch),)))
    return pl.pallas_call(
        wrapped,
        out_shape=[jax.ShapeDtypeStruct(*out) for out in outs] + [pltpu.HBM(*out) for out in stored],
        in_specs=[smem] * len(scalars)
        + [vmem] * len(arrays)
        + [hbm] * len(fetched)
        + [smem, smem, vmem][: len(masks)],
        out_specs=[vmem] * len(outs) + [hbm] * len(stored),
        scratch_shapes=scratch,
        compiler_params=pltpu.CompilerParams(vmem_limit_bytes=VMEM_LIMIT),
    )(
        *scalars,
        *(array for array, _ in arrays),
        *(pltpu.with_memory_space_constraint(array, pltpu.HBM) for array, _ in fetched),
        *masks,
    )


def body(image, out_grad, w_qkv, w_proj, norm_gain, norm_bias, logit_scale, row_band, col_band):
    position = lax.axis_index("rows")
    half = GROUP // 2
    rings = range(DEVS // GROUP)
    aligned = [[GROUP * g + i for i in ORDER] for g in rings]
    across = [[GROUP * g + i for g in ACROSS] for i in range(GROUP)]
    moved = [[(GROUP * g + half + i) % DEVS for i in MOVED] for g in rings]
    moved_position = (position + DEVS - half) % DEVS
    head0, head1 = jnp.zeros((1,), jnp.int32), jnp.zeros((1,), jnp.int32)
    for h in range(HEADS):
        head0 = head0 + h * (position % GROUP == ORDER[h])
        head1 = head1 + h * (moved_position % GROUP == MOVED[h])
    first_row = (moved_position // GROUP * WIN).reshape(1)
    core = (lax.axis_index("dp") % 2).reshape(1)
    image, head0, head1, first_row, core = lax.optimization_barrier((image, head0, head1, first_row, core))
    masks = (first_row, row_band, col_band.reshape(1, -1))

    def exchange(array, groups):
        return lax.all_to_all(array, "rows", 0, 0, axis_index_groups=groups, tiled=True)

    tokens0 = image.reshape(TOK, C)
    grad_out = out_grad.reshape(TOK, C)
    short = ((GROUP, SHORT, 128), bf16)
    narrow = ((GROUP, PACK, 128), bf16)
    cells = ((TOK, C), bf16)
    proj = ((C, HH // 2), bf16)
    gains = ((8, C), f32)
    half_early = ((C, EARLY // 2), bf16)
    half_late = ((C, LATE // 2), bf16)

    def swap(array, apart):
        return lax.ppermute(array, "dp", [(i, i ^ apart) for i in range(4)])

    (x0,) = call(first_kernel, [short], (), (), fetched=(tokens0, (w_qkv, 0), logit_scale))
    x0 = exchange(x0, aligned)
    (a0,) = call(functools.partial(attend_kernel, False), [narrow], (), (x0,))
    a0 = exchange(a0, aligned)
    x1, tokens1 = call(
        middle_kernel,
        [short],
        (),
        (a0, logit_scale, norm_gain, norm_bias, tokens0, (w_proj, 0), (w_qkv, 1)),
        stored=[cells],
    )
    x1 = exchange(x1, moved)
    (a1,) = call(functools.partial(attend_kernel, True), [narrow], (), (x1,), masks)
    a1 = exchange(a1, moved)
    d1, proj1_kept, proj1_given, gains1 = call(
        turn_kernel,
        [narrow, proj, proj, gains],
        (core,),
        (a1, norm_gain, grad_out, (w_proj, 1)),
    )
    d1 = exchange(d1, moved)
    (qkv1,) = call(
        functools.partial(attend_back_kernel, 1, True), [short], (head1, logit_scale), (x1, d1), masks
    )
    qkv1 = exchange(qkv1, moved)
    d0, gains0, grad0, kept, given = call(
        back_kernel,
        [narrow, gains],
        (core,),
        (qkv1, a0, norm_gain, (w_qkv, 1), (w_proj, 0), grad_out, proj1_kept, proj1_given, tokens1),
        stored=[cells, half_early, half_early],
    )
    d0 = exchange(d0, aligned)
    (qkv0,) = call(functools.partial(attend_back_kernel, 0, False), [short], (head0, logit_scale), (x0, d0))
    qkv0 = exchange(qkv0, aligned)
    qkv0, given = lax.optimization_barrier((qkv0, given))
    got = swap(given, 1)
    late, given_late = call(last_kernel, [half_late, half_late], (core,), (qkv0, tokens0))
    got_late = swap(given_late, 1)
    (parts,) = call(
        parts_kernel,
        [((8, SENT, 128), bf16)],
        (),
        (late, got_late, got, gains0, gains1, kept),
    )
    parts = exchange(parts, across)
    (parts,) = call(first_sum_kernel, [((8, SHARE, 128), bf16)], (), (parts,))
    parts = exchange(parts, aligned)
    (share,) = call(second_sum_kernel, [((SHARE, 128), f32)], (), (parts,))
    (share,) = call(add_kernel, [((SHARE, 128), f32)], (), (share, swap(share, 2)))
    other = swap(share, 1)
    qkv0, _ = lax.optimization_barrier((qkv0, share))
    (grad_image,) = call(image_kernel, [cells], (), (qkv0, (w_qkv, 0), grad0))
    small = ((2, 8), f32)
    grad_qkv, grad_proj, grad_gain, grad_bias = call(
        final_kernel,
        [((2, 8, 3 * HH), f32), ((2, 8, HH), f32), small, small],
        (core,),
        (share, other),
    )
    return (
        grad_image.reshape(image.shape),
        grad_qkv,
        grad_proj.transpose(0, 2, 1),
        grad_gain,
        grad_bias,
    )


def solution(mesh):
    placed = (P("dp", "rows", None, None), P("dp", "rows", None, None)) + (P(),) * 7
    return jax.shard_map(
        body,
        mesh=mesh,
        in_specs=placed,
        out_specs=(
            P("dp", "rows", None, None),
            P(None, "rows", None),
            P(None, None, "rows"),
            P(None, "rows"),
            P(None, "rows"),
        ),
        check_vma=False,
    )
```

```python
import functools

import jax
import jax.numpy as jnp
from jax import lax
from jax.experimental import pallas as pl
from jax.experimental.pallas import tpu as pltpu
from jax.sharding import PartitionSpec as P

C = 512
HEADS = 8
HD = 32
WIN = 24
HH = 256
SHIFT = 12
GROUP = 8
TOK = 144
CELLS = WIN * WIN
ROWS_DEV = 3
PACK = 40
RUNS = ((0, 40), (40, 80), (80, 112), (112, 144))
DEVS = 64
ORDER = (0, 2, 4, 6, 1, 3, 5, 7)
MOVED = (0, 2, 4, 6, 7, 5, 3, 1)
ACROSS = (7, 6, 5, 4, 3, 2, 1, 0)
VMEM_LIMIT = 24 * 2**20
EARLY = 3 * HH + 2 * HH
SHORT = 112
LATE = 3 * HH
TILES = (LATE // 2 + EARLY // 2) // 128
SENT = TILES * C // 8 + 16
SHARE = TILES * 8 + 16

norm_eps = 1e-05
f32 = jnp.float32
bf16 = jnp.bfloat16


def dot(a, b):
    return jnp.dot(a, b, preferred_element_type=f32)


def dot_t(a, b):
    return lax.dot_general(a, b, (((1,), (1,)), ((), ())), preferred_element_type=f32)


def dot_0(a, b):
    return lax.dot_general(a, b, (((0,), (0,)), ((), ())), preferred_element_type=f32)


def iota(shape, axis):
    return lax.broadcasted_iota(jnp.int32, shape, axis)


def head_sums(x):
    width = x.shape[1]
    ones = (iota((width, width), 0) // HD == iota((width, width), 1) // HD).astype(f32).astype(bf16)
    high = x.astype(bf16)
    low = (x - high.astype(f32)).astype(bf16)
    return dot(high, ones) + dot(low, ones)


def split_two(x):
    high = x.astype(bf16).astype(f32)
    return high, x - high


def lane_slice(x, at):
    return x[:, at : at + HD]


def send_projected(tokens, weight, scale_ref, block, out_ref):
    projected = dot(tokens, weight)
    query, key, value = projected[:, :HH], projected[:, HH : 2 * HH], projected[:, 2 * HH :]
    lane = iota((1, HH), 1)
    scale = jnp.zeros((1, HH), f32)
    scales = scale_ref[...][block : block + 1]
    for h in range(HEADS):
        scale = jnp.where(lane // HD == h, scales[:, h : h + 1], scale)
    q_factor = lax.rsqrt(1.0 + head_sums(query * query))
    k_factor = lax.rsqrt(1.0 + head_sums(key * key))
    q_hat = query * q_factor * jnp.exp(scale)
    k_hat = key * k_factor
    slot = iota((16, HH), 1) % HD
    factors = jnp.zeros((16, HH), f32)
    for i in range(TOK // 16):
        rows = slice(16 * i, 16 * i + 16)
        factors = jnp.where(slot == 2 * i, q_factor[rows], jnp.where(slot == 2 * i + 1, k_factor[rows], factors))
    for h in range(HEADS):
        parts = [lane_slice(part, h * HD) for part in (q_hat, k_hat, value)]
        tail = jnp.concatenate([part[SHORT:] for part in parts] + [lane_slice(factors, h * HD)], 0)
        out_ref[h] = jnp.concatenate([part[:SHORT] for part in parts] + [tail], 1).astype(bf16)


def unpack_cells(x_ref):
    x = x_ref[...].astype(f32)
    lane = iota((GROUP * 32, 128), 1)
    rolled = [
        pltpu.roll(x[:, kind * 32 : kind * 32 + 32].reshape(GROUP * 32, 128), 32 + 32 * kind, 1)
        for kind in range(3)
    ]
    tail = jnp.where(lane < HD, rolled[0], jnp.where(lane < 2 * HD, rolled[1], rolled[2]))
    return jnp.concatenate([x, tail.reshape(GROUP, 32, 128)], 1)


def unpack_factors(x_ref):
    rows = x_ref[...].astype(f32)[:, SHORT - 16 :].reshape(GROUP * 16, 128)
    rolled = [pltpu.roll(rows, 128 - 2 * i, 1) if i else rows for i in range(TOK // 16)]
    return jnp.concatenate([part.reshape(GROUP, 16, 128) for part in rolled], 1)


def unpack_heads(packed_ref):
    packed = packed_ref[...].astype(f32)
    rows = [
        jnp.concatenate([lane_slice(packed[h, : stop - start], run * HD) for h in range(HEADS)], 1)
        for run, (start, stop) in enumerate(RUNS)
    ]
    return jnp.concatenate(rows, 0).astype(bf16)


def padded(run):
    missing = PACK - run.shape[-2]
    if not missing:
        return run
    return jnp.concatenate([run, jnp.zeros((*run.shape[:-2], missing, run.shape[-1]), f32)], -2)


def pack_heads(array, out_ref):
    heads = []
    for h in range(HEADS):
        parts = [padded(lane_slice(array[start:stop], h * HD)) for start, stop in RUNS]
        heads.append(jnp.concatenate(parts, 1))
    out_ref[...] = jnp.stack(heads).astype(bf16)


def to_windows(array):
    split = array.reshape(GROUP, ROWS_DEV, 2, WIN, array.shape[-1])
    return [split[:, :, w].reshape(CELLS, array.shape[-1]) for w in range(2)]


def from_windows(pair):
    depth = pair[0].shape[-1]
    parts = [part.reshape(GROUP, ROWS_DEV, 1, WIN, depth) for part in pair]
    return jnp.concatenate(parts, 2).reshape(GROUP, TOK, depth)


def pack_cells(cells):
    tail = cells[:, SHORT:].reshape(GROUP * 32, 128)
    moved = [pltpu.roll(tail, 96 - 32 * kind, 1).reshape(GROUP, 32, 128) for kind in range(3)]
    moved = jnp.concatenate(moved + [jnp.zeros((GROUP, SHORT - 96, 128), f32)], 1)
    lane = iota(moved.shape, 2)
    return jnp.where(lane < 96, cells[:, :SHORT], moved)


def roll_tokens(array, by):
    by = by % TOK
    return jnp.concatenate([array[TOK - by :], array[: TOK - by]], 0)


def normalized(attended, weight):
    outputs = dot(attended, weight)
    centered = outputs - jnp.mean(outputs, -1, keepdims=True)
    inverse = lax.rsqrt(jnp.mean(centered * centered, -1, keepdims=True) + norm_eps)
    return centered * inverse, inverse


def finish_back(attended, weight, gain_row, grad_out):
    y_hat, inverse = normalized(attended, weight)
    grad_gain = jnp.sum(grad_out * y_hat, 0, keepdims=True)
    grad_bias = jnp.sum(grad_out, 0, keepdims=True)
    scaled = grad_out * gain_row
    grad_y = inverse * (
        scaled
        - jnp.mean(scaled, -1, keepdims=True)
        - y_hat * jnp.mean(scaled * y_hat, -1, keepdims=True)
    )
    grad_y = grad_y.astype(bf16)
    gains = jnp.concatenate([grad_gain, grad_bias, jnp.zeros((6, C), f32)], 0)
    return grad_y, dot_t(grad_y, weight), gains


def tags_of(window, first_row_ref, row_ref, col_ref):
    lane = iota((WIN, 128), 1)
    place = iota((WIN, 1), 0)
    column = place + window * WIN
    col_label = jnp.zeros((WIN, 1), jnp.int32)
    for label in (1, 2):
        cut = jnp.sum((col_ref[...] < label).astype(jnp.int32), 1, keepdims=True)
        col_label = col_label + (column >= cut).astype(jnp.int32)
    blocks = []
    for source in MOVED:
        rows = [row_ref[first_row_ref[0] + source * ROWS_DEV + r] for r in range(ROWS_DEV)]
        for r in range(ROWS_DEV):
            row_label = rows[r]
            if window == 1:
                row_label = jnp.where(column >= 36, rows[(r + 1) % ROWS_DEV], rows[r])
            blocks.append(jnp.where(lane == col_label + 3 * row_label + 96, 10.0, 0.0))
    return jnp.concatenate(blocks, 0)


def tagged(cells, window, mask_refs):
    if mask_refs is None:
        return cells
    return jnp.where(iota(cells.shape, 1) < 96, cells, tags_of(window, *mask_refs))


def with_tags(cells, at, key):
    lane = iota(cells.shape, 1)
    own = cells if at == 0 else pltpu.roll(cells, 128 - at, 1)
    tags = pltpu.roll(cells, 64, 1)
    if key:
        tags = jnp.where(lane < HD + 9, tags - 10.0, tags)
    return jnp.where(lane < HD, own, tags)[:, :64].astype(bf16)


def together(steps):
    steps = list(steps)
    while steps:
        steps = [step for step in steps if next(step, 0) is None]


def attend_kernel(masks, x_ref, *refs):
    mask_refs = refs[:3] if masks else None
    out_ref = refs[-1]
    lane = iota((CELLS, 128), 1)
    per_window = [None, None]

    def attend(w, cells):
        cells = tagged(cells, w, mask_refs)
        query = with_tags(cells, 0, False) if masks else cells[:, :HD].astype(bf16)
        key = with_tags(cells, HD, True) if masks else cells[:, HD : 2 * HD].astype(bf16)
        value = jnp.where(lane < HD, pltpu.roll(cells, 64, 1), jnp.where(lane == HD, 1.0, 0.0)).astype(bf16)
        yield
        scores = dot_t(query, key)
        yield
        weights = jnp.exp(scores).astype(bf16)
        yield
        summed = dot(weights, value)
        yield
        attended = jnp.where(lane < HD, summed * (1.0 / summed[:, HD : HD + 1]), 0.0)
        per_window[w] = attended

    together(attend(w, cells) for w, cells in enumerate(to_windows(unpack_cells(x_ref))))
    cells = from_windows(per_window)
    total = 0.0
    for run, (start, stop) in enumerate(RUNS):
        rows = padded(cells[:, start:stop]).reshape(GROUP * PACK, 128)
        total = total + (pltpu.roll(rows, run * HD, 1) if run else rows)
    out_ref[...] = total.astype(bf16).reshape(GROUP, PACK, 128)


def attend_back_kernel(block, masks, head_ref, scale_ref, x_ref, grad_ref, *refs):
    mask_refs = refs[:3] if masks else None
    out_ref = refs[-1]
    lane = iota((CELLS, 128), 1)
    low = iota((HD, CELLS), 0)
    zeros = jnp.zeros((HD, CELLS), f32)
    scale_row = jnp.exp(jnp.full((1, 128), scale_ref[block, head_ref[0]], f32))
    unscale_row = 1.0 / scale_row
    packed = grad_ref[...].astype(f32).reshape(GROUP * PACK, 128)
    rolled = [pltpu.roll(packed, 128 - run * HD, 1) if run else packed for run in range(len(RUNS))]
    rolled = [
        part.reshape(GROUP, PACK, 128)[:, : stop - start] for part, (start, stop) in zip(rolled, RUNS)
    ]
    grads = to_windows(jnp.concatenate(rolled, 1))
    factors = to_windows(unpack_factors(x_ref))
    results = [None, None]

    def attend_back(w, cells):
        cells = tagged(cells, w, mask_refs)
        turned = cells.T
        query_t = (jnp.concatenate([turned[:HD], turned[96:]], 0) if masks else turned[:HD]).astype(bf16)
        key_t = turned[HD : 2 * HD].astype(bf16)
        value_t = turned[2 * HD : 3 * HD]
        grad_t = grads[w].T[:HD]
        key = with_tags(cells, HD, True) if masks else cells[:, HD : 2 * HD].astype(bf16)
        yield
        scores = dot(key, query_t)
        yield
        weights = jnp.exp(scores).astype(bf16)
        yield
        summed = dot(jnp.concatenate([value_t, jnp.where(low == 0, 1.0, 0.0)], 0).astype(bf16), weights)
        yield
        inverse = 1.0 / summed[HD : HD + 1]
        grad_t = (grad_t * inverse).astype(bf16).astype(f32)
        row_high, row_low = split_two(jnp.sum(grad_t * summed[:HD], 0, keepdims=True) * inverse)
        rows = jnp.where(low == 0, -row_high, jnp.where(low == 1, -row_low, 0.0))
        grad_ext = jnp.concatenate([grad_t, rows], 0).astype(bf16)
        yield
        ones = jnp.where(lane < HD + 2, 1.0, 0.0)
        value_ext = jnp.where(lane < HD, pltpu.roll(cells, 64, 1), ones)[:, :64].astype(bf16)
        yield
        grad_scores = (weights.astype(f32) * dot(value_ext, grad_ext)).astype(bf16)
        yield
        query_at = jnp.where((lane >= HD) & (lane < 2 * HD), pltpu.roll(cells, HD, 1), 0.0).astype(bf16)
        grad_at = jnp.concatenate([zeros, zeros, grad_t, zeros], 0).T.astype(bf16)
        yield
        grad_kv = dot(grad_scores, query_at) + dot(weights, grad_at)
        yield
        grad_q = dot(key_t, grad_scores)
        yield
        grad_q = jnp.concatenate([grad_q, zeros, zeros, zeros], 0).T
        yield
        total = jnp.where(lane < HD, grad_q * scale_row, grad_kv)
        unit = jnp.where(lane < HD, cells * unscale_row, jnp.where(lane < 2 * HD, cells, 0.0))
        q_factor, k_factor = factors[w][:, 96:97], factors[w][:, 97:98]
        factor = jnp.where(lane < HD, q_factor, jnp.where(lane < 2 * HD, k_factor, 1.0))
        results[w] = factor * (total - unit * head_sums(unit * total))

    together(attend_back(w, cells) for w, cells in enumerate(to_windows(unpack_cells(x_ref))))
    out_ref[...] = pack_cells(from_windows(results)).astype(bf16)


def first_kernel(tokens_ref, w_ref, scale_ref, out_ref):
    send_projected(tokens_ref[...], w_ref[...], scale_ref, 0, out_ref)


def middle_kernel(packed_ref, scale_ref, gain_ref, bias_ref, tokens_ref, w_proj_ref, w_ref, out_ref, rolled_ref):
    attended = unpack_heads(packed_ref)
    y_hat, _ = normalized(attended, w_proj_ref[...])
    out = (tokens_ref[...].astype(f32) + y_hat * gain_ref[0:1] + bias_ref[0:1]).astype(bf16).astype(f32)
    rolled = roll_tokens(out, -SHIFT).astype(bf16)
    rolled_ref[...] = rolled
    send_projected(rolled, w_ref[...], scale_ref, 1, out_ref)


def turn_kernel(core_ref, packed_ref, gain_ref, grad_ref, w_proj_ref, out_ref, kept_ref, given_ref, gains_ref):
    attended = unpack_heads(packed_ref)
    grad = roll_tokens(grad_ref[...].astype(f32), -SHIFT)
    grad_y, grad_att, gains = finish_back(attended, w_proj_ref[...], gain_ref[1:2], grad)
    pack_heads(grad_att, out_ref)
    kept, given = halves(attended, core_ref[0])
    kept_ref[...] = dot_0(grad_y, kept).astype(bf16)
    given_ref[...] = dot_0(grad_y, given).astype(bf16)
    gains_ref[...] = gains


def gather_qkv(qkv_ref):
    parts = [qkv_ref[h].astype(f32) for h in range(HEADS)]
    top = [lane_slice(parts[h][:SHORT], kind * HD) for kind in range(3) for h in range(HEADS)]
    tail = [lane_slice(parts[h][kind * 32 : kind * 32 + 32], 96) for kind in range(3) for h in range(HEADS)]
    return jnp.concatenate([jnp.concatenate(top, 1), jnp.concatenate(tail, 1)], 0).astype(bf16)


def halves(array, core):
    half = array.shape[1] // 2
    left, right = array[:, :half].astype(f32), array[:, half:].astype(f32)
    return jnp.where(core == 0, left, right).astype(bf16), jnp.where(core == 0, right, left).astype(bf16)


def back_kernel(
    core_ref,
    qkv_ref,
    packed_ref,
    gain_ref,
    w_ref,
    w_proj_ref,
    grad_ref,
    proj1_kept_ref,
    proj1_given_ref,
    tokens_ref,
    out_ref,
    gains_ref,
    grad0_ref,
    kept_ref,
    given_ref,
):
    d_qkv = gather_qkv(qkv_ref)
    from_qkv = roll_tokens(dot_t(d_qkv, w_ref[...]), SHIFT)
    grad = (grad_ref[...].astype(f32) + from_qkv).astype(bf16)
    grad0_ref[...] = grad
    attended = unpack_heads(packed_ref)
    grad_y, grad_att, gains = finish_back(attended, w_proj_ref[...], gain_ref[0:1], grad.astype(f32))
    sides = zip(halves(d_qkv, core_ref[0]), (proj1_kept_ref, proj1_given_ref), halves(attended, core_ref[0]))
    kept, given = [
        jnp.concatenate(
            [dot_0(tokens_ref[...], part).astype(bf16), proj1_ref[...], dot_0(grad_y, att).astype(bf16)], 1
        )
        for part, proj1_ref, att in sides
    ]
    kept_ref[...] = kept
    given_ref[...] = given
    pack_heads(grad_att, out_ref)
    gains_ref[...] = gains


def image_kernel(qkv_ref, w_ref, grad_ref, out_ref):
    out_ref[...] = (grad_ref[...].astype(f32) + dot_t(gather_qkv(qkv_ref), w_ref[...])).astype(bf16)


def last_kernel(core_ref, qkv_ref, tokens_ref, kept_ref, given_ref):
    kept, given = halves(gather_qkv(qkv_ref), core_ref[0])
    given_ref[...] = dot_0(tokens_ref[...], given).astype(bf16)
    kept_ref[...] = dot_0(tokens_ref[...], kept).astype(bf16)


def parts_kernel(late_ref, got_late_ref, got_ref, gains0_ref, gains1_ref, kept_ref, parts_ref):
    pieces = []
    for ref in (gains0_ref, gains1_ref):
        for row in (0, 1):
            pieces += split_two(ref[row : row + 1])
    gains = jnp.concatenate(pieces + [jnp.zeros((16 - len(pieces), C), f32)], 0)
    depth = C // 8
    for ring in range(8):
        block = gains[:, ring // 2 * 128 : ring // 2 * 128 + 128]
        block = pltpu.roll(block, depth, 1) if ring % 2 else block
        parts_ref[ACROSS.index(ring), TILES * depth :] = block.astype(bf16)
    late = late_ref[...].astype(f32) + got_late_ref[...].astype(f32)
    early = kept_ref[...].astype(f32) + got_ref[...].astype(f32)
    tile = 0
    for part in (late, early):
        for at in range(0, part.shape[1], 128):
            block = part[:, at : at + 128].astype(bf16).reshape(8, depth, 128)
            parts_ref[:, tile * depth : (tile + 1) * depth, :] = jnp.stack([block[ring] for ring in ACROSS])
            tile += 1


def first_sum_kernel(parts_ref, out_ref):
    total = jnp.sum(parts_ref[...].astype(f32), 0)
    gains = total[TILES * C // 8 :]
    total = total[: TILES * C // 8].reshape(TILES, 8, 8, 128)
    for place in range(8):
        rolled = pltpu.roll(gains, 128 - 8 * place, 1) if place else gains
        block = jnp.concatenate([total[:, place].reshape(TILES * 8, 128), rolled], 0)
        out_ref[ORDER.index(place)] = block.astype(bf16)


def second_sum_kernel(parts_ref, out_ref):
    out_ref[...] = jnp.sum(parts_ref[...].astype(f32), 0)


def add_kernel(one_ref, two_ref, out_ref):
    out_ref[...] = one_ref[...] + two_ref[...]


def final_kernel(core_ref, own_ref, other_ref, qkv_ref, proj_ref, gain_ref, bias_ref):
    own = own_ref[: TILES * 8].reshape(TILES, 8, 128)
    other = other_ref[: TILES * 8].reshape(TILES, 8, 128)
    first = core_ref[0] == 0
    left, right = jnp.where(first, own, other), jnp.where(first, other, own)
    for block, tiles in ((0, (0, 1, 2)), (1, (3, 4, 5))):
        qkv_ref[block] = jnp.concatenate([side[i] for side in (left, right) for i in tiles], 1)
    proj_ref[1] = jnp.concatenate([left[6], right[6]], 1)
    proj_ref[0] = jnp.concatenate([left[7], right[7]], 1)
    gains = (own_ref[TILES * 8 :] + other_ref[TILES * 8 :])[:, :8]
    gain_ref[...] = jnp.concatenate([gains[0:1] + gains[1:2], gains[4:5] + gains[5:6]], 0)
    bias_ref[...] = jnp.concatenate([gains[2:3] + gains[3:4], gains[6:7] + gains[7:8]], 0)


def pieces_of(shape):
    return 4 if shape[0] % 64 == 0 and shape[0] * shape[1] >= 2**18 else 1


def copies_of(source, target, sems, first):
    count = pieces_of(target.shape)
    rows = target.shape[0] // count
    if count == 1:
        return [pltpu.make_async_copy(source, target, sems.at[first])]
    return [
        pltpu.make_async_copy(
            source.at[pl.ds(i * rows, rows)], target.at[pl.ds(i * rows, rows)], sems.at[first + i]
        )
        for i in range(count)
    ]


class Fetched:
    def __init__(self, source, ref, sems, first):
        self.ref, self.copies = ref, copies_of(source, ref, sems, first)
        for copy in self.copies:
            copy.start()
        self.waited = False

    def __getitem__(self, at):
        if not self.waited:
            for copy in self.copies:
                copy.wait()
            self.waited = True
        return self.ref[at]


class Stored:
    def __init__(self, ref, target, sems, first):
        self.ref, self.copies = ref, copies_of(ref, target, sems, first)

    def __setitem__(self, at, value):
        self.ref[at] = value
        for copy in self.copies:
            copy.start()


def call(kernel, outs, scalars, arrays, masks=(), fetched=(), stored=()):
    arrays = [item if isinstance(item, tuple) else (item, None) for item in arrays]
    fetched = [item if isinstance(item, tuple) else (item, None) for item in fetched]
    counts = [len(scalars), len(arrays), len(fetched), len(masks), len(outs), len(stored), len(fetched), len(stored)]

    def wrapped(*refs):
        parts, at = [], 0
        for count in counts:
            parts.append(refs[at : at + count])
            at += count
        scalar_refs, array_refs, sources, mask_refs, out_refs, targets, filled, sent = parts
        sems = refs[-1]
        near = [ref if block is None else ref.at[block] for ref, (_, block) in zip(array_refs, arrays)]
        far, results, first = [], [], 0
        for i, (_, block) in enumerate(fetched):
            source = sources[i] if block is None else sources[i].at[block]
            far.append(Fetched(source, filled[i], sems, first))
            first += pieces_of(filled[i].shape)
        for i in range(len(stored)):
            results.append(Stored(sent[i], targets[i], sems, first))
            first += pieces_of(sent[i].shape)
        kernel(*scalar_refs, *near, *far, *mask_refs, *out_refs, *results)
        for result in results:
            for copy in result.copies:
                copy.wait()

    smem = pl.BlockSpec(memory_space=pltpu.SMEM)
    vmem = pl.BlockSpec(memory_space=pltpu.VMEM)
    hbm = pl.BlockSpec(memory_space=pltpu.HBM)
    scratch = [
        pltpu.VMEM(array.shape if block is None else array.shape[1:], array.dtype) for array, block in fetched
    ]
    scratch += [pltpu.VMEM(*out) for out in stored]
    if scratch:
        scratch.append(pltpu.SemaphoreType.DMA((sum(pieces_of(buffer.shape) for buffer in scratch),)))
    return pl.pallas_call(
        wrapped,
        out_shape=[jax.ShapeDtypeStruct(*out) for out in outs] + [pltpu.HBM(*out) for out in stored],
        in_specs=[smem] * len(scalars)
        + [vmem] * len(arrays)
        + [hbm] * len(fetched)
        + [smem, smem, vmem][: len(masks)],
        out_specs=[vmem] * len(outs) + [hbm] * len(stored),
        scratch_shapes=scratch,
        compiler_params=pltpu.CompilerParams(vmem_limit_bytes=VMEM_LIMIT),
    )(
        *scalars,
        *(array for array, _ in arrays),
        *(pltpu.with_memory_space_constraint(array, pltpu.HBM) for array, _ in fetched),
        *masks,
    )


def body(image, out_grad, w_qkv, w_proj, norm_gain, norm_bias, logit_scale, row_band, col_band):
    position = lax.axis_index("rows")
    half = GROUP // 2
    rings = range(DEVS // GROUP)
    aligned = [[GROUP * g + i for i in ORDER] for g in rings]
    across = [[GROUP * g + i for g in ACROSS] for i in range(GROUP)]
    moved = [[(GROUP * g + half + i) % DEVS for i in MOVED] for g in rings]
    moved_position = (position + DEVS - half) % DEVS
    head0, head1 = jnp.zeros((1,), jnp.int32), jnp.zeros((1,), jnp.int32)
    for h in range(HEADS):
        head0 = head0 + h * (position % GROUP == ORDER[h])
        head1 = head1 + h * (moved_position % GROUP == MOVED[h])
    first_row = (moved_position // GROUP * WIN).reshape(1)
    core = (lax.axis_index("dp") % 2).reshape(1)
    image, head0, head1, first_row, core = lax.optimization_barrier((image, head0, head1, first_row, core))
    masks = (first_row, row_band, col_band.reshape(1, -1))

    def exchange(array, groups):
        return lax.all_to_all(array, "rows", 0, 0, axis_index_groups=groups, tiled=True)

    tokens0 = image.reshape(TOK, C)
    grad_out = out_grad.reshape(TOK, C)
    short = ((GROUP, SHORT, 128), bf16)
    narrow = ((GROUP, PACK, 128), bf16)
    cells = ((TOK, C), bf16)
    proj = ((C, HH // 2), bf16)
    gains = ((8, C), f32)
    half_early = ((C, EARLY // 2), bf16)
    half_late = ((C, LATE // 2), bf16)

    def swap(array, apart):
        return lax.ppermute(array, "dp", [(i, i ^ apart) for i in range(4)])

    (x0,) = call(first_kernel, [short], (), (), fetched=(tokens0, (w_qkv, 0), logit_scale))
    x0 = exchange(x0, aligned)
    (a0,) = call(functools.partial(attend_kernel, False), [narrow], (), (x0,))
    a0 = exchange(a0, aligned)
    x1, tokens1 = call(
        middle_kernel,
        [short],
        (),
        (a0, logit_scale, norm_gain, norm_bias, tokens0, (w_proj, 0), (w_qkv, 1)),
        stored=[cells],
    )
    x1 = exchange(x1, moved)
    (a1,) = call(functools.partial(attend_kernel, True), [narrow], (), (x1,), masks)
    a1 = exchange(a1, moved)
    d1, proj1_kept, proj1_given, gains1 = call(
        turn_kernel,
        [narrow, proj, proj, gains],
        (core,),
        (a1, norm_gain, grad_out, (w_proj, 1)),
    )
    d1 = exchange(d1, moved)
    (qkv1,) = call(
        functools.partial(attend_back_kernel, 1, True), [short], (head1, logit_scale), (x1, d1), masks
    )
    qkv1 = exchange(qkv1, moved)
    d0, gains0, grad0, kept, given = call(
        back_kernel,
        [narrow, gains],
        (core,),
        (qkv1, a0, norm_gain, (w_qkv, 1), (w_proj, 0), grad_out, proj1_kept, proj1_given, tokens1),
        stored=[cells, half_early, half_early],
    )
    d0 = exchange(d0, aligned)
    (qkv0,) = call(functools.partial(attend_back_kernel, 0, False), [short], (head0, logit_scale), (x0, d0))
    qkv0 = exchange(qkv0, aligned)
    qkv0, given = lax.optimization_barrier((qkv0, given))
    got = swap(given, 1)
    late, given_late = call(last_kernel, [half_late, half_late], (core,), (qkv0, tokens0))
    got_late = swap(given_late, 1)
    (parts,) = call(
        parts_kernel,
        [((8, SENT, 128), bf16)],
        (),
        (late, got_late, got, gains0, gains1, kept),
    )
    parts = exchange(parts, across)
    (parts,) = call(first_sum_kernel, [((8, SHARE, 128), bf16)], (), (parts,))
    parts = exchange(parts, aligned)
    (share,) = call(second_sum_kernel, [((SHARE, 128), f32)], (), (parts,))
    (share,) = call(add_kernel, [((SHARE, 128), f32)], (), (share, swap(share, 2)))
    other = swap(share, 1)
    qkv0, _ = lax.optimization_barrier((qkv0, share))
    (grad_image,) = call(image_kernel, [cells], (), (qkv0, (w_qkv, 0), grad0))
    small = ((2, 8), f32)
    grad_qkv, grad_proj, grad_gain, grad_bias = call(
        final_kernel,
        [((2, 8, 3 * HH), f32), ((2, 8, HH), f32), small, small],
        (core,),
        (share, other),
    )
    return (
        grad_image.reshape(image.shape),
        grad_qkv,
        grad_proj.transpose(0, 2, 1),
        grad_gain,
        grad_bias,
    )


def solution(mesh):
    placed = (P("dp", "rows", None, None), P("dp", "rows", None, None)) + (P(),) * 7
    return jax.shard_map(
        body,
        mesh=mesh,
        in_specs=placed,
        out_specs=(
            P("dp", "rows", None, None),
            P(None, "rows", None),
            P(None, None, "rows"),
            P(None, "rows"),
            P(None, "rows"),
        ),
        check_vma=False,
    )
```

```python
import functools

import jax
import jax.numpy as jnp
from jax import lax
from jax.experimental import pallas as pl
from jax.experimental.pallas import tpu as pltpu
from jax.sharding import PartitionSpec as P

C = 512
HEADS = 8
HD = 32
WIN = 24
HH = 256
SHIFT = 12
GROUP = 8
TOK = 144
CELLS = WIN * WIN
ROWS_DEV = 3
PACK = 40
RUNS = ((0, 40), (40, 80), (80, 112), (112, 144))
DEVS = 64
ORDER = (0, 2, 4, 6, 1, 3, 5, 7)
MOVED = (0, 2, 4, 6, 7, 5, 3, 1)
ACROSS = (7, 6, 5, 4, 3, 2, 1, 0)
VMEM_LIMIT = 24 * 2**20
EARLY = 3 * HH + 2 * HH
SHORT = 112
LATE = 3 * HH
TILES = (LATE // 2 + EARLY // 2) // 128
SENT = TILES * C // 8 + 16
SHARE = TILES * 8 + 16

norm_eps = 1e-05
f32 = jnp.float32
bf16 = jnp.bfloat16


def dot(a, b):
    return jnp.dot(a, b, preferred_element_type=f32)


def dot_t(a, b):
    return lax.dot_general(a, b, (((1,), (1,)), ((), ())), preferred_element_type=f32)


def dot_0(a, b):
    return lax.dot_general(a, b, (((0,), (0,)), ((), ())), preferred_element_type=f32)


def iota(shape, axis):
    return lax.broadcasted_iota(jnp.int32, shape, axis)


def head_sums(x):
    width = x.shape[1]
    ones = (iota((width, width), 0) // HD == iota((width, width), 1) // HD).astype(f32).astype(bf16)
    high = x.astype(bf16)
    low = (x - high.astype(f32)).astype(bf16)
    return dot(high, ones) + dot(low, ones)


def split_two(x):
    high = x.astype(bf16).astype(f32)
    return high, x - high


def lane_slice(x, at):
    return x[:, at : at + HD]


def send_projected(tokens, weight, scale_ref, block, out_ref):
    projected = dot(tokens, weight)
    query, key, value = projected[:, :HH], projected[:, HH : 2 * HH], projected[:, 2 * HH :]
    lane = iota((1, HH), 1)
    scale = jnp.zeros((1, HH), f32)
    scales = scale_ref[...][block : block + 1]
    for h in range(HEADS):
        scale = jnp.where(lane // HD == h, scales[:, h : h + 1], scale)
    q_factor = lax.rsqrt(1.0 + head_sums(query * query))
    k_factor = lax.rsqrt(1.0 + head_sums(key * key))
    q_hat = query * q_factor * jnp.exp(scale)
    k_hat = key * k_factor
    slot = iota((16, HH), 1) % HD
    factors = jnp.zeros((16, HH), f32)
    for i in range(TOK // 16):
        rows = slice(16 * i, 16 * i + 16)
        factors = jnp.where(slot == 2 * i, q_factor[rows], jnp.where(slot == 2 * i + 1, k_factor[rows], factors))
    for h in range(HEADS):
        parts = [lane_slice(part, h * HD) for part in (q_hat, k_hat, value)]
        tail = jnp.concatenate([part[SHORT:] for part in parts] + [lane_slice(factors, h * HD)], 0)
        out_ref[h] = jnp.concatenate([part[:SHORT] for part in parts] + [tail], 1).astype(bf16)


def unpack_cells(x_ref):
    x = x_ref[...].astype(f32)
    lane = iota((GROUP * 32, 128), 1)
    rolled = [
        pltpu.roll(x[:, kind * 32 : kind * 32 + 32].reshape(GROUP * 32, 128), 32 + 32 * kind, 1)
        for kind in range(3)
    ]
    tail = jnp.where(lane < HD, rolled[0], jnp.where(lane < 2 * HD, rolled[1], rolled[2]))
    return jnp.concatenate([x, tail.reshape(GROUP, 32, 128)], 1)


def unpack_factors(x_ref):
    rows = x_ref[...].astype(f32)[:, SHORT - 16 :].reshape(GROUP * 16, 128)
    rolled = [pltpu.roll(rows, 128 - 2 * i, 1) if i else rows for i in range(TOK // 16)]
    return jnp.concatenate([part.reshape(GROUP, 16, 128) for part in rolled], 1)


def unpack_heads(packed_ref):
    packed = packed_ref[...].astype(f32)
    rows = [
        jnp.concatenate([lane_slice(packed[h, : stop - start], run * HD) for h in range(HEADS)], 1)
        for run, (start, stop) in enumerate(RUNS)
    ]
    return jnp.concatenate(rows, 0).astype(bf16)


def padded(run):
    missing = PACK - run.shape[-2]
    if not missing:
        return run
    return jnp.concatenate([run, jnp.zeros((*run.shape[:-2], missing, run.shape[-1]), f32)], -2)


def pack_heads(array, out_ref):
    heads = []
    for h in range(HEADS):
        parts = [padded(lane_slice(array[start:stop], h * HD)) for start, stop in RUNS]
        heads.append(jnp.concatenate(parts, 1))
    out_ref[...] = jnp.stack(heads).astype(bf16)


def to_windows(array):
    split = array.reshape(GROUP, ROWS_DEV, 2, WIN, array.shape[-1])
    return [split[:, :, w].reshape(CELLS, array.shape[-1]) for w in range(2)]


def from_windows(pair):
    depth = pair[0].shape[-1]
    parts = [part.reshape(GROUP, ROWS_DEV, 1, WIN, depth) for part in pair]
    return jnp.concatenate(parts, 2).reshape(GROUP, TOK, depth)


def pack_cells(cells):
    tail = cells[:, SHORT:].reshape(GROUP * 32, 128)
    moved = [pltpu.roll(tail, 96 - 32 * kind, 1).reshape(GROUP, 32, 128) for kind in range(3)]
    moved = jnp.concatenate(moved + [jnp.zeros((GROUP, SHORT - 96, 128), f32)], 1)
    lane = iota(moved.shape, 2)
    return jnp.where(lane < 96, cells[:, :SHORT], moved)


def roll_tokens(array, by):
    by = by % TOK
    return jnp.concatenate([array[TOK - by :], array[: TOK - by]], 0)


def normalized(attended, weight):
    outputs = dot(attended, weight)
    centered = outputs - jnp.mean(outputs, -1, keepdims=True)
    inverse = lax.rsqrt(jnp.mean(centered * centered, -1, keepdims=True) + norm_eps)
    return centered * inverse, inverse


def finish_back(attended, weight, gain_row, grad_out):
    y_hat, inverse = normalized(attended, weight)
    grad_gain = jnp.sum(grad_out * y_hat, 0, keepdims=True)
    grad_bias = jnp.sum(grad_out, 0, keepdims=True)
    scaled = grad_out * gain_row
    grad_y = inverse * (
        scaled
        - jnp.mean(scaled, -1, keepdims=True)
        - y_hat * jnp.mean(scaled * y_hat, -1, keepdims=True)
    )
    grad_y = grad_y.astype(bf16)
    gains = jnp.concatenate([grad_gain, grad_bias, jnp.zeros((6, C), f32)], 0)
    return grad_y, dot_t(grad_y, weight), gains


def tags_of(window, first_row_ref, row_ref, col_ref):
    lane = iota((WIN, 128), 1)
    place = iota((WIN, 1), 0)
    column = place + window * WIN
    col_label = jnp.zeros((WIN, 1), jnp.int32)
    for label in (1, 2):
        cut = jnp.sum((col_ref[...] < label).astype(jnp.int32), 1, keepdims=True)
        col_label = col_label + (column >= cut).astype(jnp.int32)
    blocks = []
    for source in MOVED:
        rows = [row_ref[first_row_ref[0] + source * ROWS_DEV + r] for r in range(ROWS_DEV)]
        for r in range(ROWS_DEV):
            row_label = rows[r]
            if window == 1:
                row_label = jnp.where(column >= 36, rows[(r + 1) % ROWS_DEV], rows[r])
            blocks.append(jnp.where(lane == col_label + 3 * row_label + 96, 10.0, 0.0))
    return jnp.concatenate(blocks, 0)


def tagged(cells, window, mask_refs):
    if mask_refs is None:
        return cells
    return jnp.where(iota(cells.shape, 1) < 96, cells, tags_of(window, *mask_refs))


def with_tags(cells, at, key):
    lane = iota(cells.shape, 1)
    own = cells if at == 0 else pltpu.roll(cells, 128 - at, 1)
    tags = pltpu.roll(cells, 64, 1)
    if key:
        tags = jnp.where(lane < HD + 9, tags - 10.0, tags)
    return jnp.where(lane < HD, own, tags)[:, :64].astype(bf16)


def together(steps):
    steps = list(steps)
    while steps:
        steps = [step for step in steps if next(step, 0) is None]


def attend_kernel(masks, x_ref, *refs):
    mask_refs = refs[:3] if masks else None
    out_ref = refs[-1]
    lane = iota((CELLS, 128), 1)
    per_window = [None, None]

    def attend(w, cells):
        cells = tagged(cells, w, mask_refs)
        query = with_tags(cells, 0, False) if masks else cells[:, :HD].astype(bf16)
        key = with_tags(cells, HD, True) if masks else cells[:, HD : 2 * HD].astype(bf16)
        value = jnp.where(lane < HD, pltpu.roll(cells, 64, 1), jnp.where(lane == HD, 1.0, 0.0)).astype(bf16)
        yield
        scores = dot_t(query, key)
        yield
        weights = jnp.exp(scores).astype(bf16)
        yield
        summed = dot(weights, value)
        yield
        attended = jnp.where(lane < HD, summed * (1.0 / summed[:, HD : HD + 1]), 0.0)
        per_window[w] = attended

    together(attend(w, cells) for w, cells in enumerate(to_windows(unpack_cells(x_ref))))
    cells = from_windows(per_window)
    total = 0.0
    for run, (start, stop) in enumerate(RUNS):
        rows = padded(cells[:, start:stop]).reshape(GROUP * PACK, 128)
        total = total + (pltpu.roll(rows, run * HD, 1) if run else rows)
    out_ref[...] = total.astype(bf16).reshape(GROUP, PACK, 128)


def attend_back_kernel(block, masks, head_ref, scale_ref, x_ref, grad_ref, *refs):
    mask_refs = refs[:3] if masks else None
    out_ref = refs[-1]
    lane = iota((CELLS, 128), 1)
    low = iota((HD, CELLS), 0)
    zeros = jnp.zeros((HD, CELLS), f32)
    scale_row = jnp.exp(jnp.full((1, 128), scale_ref[block, head_ref[0]], f32))
    unscale_row = 1.0 / scale_row
    packed = grad_ref[...].astype(f32).reshape(GROUP * PACK, 128)
    rolled = [pltpu.roll(packed, 128 - run * HD, 1) if run else packed for run in range(len(RUNS))]
    rolled = [
        part.reshape(GROUP, PACK, 128)[:, : stop - start] for part, (start, stop) in zip(rolled, RUNS)
    ]
    grads = to_windows(jnp.concatenate(rolled, 1))
    factors = to_windows(unpack_factors(x_ref))
    results = [None, None]

    def attend_back(w, cells):
        cells = tagged(cells, w, mask_refs)
        turned = cells.T
        query_t = (jnp.concatenate([turned[:HD], turned[96:]], 0) if masks else turned[:HD]).astype(bf16)
        key_t = turned[HD : 2 * HD].astype(bf16)
        value_t = turned[2 * HD : 3 * HD]
        grad_t = grads[w].T[:HD]
        key = with_tags(cells, HD, True) if masks else cells[:, HD : 2 * HD].astype(bf16)
        yield
        scores = dot(key, query_t)
        yield
        weights = jnp.exp(scores).astype(bf16)
        yield
        summed = dot(jnp.concatenate([value_t, jnp.where(low == 0, 1.0, 0.0)], 0).astype(bf16), weights)
        yield
        inverse = 1.0 / summed[HD : HD + 1]
        grad_t = (grad_t * inverse).astype(bf16).astype(f32)
        row_high, row_low = split_two(jnp.sum(grad_t * summed[:HD], 0, keepdims=True) * inverse)
        rows = jnp.where(low == 0, -row_high, jnp.where(low == 1, -row_low, 0.0))
        grad_ext = jnp.concatenate([grad_t, rows], 0).astype(bf16)
        yield
        ones = jnp.where(lane < HD + 2, 1.0, 0.0)
        value_ext = jnp.where(lane < HD, pltpu.roll(cells, 64, 1), ones)[:, :64].astype(bf16)
        yield
        grad_scores = (weights.astype(f32) * dot(value_ext, grad_ext)).astype(bf16)
        yield
        query_at = jnp.where((lane >= HD) & (lane < 2 * HD), pltpu.roll(cells, HD, 1), 0.0).astype(bf16)
        grad_at = jnp.concatenate([zeros, zeros, grad_t, zeros], 0).T.astype(bf16)
        yield
        grad_kv = dot(grad_scores, query_at) + dot(weights, grad_at)
        yield
        grad_q = dot(key_t, grad_scores)
        yield
        grad_q = jnp.concatenate([grad_q, zeros, zeros, zeros], 0).T
        yield
        total = jnp.where(lane < HD, grad_q * scale_row, grad_kv)
        unit = jnp.where(lane < HD, cells * unscale_row, jnp.where(lane < 2 * HD, cells, 0.0))
        q_factor, k_factor = factors[w][:, 96:97], factors[w][:, 97:98]
        factor = jnp.where(lane < HD, q_factor, jnp.where(lane < 2 * HD, k_factor, 1.0))
        results[w] = factor * (total - unit * head_sums(unit * total))

    together(attend_back(w, cells) for w, cells in enumerate(to_windows(unpack_cells(x_ref))))
    out_ref[...] = pack_cells(from_windows(results)).astype(bf16)


def first_kernel(tokens_ref, w_ref, scale_ref, out_ref):
    send_projected(tokens_ref[...], w_ref[...], scale_ref, 0, out_ref)


def middle_kernel(packed_ref, scale_ref, gain_ref, bias_ref, tokens_ref, w_proj_ref, w_ref, out_ref, rolled_ref):
    attended = unpack_heads(packed_ref)
    y_hat, _ = normalized(attended, w_proj_ref[...])
    out = (tokens_ref[...].astype(f32) + y_hat * gain_ref[0:1] + bias_ref[0:1]).astype(bf16).astype(f32)
    rolled = roll_tokens(out, -SHIFT).astype(bf16)
    rolled_ref[...] = rolled
    send_projected(rolled, w_ref[...], scale_ref, 1, out_ref)


def turn_kernel(core_ref, packed_ref, gain_ref, grad_ref, w_proj_ref, out_ref, kept_ref, given_ref, gains_ref):
    attended = unpack_heads(packed_ref)
    grad = roll_tokens(grad_ref[...].astype(f32), -SHIFT)
    grad_y, grad_att, gains = finish_back(attended, w_proj_ref[...], gain_ref[1:2], grad)
    pack_heads(grad_att, out_ref)
    kept, given = halves(attended, core_ref[0])
    kept_ref[...] = dot_0(grad_y, kept).astype(bf16)
    given_ref[...] = dot_0(grad_y, given).astype(bf16)
    gains_ref[...] = gains


def gather_qkv(qkv_ref):
    parts = [qkv_ref[h].astype(f32) for h in range(HEADS)]
    top = [lane_slice(parts[h][:SHORT], kind * HD) for kind in range(3) for h in range(HEADS)]
    tail = [lane_slice(parts[h][kind * 32 : kind * 32 + 32], 96) for kind in range(3) for h in range(HEADS)]
    return jnp.concatenate([jnp.concatenate(top, 1), jnp.concatenate(tail, 1)], 0).astype(bf16)


def halves(array, core):
    half = array.shape[1] // 2
    left, right = array[:, :half].astype(f32), array[:, half:].astype(f32)
    return jnp.where(core == 0, left, right).astype(bf16), jnp.where(core == 0, right, left).astype(bf16)


def back_kernel(
    core_ref,
    qkv_ref,
    packed_ref,
    gain_ref,
    w_ref,
    w_proj_ref,
    grad_ref,
    proj1_kept_ref,
    proj1_given_ref,
    tokens_ref,
    out_ref,
    gains_ref,
    grad0_ref,
    kept_ref,
    given_ref,
):
    d_qkv = gather_qkv(qkv_ref)
    from_qkv = roll_tokens(dot_t(d_qkv, w_ref[...]), SHIFT)
    grad = (grad_ref[...].astype(f32) + from_qkv).astype(bf16)
    grad0_ref[...] = grad
    attended = unpack_heads(packed_ref)
    grad_y, grad_att, gains = finish_back(attended, w_proj_ref[...], gain_ref[0:1], grad.astype(f32))
    sides = zip(halves(d_qkv, core_ref[0]), (proj1_kept_ref, proj1_given_ref), halves(attended, core_ref[0]))
    kept, given = [
        jnp.concatenate(
            [dot_0(tokens_ref[...], part).astype(bf16), proj1_ref[...], dot_0(grad_y, att).astype(bf16)], 1
        )
        for part, proj1_ref, att in sides
    ]
    kept_ref[...] = kept
    given_ref[...] = given
    pack_heads(grad_att, out_ref)
    gains_ref[...] = gains


def image_kernel(qkv_ref, w_ref, grad_ref, out_ref):
    out_ref[...] = (grad_ref[...].astype(f32) + dot_t(gather_qkv(qkv_ref), w_ref[...])).astype(bf16)


def late_kernel(given, core_ref, qkv_ref, tokens_ref, out_ref):
    half = halves(gather_qkv(qkv_ref), core_ref[0])[given]
    out_ref[...] = dot_0(tokens_ref[...], half).astype(bf16)


def parts_kernel(late_ref, got_late_ref, got_ref, gains0_ref, gains1_ref, kept_ref, parts_ref):
    pieces = []
    for ref in (gains0_ref, gains1_ref):
        for row in (0, 1):
            pieces += split_two(ref[row : row + 1])
    gains = jnp.concatenate(pieces + [jnp.zeros((16 - len(pieces), C), f32)], 0)
    depth = C // 8
    for ring in range(8):
        block = gains[:, ring // 2 * 128 : ring // 2 * 128 + 128]
        block = pltpu.roll(block, depth, 1) if ring % 2 else block
        parts_ref[ACROSS.index(ring), TILES * depth :] = block.astype(bf16)
    late = late_ref[...].astype(f32) + got_late_ref[...].astype(f32)
    early = kept_ref[...].astype(f32) + got_ref[...].astype(f32)
    tile = 0
    for part in (late, early):
        for at in range(0, part.shape[1], 128):
            block = part[:, at : at + 128].astype(bf16).reshape(8, depth, 128)
            parts_ref[:, tile * depth : (tile + 1) * depth, :] = jnp.stack([block[ring] for ring in ACROSS])
            tile += 1


def first_sum_kernel(parts_ref, out_ref):
    total = jnp.sum(parts_ref[...].astype(f32), 0)
    gains = total[TILES * C // 8 :]
    high, low = split_two(gains + pltpu.roll(gains, 15, 0))
    gains = jnp.where(iota(gains.shape, 0) % 2 == 0, high, pltpu.roll(low, 1, 0))
    total = total[: TILES * C // 8].reshape(TILES, 8, 8, 128)
    for place in range(8):
        rolled = pltpu.roll(gains, 128 - 8 * place, 1) if place else gains
        block = jnp.concatenate([total[:, place].reshape(TILES * 8, 128), rolled], 0)
        out_ref[ORDER.index(place)] = block.astype(bf16)


def second_sum_kernel(parts_ref, out_ref):
    out_ref[...] = jnp.sum(parts_ref[...].astype(f32), 0)


def add_kernel(one_ref, two_ref, out_ref):
    out_ref[...] = one_ref[...] + two_ref[...]


def final_kernel(core_ref, own_ref, other_ref, qkv_ref, proj_ref, gain_ref, bias_ref):
    own = own_ref[: TILES * 8].reshape(TILES, 8, 128)
    other = other_ref[: TILES * 8].reshape(TILES, 8, 128)
    first = core_ref[0] == 0
    left, right = jnp.where(first, own, other), jnp.where(first, other, own)
    for block, tiles in ((0, (0, 1, 2)), (1, (3, 4, 5))):
        qkv_ref[block] = jnp.concatenate([side[i] for side in (left, right) for i in tiles], 1)
    proj_ref[1] = jnp.concatenate([left[6], right[6]], 1)
    proj_ref[0] = jnp.concatenate([left[7], right[7]], 1)
    gains = (own_ref[TILES * 8 :] + other_ref[TILES * 8 :])[:, :8]
    gain_ref[...] = jnp.concatenate([gains[0:1] + gains[1:2], gains[4:5] + gains[5:6]], 0)
    bias_ref[...] = jnp.concatenate([gains[2:3] + gains[3:4], gains[6:7] + gains[7:8]], 0)


def pieces_of(shape):
    return 2 if shape[0] % 64 == 0 and shape[0] * shape[1] >= 2**18 else 1


def copies_of(source, target, sems, first):
    count = pieces_of(target.shape)
    rows = target.shape[0] // count
    if count == 1:
        return [pltpu.make_async_copy(source, target, sems.at[first])]
    return [
        pltpu.make_async_copy(
            source.at[pl.ds(i * rows, rows)], target.at[pl.ds(i * rows, rows)], sems.at[first + i]
        )
        for i in range(count)
    ]


class Fetched:
    def __init__(self, source, ref, sems, first):
        self.ref, self.copies = ref, copies_of(source, ref, sems, first)
        for copy in self.copies:
            copy.start()
        self.waited = False

    def __getitem__(self, at):
        if not self.waited:
            for copy in self.copies:
                copy.wait()
            self.waited = True
        return self.ref[at]


class Stored:
    def __init__(self, ref, target, sems, first):
        self.ref, self.copies = ref, copies_of(ref, target, sems, first)

    def __setitem__(self, at, value):
        self.ref[at] = value
        for copy in self.copies:
            copy.start()


def call(kernel, outs, scalars, arrays, masks=(), fetched=(), stored=()):
    arrays = [item if isinstance(item, tuple) else (item, None) for item in arrays]
    fetched = [item if isinstance(item, tuple) else (item, None) for item in fetched]
    counts = [len(scalars), len(arrays), len(fetched), len(masks), len(outs), len(stored), len(fetched), len(stored)]

    def wrapped(*refs):
        parts, at = [], 0
        for count in counts:
            parts.append(refs[at : at + count])
            at += count
        scalar_refs, array_refs, sources, mask_refs, out_refs, targets, filled, sent = parts
        sems = refs[-1]
        near = [ref if block is None else ref.at[block] for ref, (_, block) in zip(array_refs, arrays)]
        far, results, first = [], [], 0
        for i, (_, block) in enumerate(fetched):
            source = sources[i] if block is None else sources[i].at[block]
            far.append(Fetched(source, filled[i], sems, first))
            first += pieces_of(filled[i].shape)
        for i in range(len(stored)):
            results.append(Stored(sent[i], targets[i], sems, first))
            first += pieces_of(sent[i].shape)
        kernel(*scalar_refs, *near, *far, *mask_refs, *out_refs, *results)
        for result in results:
            for copy in result.copies:
                copy.wait()

    smem = pl.BlockSpec(memory_space=pltpu.SMEM)
    vmem = pl.BlockSpec(memory_space=pltpu.VMEM)
    hbm = pl.BlockSpec(memory_space=pltpu.HBM)
    scratch = [
        pltpu.VMEM(array.shape if block is None else array.shape[1:], array.dtype) for array, block in fetched
    ]
    scratch += [pltpu.VMEM(*out) for out in stored]
    if scratch:
        scratch.append(pltpu.SemaphoreType.DMA((sum(pieces_of(buffer.shape) for buffer in scratch),)))
    return pl.pallas_call(
        wrapped,
        out_shape=[jax.ShapeDtypeStruct(*out) for out in outs] + [pltpu.HBM(*out) for out in stored],
        in_specs=[smem] * len(scalars)
        + [vmem] * len(arrays)
        + [hbm] * len(fetched)
        + [smem, smem, vmem][: len(masks)],
        out_specs=[vmem] * len(outs) + [hbm] * len(stored),
        scratch_shapes=scratch,
        compiler_params=pltpu.CompilerParams(vmem_limit_bytes=VMEM_LIMIT),
    )(
        *scalars,
        *(array for array, _ in arrays),
        *(pltpu.with_memory_space_constraint(array, pltpu.HBM) for array, _ in fetched),
        *masks,
    )


def body(image, out_grad, w_qkv, w_proj, norm_gain, norm_bias, logit_scale, row_band, col_band):
    position = lax.axis_index("rows")
    half = GROUP // 2
    rings = range(DEVS // GROUP)
    aligned = [[GROUP * g + i for i in ORDER] for g in rings]
    across = [[GROUP * g + i for g in ACROSS] for i in range(GROUP)]
    moved = [[(GROUP * g + half + i) % DEVS for i in MOVED] for g in rings]
    moved_position = (position + DEVS - half) % DEVS
    head0, head1 = jnp.zeros((1,), jnp.int32), jnp.zeros((1,), jnp.int32)
    for h in range(HEADS):
        head0 = head0 + h * (position % GROUP == ORDER[h])
        head1 = head1 + h * (moved_position % GROUP == MOVED[h])
    first_row = (moved_position // GROUP * WIN).reshape(1)
    core = (lax.axis_index("dp") % 2).reshape(1)
    image, head0, head1, first_row, core = lax.optimization_barrier((image, head0, head1, first_row, core))
    masks = (first_row, row_band, col_band.reshape(1, -1))

    def exchange(array, groups):
        return lax.all_to_all(array, "rows", 0, 0, axis_index_groups=groups, tiled=True)

    tokens0 = image.reshape(TOK, C)
    grad_out = out_grad.reshape(TOK, C)
    short = ((GROUP, SHORT, 128), bf16)
    narrow = ((GROUP, PACK, 128), bf16)
    cells = ((TOK, C), bf16)
    proj = ((C, HH // 2), bf16)
    gains = ((8, C), f32)
    half_early = ((C, EARLY // 2), bf16)
    half_late = ((C, LATE // 2), bf16)

    def swap(array, apart):
        return lax.ppermute(array, "dp", [(i, i ^ apart) for i in range(4)])

    (x0,) = call(first_kernel, [short], (), (), fetched=(tokens0, (w_qkv, 0), logit_scale))
    x0 = exchange(x0, aligned)
    (a0,) = call(functools.partial(attend_kernel, False), [narrow], (), (x0,))
    a0 = exchange(a0, aligned)
    x1, tokens1 = call(
        middle_kernel,
        [short],
        (),
        (a0, logit_scale, norm_gain, norm_bias, tokens0, (w_proj, 0), (w_qkv, 1)),
        stored=[cells],
    )
    x1 = exchange(x1, moved)
    (a1,) = call(functools.partial(attend_kernel, True), [narrow], (), (x1,), masks)
    a1 = exchange(a1, moved)
    d1, proj1_kept, proj1_given, gains1 = call(
        turn_kernel,
        [narrow, proj, proj, gains],
        (core,),
        (a1, norm_gain, grad_out, (w_proj, 1)),
    )
    d1 = exchange(d1, moved)
    (qkv1,) = call(
        functools.partial(attend_back_kernel, 1, True), [short], (head1, logit_scale), (x1, d1), masks
    )
    qkv1 = exchange(qkv1, moved)
    d0, gains0, grad0, kept, given = call(
        back_kernel,
        [narrow, gains],
        (core,),
        (qkv1, a0, norm_gain, (w_qkv, 1), (w_proj, 0), grad_out, proj1_kept, proj1_given, tokens1),
        stored=[cells, half_early, half_early],
    )
    d0 = exchange(d0, aligned)
    (qkv0,) = call(functools.partial(attend_back_kernel, 0, False), [short], (head0, logit_scale), (x0, d0))
    qkv0 = exchange(qkv0, aligned)
    qkv0, given = lax.optimization_barrier((qkv0, given))
    got = swap(given, 1)
    (given_late,) = call(functools.partial(late_kernel, 1), [half_late], (core,), (qkv0, tokens0))
    got_late = swap(given_late, 1)
    qkv0, given_late = lax.optimization_barrier((qkv0, given_late))
    (late,) = call(functools.partial(late_kernel, 0), [half_late], (core,), (qkv0, tokens0))
    (parts,) = call(
        parts_kernel,
        [((8, SENT, 128), bf16)],
        (),
        (late, got_late, got, gains0, gains1, kept),
    )
    parts = exchange(parts, across)
    (parts,) = call(first_sum_kernel, [((8, SHARE, 128), bf16)], (), (parts,))
    parts = exchange(parts, aligned)
    (share,) = call(second_sum_kernel, [((SHARE, 128), f32)], (), (parts,))
    (share,) = call(add_kernel, [((SHARE, 128), f32)], (), (share, swap(share, 2)))
    other = swap(share, 1)
    qkv0, _ = lax.optimization_barrier((qkv0, share))
    (grad_image,) = call(image_kernel, [cells], (), (qkv0, (w_qkv, 0), grad0))
    small = ((2, 8), f32)
    grad_qkv, grad_proj, grad_gain, grad_bias = call(
        final_kernel,
        [((2, 8, 3 * HH), f32), ((2, 8, HH), f32), small, small],
        (core,),
        (share, other),
    )
    return (
        grad_image.reshape(image.shape),
        grad_qkv,
        grad_proj.transpose(0, 2, 1),
        grad_gain,
        grad_bias,
    )


def solution(mesh):
    placed = (P("dp", "rows", None, None), P("dp", "rows", None, None)) + (P(),) * 7
    return jax.shard_map(
        body,
        mesh=mesh,
        in_specs=placed,
        out_specs=(
            P("dp", "rows", None, None),
            P(None, "rows", None),
            P(None, None, "rows"),
            P(None, "rows"),
            P(None, "rows"),
        ),
        check_vma=False,
    )
```

```python
import functools

import jax
import jax.numpy as jnp
from jax import lax
from jax.experimental import pallas as pl
from jax.experimental.pallas import tpu as pltpu
from jax.sharding import PartitionSpec as P

C = 512
HEADS = 8
HD = 32
WIN = 24
HH = 256
SHIFT = 12
GROUP = 8
TOK = 144
CELLS = WIN * WIN
ROWS_DEV = 3
PACK = 40
RUNS = ((0, 40), (40, 80), (80, 112), (112, 144))
DEVS = 64
ORDER = (0, 2, 4, 6, 1, 3, 5, 7)
MOVED = (0, 2, 4, 6, 7, 5, 3, 1)
ACROSS = (7, 6, 5, 4, 3, 2, 1, 0)
VMEM_LIMIT = 24 * 2**20
EARLY = 3 * HH + 2 * HH
SHORT = 112
LATE = 3 * HH
TILES = (LATE // 2 + EARLY // 2) // 128
SENT = TILES * C // 8 + 16
SHARE = TILES * 8 + 16

norm_eps = 1e-05
f32 = jnp.float32
bf16 = jnp.bfloat16


def dot(a, b):
    return jnp.dot(a, b, preferred_element_type=f32)


def dot_t(a, b):
    return lax.dot_general(a, b, (((1,), (1,)), ((), ())), preferred_element_type=f32)


def dot_0(a, b):
    return lax.dot_general(a, b, (((0,), (0,)), ((), ())), preferred_element_type=f32)


def iota(shape, axis):
    return lax.broadcasted_iota(jnp.int32, shape, axis)


def head_sums(x):
    width = x.shape[1]
    ones = (iota((width, width), 0) // HD == iota((width, width), 1) // HD).astype(f32).astype(bf16)
    high = x.astype(bf16)
    low = (x - high.astype(f32)).astype(bf16)
    return dot(high, ones) + dot(low, ones)


def split_two(x):
    high = x.astype(bf16).astype(f32)
    return high, x - high


def lane_slice(x, at):
    return x[:, at : at + HD]


def send_projected(tokens, weight, scale_ref, block, out_ref):
    projected = dot(tokens, weight)
    query, key, value = projected[:, :HH], projected[:, HH : 2 * HH], projected[:, 2 * HH :]
    lane = iota((1, HH), 1)
    scale = jnp.zeros((1, HH), f32)
    scales = scale_ref[...][block : block + 1]
    for h in range(HEADS):
        scale = jnp.where(lane // HD == h, scales[:, h : h + 1], scale)
    q_factor = lax.rsqrt(1.0 + head_sums(query * query))
    k_factor = lax.rsqrt(1.0 + head_sums(key * key))
    q_hat = query * q_factor * jnp.exp(scale)
    k_hat = key * k_factor
    slot = iota((16, HH), 1) % HD
    factors = jnp.zeros((16, HH), f32)
    for i in range(TOK // 16):
        rows = slice(16 * i, 16 * i + 16)
        factors = jnp.where(slot == 2 * i, q_factor[rows], jnp.where(slot == 2 * i + 1, k_factor[rows], factors))
    for h in range(HEADS):
        parts = [lane_slice(part, h * HD) for part in (q_hat, k_hat, value)]
        tail = jnp.concatenate([part[SHORT:] for part in parts] + [lane_slice(factors, h * HD)], 0)
        out_ref[h] = jnp.concatenate([part[:SHORT] for part in parts] + [tail], 1).astype(bf16)


def unpack_cells(x_ref):
    x = x_ref[...].astype(f32)
    lane = iota((GROUP * 32, 128), 1)
    rolled = [
        pltpu.roll(x[:, kind * 32 : kind * 32 + 32].reshape(GROUP * 32, 128), 32 + 32 * kind, 1)
        for kind in range(3)
    ]
    tail = jnp.where(lane < HD, rolled[0], jnp.where(lane < 2 * HD, rolled[1], rolled[2]))
    return jnp.concatenate([x, tail.reshape(GROUP, 32, 128)], 1)


def unpack_factors(x_ref):
    rows = x_ref[...].astype(f32)[:, SHORT - 16 :].reshape(GROUP * 16, 128)
    rolled = [pltpu.roll(rows, 128 - 2 * i, 1) if i else rows for i in range(TOK // 16)]
    return jnp.concatenate([part.reshape(GROUP, 16, 128) for part in rolled], 1)


def unpack_heads(packed_ref):
    packed = packed_ref[...].astype(f32)
    rows = [
        jnp.concatenate([lane_slice(packed[h, : stop - start], run * HD) for h in range(HEADS)], 1)
        for run, (start, stop) in enumerate(RUNS)
    ]
    return jnp.concatenate(rows, 0).astype(bf16)


def padded(run):
    missing = PACK - run.shape[-2]
    if not missing:
        return run
    return jnp.concatenate([run, jnp.zeros((*run.shape[:-2], missing, run.shape[-1]), f32)], -2)


def pack_heads(array, out_ref):
    heads = []
    for h in range(HEADS):
        parts = [padded(lane_slice(array[start:stop], h * HD)) for start, stop in RUNS]
        heads.append(jnp.concatenate(parts, 1))
    out_ref[...] = jnp.stack(heads).astype(bf16)


def to_windows(array):
    split = array.reshape(GROUP, ROWS_DEV, 2, WIN, array.shape[-1])
    return [split[:, :, w].reshape(CELLS, array.shape[-1]) for w in range(2)]


def from_windows(pair):
    depth = pair[0].shape[-1]
    parts = [part.reshape(GROUP, ROWS_DEV, 1, WIN, depth) for part in pair]
    return jnp.concatenate(parts, 2).reshape(GROUP, TOK, depth)


def pack_cells(cells):
    tail = cells[:, SHORT:].reshape(GROUP * 32, 128)
    moved = [pltpu.roll(tail, 96 - 32 * kind, 1).reshape(GROUP, 32, 128) for kind in range(3)]
    moved = jnp.concatenate(moved + [jnp.zeros((GROUP, SHORT - 96, 128), f32)], 1)
    lane = iota(moved.shape, 2)
    return jnp.where(lane < 96, cells[:, :SHORT], moved)


def roll_tokens(array, by):
    by = by % TOK
    return jnp.concatenate([array[TOK - by :], array[: TOK - by]], 0)


def normalized(attended, weight):
    outputs = dot(attended, weight)
    centered = outputs - jnp.mean(outputs, -1, keepdims=True)
    inverse = lax.rsqrt(jnp.mean(centered * centered, -1, keepdims=True) + norm_eps)
    return centered * inverse, inverse


def finish_back(attended, weight, gain_row, grad_out):
    y_hat, inverse = normalized(attended, weight)
    grad_gain = jnp.sum(grad_out * y_hat, 0, keepdims=True)
    grad_bias = jnp.sum(grad_out, 0, keepdims=True)
    scaled = grad_out * gain_row
    grad_y = inverse * (
        scaled
        - jnp.mean(scaled, -1, keepdims=True)
        - y_hat * jnp.mean(scaled * y_hat, -1, keepdims=True)
    )
    grad_y = grad_y.astype(bf16)
    gains = jnp.concatenate([grad_gain, grad_bias, jnp.zeros((6, C), f32)], 0)
    return grad_y, dot_t(grad_y, weight), gains


def tags_of(window, first_row_ref, row_ref, col_ref):
    lane = iota((WIN, 128), 1)
    place = iota((WIN, 1), 0)
    column = place + window * WIN
    col_label = jnp.zeros((WIN, 1), jnp.int32)
    for label in (1, 2):
        cut = jnp.sum((col_ref[...] < label).astype(jnp.int32), 1, keepdims=True)
        col_label = col_label + (column >= cut).astype(jnp.int32)
    blocks = []
    for source in MOVED:
        rows = [row_ref[first_row_ref[0] + source * ROWS_DEV + r] for r in range(ROWS_DEV)]
        for r in range(ROWS_DEV):
            row_label = rows[r]
            if window == 1:
                row_label = jnp.where(column >= 36, rows[(r + 1) % ROWS_DEV], rows[r])
            blocks.append(jnp.where(lane == col_label + 3 * row_label + 96, 10.0, 0.0))
    return jnp.concatenate(blocks, 0)


def tagged(cells, window, mask_refs):
    if mask_refs is None:
        return cells
    return jnp.where(iota(cells.shape, 1) < 96, cells, tags_of(window, *mask_refs))


def with_tags(cells, at, key):
    lane = iota(cells.shape, 1)
    own = cells if at == 0 else pltpu.roll(cells, 128 - at, 1)
    tags = pltpu.roll(cells, 64, 1)
    if key:
        tags = jnp.where(lane < HD + 9, tags - 10.0, tags)
    return jnp.where(lane < HD, own, tags)[:, :64].astype(bf16)


def together(steps):
    steps = list(steps)
    while steps:
        steps = [step for step in steps if next(step, 0) is None]


def attend_kernel(masks, x_ref, *refs):
    mask_refs = refs[:3] if masks else None
    out_ref = refs[-1]
    lane = iota((CELLS, 128), 1)
    per_window = [None, None]

    def attend(w, cells):
        cells = tagged(cells, w, mask_refs)
        query = with_tags(cells, 0, False) if masks else cells[:, :HD].astype(bf16)
        key = with_tags(cells, HD, True) if masks else cells[:, HD : 2 * HD].astype(bf16)
        value = jnp.where(lane < HD, pltpu.roll(cells, 64, 1), jnp.where(lane == HD, 1.0, 0.0)).astype(bf16)
        yield
        scores = dot_t(query, key)
        yield
        weights = jnp.exp(scores).astype(bf16)
        yield
        summed = dot(weights, value)
        yield
        attended = jnp.where(lane < HD, summed * (1.0 / summed[:, HD : HD + 1]), 0.0)
        per_window[w] = attended

    together(attend(w, cells) for w, cells in enumerate(to_windows(unpack_cells(x_ref))))
    cells = from_windows(per_window)
    total = 0.0
    for run, (start, stop) in enumerate(RUNS):
        rows = padded(cells[:, start:stop]).reshape(GROUP * PACK, 128)
        total = total + (pltpu.roll(rows, run * HD, 1) if run else rows)
    out_ref[...] = total.astype(bf16).reshape(GROUP, PACK, 128)


def attend_back_kernel(block, masks, head_ref, scale_ref, x_ref, grad_ref, *refs):
    mask_refs = refs[:3] if masks else None
    out_ref = refs[-1]
    lane = iota((CELLS, 128), 1)
    low = iota((HD, CELLS), 0)
    zeros = jnp.zeros((HD, CELLS), f32)
    scale_row = jnp.exp(jnp.full((1, 128), scale_ref[block, head_ref[0]], f32))
    unscale_row = 1.0 / scale_row
    packed = grad_ref[...].astype(f32).reshape(GROUP * PACK, 128)
    rolled = [pltpu.roll(packed, 128 - run * HD, 1) if run else packed for run in range(len(RUNS))]
    rolled = [
        part.reshape(GROUP, PACK, 128)[:, : stop - start] for part, (start, stop) in zip(rolled, RUNS)
    ]
    grads = to_windows(jnp.concatenate(rolled, 1))
    factors = to_windows(unpack_factors(x_ref))
    results = [None, None]

    def attend_back(w, cells):
        cells = tagged(cells, w, mask_refs)
        turned = cells.T
        query_t = (jnp.concatenate([turned[:HD], turned[96:]], 0) if masks else turned[:HD]).astype(bf16)
        key_t = turned[HD : 2 * HD].astype(bf16)
        value_t = turned[2 * HD : 3 * HD]
        grad_t = grads[w].T[:HD]
        key = with_tags(cells, HD, True) if masks else cells[:, HD : 2 * HD].astype(bf16)
        yield
        scores = dot(key, query_t)
        yield
        weights = jnp.exp(scores).astype(bf16)
        yield
        summed = dot(jnp.concatenate([value_t, jnp.where(low == 0, 1.0, 0.0)], 0).astype(bf16), weights)
        yield
        inverse = 1.0 / summed[HD : HD + 1]
        grad_t = (grad_t * inverse).astype(bf16).astype(f32)
        row_high, row_low = split_two(jnp.sum(grad_t * summed[:HD], 0, keepdims=True) * inverse)
        rows = jnp.where(low == 0, -row_high, jnp.where(low == 1, -row_low, 0.0))
        grad_ext = jnp.concatenate([grad_t, rows], 0).astype(bf16)
        yield
        ones = jnp.where(lane < HD + 2, 1.0, 0.0)
        value_ext = jnp.where(lane < HD, pltpu.roll(cells, 64, 1), ones)[:, :64].astype(bf16)
        yield
        grad_scores = (weights.astype(f32) * dot(value_ext, grad_ext)).astype(bf16)
        yield
        query_at = jnp.where((lane >= HD) & (lane < 2 * HD), pltpu.roll(cells, HD, 1), 0.0).astype(bf16)
        grad_at = jnp.concatenate([zeros, zeros, grad_t, zeros], 0).T.astype(bf16)
        yield
        grad_kv = dot(grad_scores, query_at) + dot(weights, grad_at)
        yield
        grad_q = dot(key_t, grad_scores)
        yield
        grad_q = jnp.concatenate([grad_q, zeros, zeros, zeros], 0).T
        yield
        total = jnp.where(lane < HD, grad_q * scale_row, grad_kv)
        unit = jnp.where(lane < HD, cells * unscale_row, jnp.where(lane < 2 * HD, cells, 0.0))
        q_factor, k_factor = factors[w][:, 96:97], factors[w][:, 97:98]
        factor = jnp.where(lane < HD, q_factor, jnp.where(lane < 2 * HD, k_factor, 1.0))
        results[w] = factor * (total - unit * head_sums(unit * total))

    together(attend_back(w, cells) for w, cells in enumerate(to_windows(unpack_cells(x_ref))))
    out_ref[...] = pack_cells(from_windows(results)).astype(bf16)


def first_kernel(tokens_ref, w_ref, scale_ref, out_ref):
    send_projected(tokens_ref[...], w_ref[...], scale_ref, 0, out_ref)


def middle_kernel(packed_ref, scale_ref, gain_ref, bias_ref, tokens_ref, w_proj_ref, w_ref, out_ref, rolled_ref):
    attended = unpack_heads(packed_ref)
    y_hat, _ = normalized(attended, w_proj_ref[...])
    out = (tokens_ref[...].astype(f32) + y_hat * gain_ref[0:1] + bias_ref[0:1]).astype(bf16).astype(f32)
    rolled = roll_tokens(out, -SHIFT).astype(bf16)
    rolled_ref[...] = rolled
    send_projected(rolled, w_ref[...], scale_ref, 1, out_ref)


def turn_kernel(core_ref, packed_ref, gain_ref, grad_ref, w_proj_ref, out_ref, kept_ref, given_ref, gains_ref):
    attended = unpack_heads(packed_ref)
    grad = roll_tokens(grad_ref[...].astype(f32), -SHIFT)
    grad_y, grad_att, gains = finish_back(attended, w_proj_ref[...], gain_ref[1:2], grad)
    pack_heads(grad_att, out_ref)
    kept, given = halves(attended, core_ref[0])
    kept_ref[...] = dot_0(grad_y, kept).astype(bf16)
    given_ref[...] = dot_0(grad_y, given).astype(bf16)
    gains_ref[...] = gains


def gather_qkv(qkv_ref):
    parts = [qkv_ref[h].astype(f32) for h in range(HEADS)]
    top = [lane_slice(parts[h][:SHORT], kind * HD) for kind in range(3) for h in range(HEADS)]
    tail = [lane_slice(parts[h][kind * 32 : kind * 32 + 32], 96) for kind in range(3) for h in range(HEADS)]
    return jnp.concatenate([jnp.concatenate(top, 1), jnp.concatenate(tail, 1)], 0).astype(bf16)


def halves(array, core):
    half = array.shape[1] // 2
    left, right = array[:, :half].astype(f32), array[:, half:].astype(f32)
    return jnp.where(core == 0, left, right).astype(bf16), jnp.where(core == 0, right, left).astype(bf16)


def back_kernel(
    core_ref,
    qkv_ref,
    packed_ref,
    gain_ref,
    w_ref,
    w_proj_ref,
    grad_ref,
    proj1_kept_ref,
    proj1_given_ref,
    tokens_ref,
    out_ref,
    gains_ref,
    grad0_ref,
    kept_ref,
    given_ref,
):
    d_qkv = gather_qkv(qkv_ref)
    from_qkv = roll_tokens(dot_t(d_qkv, w_ref[...]), SHIFT)
    grad = (grad_ref[...].astype(f32) + from_qkv).astype(bf16)
    grad0_ref[...] = grad
    attended = unpack_heads(packed_ref)
    grad_y, grad_att, gains = finish_back(attended, w_proj_ref[...], gain_ref[0:1], grad.astype(f32))
    sides = zip(halves(d_qkv, core_ref[0]), (proj1_kept_ref, proj1_given_ref), halves(attended, core_ref[0]))
    kept, given = [
        jnp.concatenate(
            [dot_0(tokens_ref[...], part).astype(bf16), proj1_ref[...], dot_0(grad_y, att).astype(bf16)], 1
        )
        for part, proj1_ref, att in sides
    ]
    kept_ref[...] = kept
    given_ref[...] = given
    pack_heads(grad_att, out_ref)
    gains_ref[...] = gains


def image_kernel(qkv_ref, w_ref, grad_ref, out_ref):
    out_ref[...] = (grad_ref[...].astype(f32) + dot_t(gather_qkv(qkv_ref), w_ref[...])).astype(bf16)


def late_kernel(given, core_ref, qkv_ref, tokens_ref, out_ref):
    half = halves(gather_qkv(qkv_ref), core_ref[0])[given]
    out_ref[...] = dot_0(tokens_ref[...], half).astype(bf16)


def parts_kernel(late_ref, got_late_ref, got_ref, gains0_ref, gains1_ref, kept_ref, parts_ref):
    pieces = []
    for ref in (gains0_ref, gains1_ref):
        for row in (0, 1):
            pieces += split_two(ref[row : row + 1])
    gains = jnp.concatenate(pieces + [jnp.zeros((16 - len(pieces), C), f32)], 0)
    depth = C // 8
    for ring in range(8):
        block = gains[:, ring // 2 * 128 : ring // 2 * 128 + 128]
        block = pltpu.roll(block, depth, 1) if ring % 2 else block
        parts_ref[ACROSS.index(ring), TILES * depth :] = block.astype(bf16)
    late = late_ref[...].astype(f32) + got_late_ref[...].astype(f32)
    early = kept_ref[...].astype(f32) + got_ref[...].astype(f32)
    tile = 0
    for part in (late, early):
        for at in range(0, part.shape[1], 128):
            block = part[:, at : at + 128].astype(bf16).reshape(8, depth, 128)
            parts_ref[:, tile * depth : (tile + 1) * depth, :] = jnp.stack([block[ring] for ring in ACROSS])
            tile += 1


def first_sum_kernel(parts_ref, out_ref):
    total = jnp.sum(parts_ref[...].astype(f32), 0)
    gains = total[TILES * C // 8 :]
    high, low = split_two(gains + pltpu.roll(gains, 15, 0))
    gains = jnp.where(iota(gains.shape, 0) % 2 == 0, high, pltpu.roll(low, 1, 0))
    total = total[: TILES * C // 8].reshape(TILES, 8, 8, 128)
    for place in range(8):
        rolled = pltpu.roll(gains, 128 - 8 * place, 1) if place else gains
        block = jnp.concatenate([total[:, place].reshape(TILES * 8, 128), rolled], 0)
        out_ref[ORDER.index(place)] = block.astype(bf16)


def second_sum_kernel(parts_ref, out_ref):
    out_ref[...] = jnp.sum(parts_ref[...].astype(f32), 0)


def add_kernel(one_ref, two_ref, out_ref):
    out_ref[...] = one_ref[...] + two_ref[...]


def final_kernel(core_ref, own_ref, other_ref, qkv_ref, proj_ref, gain_ref, bias_ref):
    own = own_ref[: TILES * 8].reshape(TILES, 8, 128)
    other = other_ref[: TILES * 8].reshape(TILES, 8, 128)
    first = core_ref[0] == 0
    left, right = jnp.where(first, own, other), jnp.where(first, other, own)
    for block, tiles in ((0, (0, 1, 2)), (1, (3, 4, 5))):
        qkv_ref[block] = jnp.concatenate([side[i] for side in (left, right) for i in tiles], 1)
    proj_ref[1] = jnp.concatenate([left[6], right[6]], 1)
    proj_ref[0] = jnp.concatenate([left[7], right[7]], 1)
    gains = (own_ref[TILES * 8 :] + other_ref[TILES * 8 :])[:, :8]
    gain_ref[...] = jnp.concatenate([gains[0:1] + gains[1:2], gains[4:5] + gains[5:6]], 0)
    bias_ref[...] = jnp.concatenate([gains[2:3] + gains[3:4], gains[6:7] + gains[7:8]], 0)


def pieces_of(shape):
    return 4 if shape[0] % 64 == 0 and shape[0] * shape[1] >= 2**18 else 1


def copies_of(source, target, sems, first):
    count = pieces_of(target.shape)
    rows = target.shape[0] // count
    if count == 1:
        return [pltpu.make_async_copy(source, target, sems.at[first])]
    return [
        pltpu.make_async_copy(
            source.at[pl.ds(i * rows, rows)], target.at[pl.ds(i * rows, rows)], sems.at[first + i]
        )
        for i in range(count)
    ]


class Fetched:
    def __init__(self, source, ref, sems, first):
        self.ref, self.copies = ref, copies_of(source, ref, sems, first)
        for copy in self.copies:
            copy.start()
        self.waited = False

    def __getitem__(self, at):
        if not self.waited:
            for copy in self.copies:
                copy.wait()
            self.waited = True
        return self.ref[at]


class Stored:
    def __init__(self, ref, target, sems, first):
        self.ref, self.copies = ref, copies_of(ref, target, sems, first)

    def __setitem__(self, at, value):
        self.ref[at] = value
        for copy in self.copies:
            copy.start()


def call(kernel, outs, scalars, arrays, masks=(), fetched=(), stored=()):
    arrays = [item if isinstance(item, tuple) else (item, None) for item in arrays]
    fetched = [item if isinstance(item, tuple) else (item, None) for item in fetched]
    counts = [len(scalars), len(arrays), len(fetched), len(masks), len(outs), len(stored), len(fetched), len(stored)]

    def wrapped(*refs):
        parts, at = [], 0
        for count in counts:
            parts.append(refs[at : at + count])
            at += count
        scalar_refs, array_refs, sources, mask_refs, out_refs, targets, filled, sent = parts
        sems = refs[-1]
        near = [ref if block is None else ref.at[block] for ref, (_, block) in zip(array_refs, arrays)]
        far, results, first = [], [], 0
        for i, (_, block) in enumerate(fetched):
            source = sources[i] if block is None else sources[i].at[block]
            far.append(Fetched(source, filled[i], sems, first))
            first += pieces_of(filled[i].shape)
        for i in range(len(stored)):
            results.append(Stored(sent[i], targets[i], sems, first))
            first += pieces_of(sent[i].shape)
        kernel(*scalar_refs, *near, *far, *mask_refs, *out_refs, *results)
        for result in results:
            for copy in result.copies:
                copy.wait()

    smem = pl.BlockSpec(memory_space=pltpu.SMEM)
    vmem = pl.BlockSpec(memory_space=pltpu.VMEM)
    hbm = pl.BlockSpec(memory_space=pltpu.HBM)
    scratch = [
        pltpu.VMEM(array.shape if block is None else array.shape[1:], array.dtype) for array, block in fetched
    ]
    scratch += [pltpu.VMEM(*out) for out in stored]
    if scratch:
        scratch.append(pltpu.SemaphoreType.DMA((sum(pieces_of(buffer.shape) for buffer in scratch),)))
    return pl.pallas_call(
        wrapped,
        out_shape=[jax.ShapeDtypeStruct(*out) for out in outs] + [pltpu.HBM(*out) for out in stored],
        in_specs=[smem] * len(scalars)
        + [vmem] * len(arrays)
        + [hbm] * len(fetched)
        + [smem, smem, vmem][: len(masks)],
        out_specs=[vmem] * len(outs) + [hbm] * len(stored),
        scratch_shapes=scratch,
        compiler_params=pltpu.CompilerParams(vmem_limit_bytes=VMEM_LIMIT),
    )(
        *scalars,
        *(array for array, _ in arrays),
        *(pltpu.with_memory_space_constraint(array, pltpu.HBM) for array, _ in fetched),
        *masks,
    )


def body(image, out_grad, w_qkv, w_proj, norm_gain, norm_bias, logit_scale, row_band, col_band):
    position = lax.axis_index("rows")
    half = GROUP // 2
    rings = range(DEVS // GROUP)
    aligned = [[GROUP * g + i for i in ORDER] for g in rings]
    across = [[GROUP * g + i for g in ACROSS] for i in range(GROUP)]
    moved = [[(GROUP * g + half + i) % DEVS for i in MOVED] for g in rings]
    moved_position = (position + DEVS - half) % DEVS
    head0, head1 = jnp.zeros((1,), jnp.int32), jnp.zeros((1,), jnp.int32)
    for h in range(HEADS):
        head0 = head0 + h * (position % GROUP == ORDER[h])
        head1 = head1 + h * (moved_position % GROUP == MOVED[h])
    first_row = (moved_position // GROUP * WIN).reshape(1)
    core = (lax.axis_index("dp") % 2).reshape(1)
    image, head0, head1, first_row, core = lax.optimization_barrier((image, head0, head1, first_row, core))
    masks = (first_row, row_band, col_band.reshape(1, -1))

    def exchange(array, groups):
        return lax.all_to_all(array, "rows", 0, 0, axis_index_groups=groups, tiled=True)

    tokens0 = image.reshape(TOK, C)
    grad_out = out_grad.reshape(TOK, C)
    short = ((GROUP, SHORT, 128), bf16)
    narrow = ((GROUP, PACK, 128), bf16)
    cells = ((TOK, C), bf16)
    proj = ((C, HH // 2), bf16)
    gains = ((8, C), f32)
    half_early = ((C, EARLY // 2), bf16)
    half_late = ((C, LATE // 2), bf16)

    def swap(array, apart):
        return lax.ppermute(array, "dp", [(i, i ^ apart) for i in range(4)])

    (x0,) = call(first_kernel, [short], (), (), fetched=(tokens0, (w_qkv, 0), logit_scale))
    x0 = exchange(x0, aligned)
    (a0,) = call(functools.partial(attend_kernel, False), [narrow], (), (x0,))
    a0 = exchange(a0, aligned)
    x1, tokens1 = call(
        middle_kernel,
        [short],
        (),
        (a0, logit_scale, norm_gain, norm_bias, tokens0, (w_proj, 0), (w_qkv, 1)),
        stored=[cells],
    )
    x1 = exchange(x1, moved)
    (a1,) = call(functools.partial(attend_kernel, True), [narrow], (), (x1,), masks)
    a1 = exchange(a1, moved)
    d1, proj1_kept, proj1_given, gains1 = call(
        turn_kernel,
        [narrow, proj, proj, gains],
        (core,),
        (a1, norm_gain, grad_out, (w_proj, 1)),
    )
    d1 = exchange(d1, moved)
    (qkv1,) = call(
        functools.partial(attend_back_kernel, 1, True), [short], (head1, logit_scale), (x1, d1), masks
    )
    qkv1 = exchange(qkv1, moved)
    d0, gains0, grad0, kept, given = call(
        back_kernel,
        [narrow, gains],
        (core,),
        (qkv1, a0, norm_gain, (w_qkv, 1), (w_proj, 0), grad_out, proj1_kept, proj1_given, tokens1),
        stored=[cells, half_early, half_early],
    )
    d0 = exchange(d0, aligned)
    (qkv0,) = call(functools.partial(attend_back_kernel, 0, False), [short], (head0, logit_scale), (x0, d0))
    qkv0 = exchange(qkv0, aligned)
    qkv0, given = lax.optimization_barrier((qkv0, given))
    got = swap(given, 1)
    (given_late,) = call(functools.partial(late_kernel, 1), [half_late], (core,), (qkv0, tokens0))
    got_late = swap(given_late, 1)
    qkv0, given_late = lax.optimization_barrier((qkv0, given_late))
    (late,) = call(functools.partial(late_kernel, 0), [half_late], (core,), (qkv0, tokens0))
    (parts,) = call(
        parts_kernel,
        [((8, SENT, 128), bf16)],
        (),
        (late, got_late, got, gains0, gains1, kept),
    )
    parts = exchange(parts, across)
    (parts,) = call(first_sum_kernel, [((8, SHARE, 128), bf16)], (), (parts,))
    parts = exchange(parts, aligned)
    (share,) = call(second_sum_kernel, [((SHARE, 128), f32)], (), (parts,))
    (share,) = call(add_kernel, [((SHARE, 128), f32)], (), (share, swap(share, 2)))
    other = swap(share, 1)
    qkv0, _ = lax.optimization_barrier((qkv0, share))
    (grad_image,) = call(image_kernel, [cells], (), (qkv0, (w_qkv, 0), grad0))
    small = ((2, 8), f32)
    grad_qkv, grad_proj, grad_gain, grad_bias = call(
        final_kernel,
        [((2, 8, 3 * HH), f32), ((2, 8, HH), f32), small, small],
        (core,),
        (share, other),
    )
    return (
        grad_image.reshape(image.shape),
        grad_qkv,
        grad_proj.transpose(0, 2, 1),
        grad_gain,
        grad_bias,
    )


def solution(mesh):
    placed = (P("dp", "rows", None, None), P("dp", "rows", None, None)) + (P(),) * 7
    return jax.shard_map(
        body,
        mesh=mesh,
        in_specs=placed,
        out_specs=(
            P("dp", "rows", None, None),
            P(None, "rows", None),
            P(None, None, "rows"),
            P(None, "rows"),
            P(None, "rows"),
        ),
        check_vma=False,
    )
```
